32 devices in a mesh: dp: 8 (over z, x), seq: 4 (over y, core).
Axes of the slice: x: 2, y: 2, z: 4, core: 2. Of those that a mesh axis runs over, the one named last changes fastest.
Arguments:
- inputs: bfloat16 [8, 1024, 768], P('dp', 'seq'), may hold values from -6 to 6
- cotangent: bfloat16 [8, 1024, 768], P('dp', 'seq'), may hold values from -6 to 6
- image_lengths: int32 [8, 8], P('dp'), may hold values from 1 to 384, 1024 in all within a row
- attention_weight: float32 [2, 4, 768, 768], P(None, None, ('dp', 'seq')), may hold values from -1.299038 to 1.299038
- attention_moment: float32 [2, 4, 768, 768], P(None, None, ('dp', 'seq')), may hold values from -56 to 56
- attention_average: float32 [2, 4, 768, 768], P(None, None, ('dp', 'seq')), may hold values from -0.21875 to 0.21875
- up_weight: float32 [2, 768, 3072], P(None, ('dp', 'seq')), may hold values from -0.21875 to 0.21875
- up_moment: float32 [2, 768, 3072], P(None, ('dp', 'seq')), may hold values from -112 to 112
- up_average: float32 [2, 768, 3072], P(None, ('dp', 'seq')), may hold values from -0.21875 to 0.21875
- down_weight: float32 [2, 3072, 768], P(None, ('dp', 'seq')), may hold values from -0.109375 to 0.109375
- down_moment: float32 [2, 3072, 768], P(None, ('dp', 'seq')), may hold values from -256 to 256
- down_average: float32 [2, 3072, 768], P(None, ('dp', 'seq')), may hold values from -0.109375 to 0.109375
- layer_vectors: float32 [2, 8, 768], P(None, None, ('dp', 'seq')), may hold values from -0.6 to 1.6
- vector_moment: float32 [2, 8, 768], P(None, None, ('dp', 'seq')), may hold values from -256 to 256
- vector_average: float32 [2, 8, 768], P(None, None, ('dp', 'seq')), may hold values from -0.6 to 1.6
- hidden_bias: float32 [2, 3072], P(None, ('dp', 'seq')), may hold values from -1.5 to 1.5
- bias_moment: float32 [2, 3072], P(None, ('dp', 'seq')), may hold values from -112 to 112
- bias_average: float32 [2, 3072], P(None, ('dp', 'seq')), may hold values from -1.5 to 1.5
Outputs:
- output: bfloat16 [8, 1024, 768], P('dp', 'seq')
- input_grad: bfloat16 [8, 1024, 768], P('dp', 'seq')
- attention_grad: float32 [2, 4, 768, 768], P(None, None, ('dp', 'seq'))
- attention_moment_new: float32 [2, 4, 768, 768], P(None, None, ('dp', 'seq'))
- attention_average_new: float32 [2, 4, 768, 768], P(None, None, ('dp', 'seq'))
- attention_weight_new: float32 [2, 4, 768, 768], P(None, None, ('dp', 'seq'))
- attention_weight_copy: bfloat16 [2, 4, 768, 768], P(None, None, ('dp', 'seq'))
- up_grad: float32 [2, 768, 3072], P(None, ('dp', 'seq'))
- up_moment_new: float32 [2, 768, 3072], P(None, ('dp', 'seq'))
- up_average_new: float32 [2, 768, 3072], P(None, ('dp', 'seq'))
- up_weight_new: float32 [2, 768, 3072], P(None, ('dp', 'seq'))
- up_weight_copy: bfloat16 [2, 768, 3072], P(None, ('dp', 'seq'))
- down_grad: float32 [2, 3072, 768], P(None, ('dp', 'seq'))
- down_moment_new: float32 [2, 3072, 768], P(None, ('dp', 'seq'))
- down_average_new: float32 [2, 3072, 768], P(None, ('dp', 'seq'))
- down_weight_new: float32 [2, 3072, 768], P(None, ('dp', 'seq'))
- down_weight_copy: bfloat16 [2, 3072, 768], P(None, ('dp', 'seq'))
- vector_grad: float32 [2, 8, 768], P(None, None, ('dp', 'seq'))
- vector_moment_new: float32 [2, 8, 768], P(None, None, ('dp', 'seq'))
- vector_average_new: float32 [2, 8, 768], P(None, None, ('dp', 'seq'))
- layer_vectors_new: float32 [2, 8, 768], P(None, None, ('dp', 'seq'))
- layer_vectors_copy: bfloat16 [2, 8, 768], P(None, None, ('dp', 'seq'))
- bias_grad: float32 [2, 3072], P(None, ('dp', 'seq'))
- bias_moment_new: float32 [2, 3072], P(None, ('dp', 'seq'))
- bias_average_new: float32 [2, 3072], P(None, ('dp', 'seq'))
- hidden_bias_new: float32 [2, 3072], P(None, ('dp', 'seq'))
- hidden_bias_copy: bfloat16 [2, 3072], P(None, ('dp', 'seq'))
The draws below stay inside these ranges and needn't reach their ends.
Inputs may be any that keep to these rules, and one draw needn't show every extreme that they name: `image_lengths`: in each row the first 7 entries are image lengths and the last is the padding; a row's entries sum to 1024, and its largest entry is 384.
All inputs are finite; a program needn't handle non-finite values.
Results may differ from the reference program's by a relative error of at most 0.014.
Values may be sent and summed in bfloat16 or wider, within the bound.
A program may use at most 320 MiB of HBM per device.

```python
import math
import jax
import jax.numpy as jnp
import numpy as np
from jax import lax

D = 768
HEADS = 12
HEAD_DIM = 64
FF = 3072
LAYERS = 2
ROW_LEN = 1024
SEGS = 8
IMAGE_MOST = 384
ROWS = 8
TOKENS = 8192


def attention_law(key):
    noise = jnp.clip(jax.random.normal(key, (LAYERS, 4, D, D), jnp.float32), -6.0, 6.0)
    which = lax.broadcasted_iota(jnp.int32, (LAYERS, 4, D, D), 1)
    return noise * D ** (-0.5) * jnp.where(which == 3, 6.0, 1.0)


def draw_attention_weight(key, part):
    return attention_law(jax.random.fold_in(key, 101))


def vector_law(key):
    noise = jnp.clip(jax.random.normal(key, (LAYERS, 8, D), jnp.float32), -6.0, 6.0)
    which = lax.broadcasted_iota(jnp.int32, (LAYERS, 8, D), 1)
    gains = (which == 0) | (which == 5)
    return jnp.where(gains, 1.0 + 0.1 * noise, 0.1 * noise)


def draw_layer_vectors(key, part):
    return vector_law(jax.random.fold_in(key, 202))


def draw_vector_average(key, part):
    return vector_law(jax.random.fold_in(key, 303))


def raised(values, rng, source, target, parts, factor):
    def block_of(position):
        return (jnp.arange(values.shape[position]) // (values.shape[position] // parts)).reshape((-1,) + (1,) * (values.ndim - 1 - position))

    near = jax.random.permutation(rng, parts)[block_of(target)]
    other_side = (block_of(target) + parts // 2) % parts
    return jnp.where((block_of(source) == near) | (block_of(source) == other_side), factor * values, values)


def block_levels(own_key, extent, cuts, low, high):
    gain = 1.0
    for position, shards_of in cuts:
        heights = jax.random.uniform(jax.random.fold_in(jax.random.fold_in(own_key, 6), position), (shards_of,), jnp.float32, low / len(cuts), high / len(cuts))
        gain = gain * jnp.repeat(jnp.exp(heights), extent[position] // shards_of).reshape((-1,) + (1,) * (len(extent) - 1 - position))
    return gain


def split_up(amount, total, reach, skew):
    portions = [(1 << 20) // math.isqrt(standing ** skew) + 1 for standing in range(2, amount + 1)]
    surplus, holding = total - reach - (amount - 1), [1] * (amount - 1)
    while surplus > 0:
        free = [i for i in range(amount - 1) if holding[i] < reach]
        mass, left = sum([portions[i] for i in free]), surplus
        for i in free:
            addition = min(reach - holding[i], max(1, left * portions[i] // mass), surplus)
            holding[i] = holding[i] + addition
            surplus = surplus - addition
    return np.array([reach] + holding)


def ragged_sizes(key, number_of, total, limit, slope):
    if number_of == 2:
        one = jax.random.randint(key, (), max(1, total - limit), min(limit, total - 1) + 1)
        return jnp.stack([one, total - one])
    sizes = jnp.asarray(split_up(number_of, total, limit, slope), jnp.int32)
    pairs = (number_of - 1) // 2
    source_of, receiver = sizes[1:1 + 2 * pairs:2], sizes[2:2 + 2 * pairs:2]
    margin = jnp.minimum(source_of - 1, limit - receiver)
    passed = jax.random.randint(jax.random.fold_in(key, 1), (pairs,), 0, 1 << 20) % (margin + 1)
    sizes = sizes.at[1:1 + 2 * pairs:2].set(source_of - passed).at[2:2 + 2 * pairs:2].set(receiver + passed)
    return sizes[jax.random.permutation(jax.random.fold_in(key, 2), number_of)]


def gaussian(rng, shape, deviation, reach, split=(), kind=jnp.bfloat16):
    drawn = jax.random.normal(rng, shape, jnp.float32) * deviation
    if len(split) > 0:
        drawn = block_levels(rng, shape, split, -0.22, 0.18) * drawn
    return jnp.clip(drawn, min=-reach, max=reach).astype(kind)


def bell_draw_with(stream_key, extent, deviation, reach, shards, heavy, kind=jnp.bfloat16):
    entries = deviation * jax.random.normal(stream_key, extent, jnp.float32)
    if shards:
        entries = entries * block_levels(stream_key, extent, shards, -0.22, 0.18)
    return jnp.clip(raised(entries, jax.random.fold_in(stream_key, 3), *heavy), -reach, reach).astype(kind)


def setup_inputs(seed: int = 0) -> dict:
    seeds = jax.random.split(jax.random.key(seed), 19)
    inputs = bell_draw_with(seeds[0], (ROWS, ROW_LEN, D), 1.0, 6.0, ((0, 8), (1, 4)), (0, 2, 8, 2.0))
    cotangent = gaussian(seeds[1], (ROWS, ROW_LEN, D), 1.0, 6.0, ((0, 8), (1, 4)))
    image_lengths = jax.vmap(lambda own: ragged_sizes(own, SEGS, ROW_LEN, IMAGE_MOST, 1))(jax.random.split(seeds[2], ROWS)).reshape((ROWS, SEGS)).astype(jnp.int32)
    attention_weight = draw_attention_weight(jax.random.fold_in(seeds[18], 71), 0)
    attention_moment = gaussian(seeds[4], (LAYERS, 4, D, D), (0.1 * TOKENS ** 0.5), 56.0, ((2, 32),), jnp.float32)
    attention_average = gaussian(seeds[5], (LAYERS, 4, D, D), D ** -0.5, 0.21875, ((2, 32),), jnp.float32)
    up_weight = gaussian(seeds[6], (LAYERS, D, FF), D ** -0.5, 0.21875, ((1, 32),), jnp.float32)
    up_moment = gaussian(seeds[7], (LAYERS, D, FF), (0.2 * TOKENS ** 0.5), 112.0, ((1, 32),), jnp.float32)
    up_average = gaussian(seeds[8], (LAYERS, D, FF), D ** -0.5, 0.21875, ((1, 32),), jnp.float32)
    down_weight = gaussian(seeds[9], (LAYERS, FF, D), FF ** -0.5, 0.109375, ((1, 32),), jnp.float32)
    down_moment = gaussian(seeds[10], (LAYERS, FF, D), (0.5 * TOKENS ** 0.5), 256.0, ((1, 32),), jnp.float32)
    down_average = gaussian(seeds[11], (LAYERS, FF, D), FF ** -0.5, 0.109375, ((1, 32),), jnp.float32)
    layer_vectors = draw_layer_vectors(jax.random.fold_in(seeds[18], 71), 0)
    vector_moment = gaussian(seeds[13], (LAYERS, 8, D), (0.5 * TOKENS ** 0.5), 256.0, ((2, 32),), jnp.float32)
    vector_average = draw_vector_average(jax.random.fold_in(seeds[18], 71), 0)
    hidden_bias = gaussian(seeds[15], (LAYERS, FF), 0.1, 1.5, ((1, 32),), jnp.float32)
    bias_moment = gaussian(seeds[16], (LAYERS, FF), (0.2 * TOKENS ** 0.5), 112.0, ((1, 32),), jnp.float32)
    bias_average = gaussian(seeds[17], (LAYERS, FF), 0.1, 1.5, ((1, 32),), jnp.float32)
    return {"inputs": inputs, "cotangent": cotangent, "image_lengths": image_lengths, "attention_weight": attention_weight, "attention_moment": attention_moment, "attention_average": attention_average, "up_weight": up_weight, "up_moment": up_moment, "up_average": up_average, "down_weight": down_weight, "down_moment": down_moment, "down_average": down_average, "layer_vectors": layer_vectors, "vector_moment": vector_moment, "vector_average": vector_average, "hidden_bias": hidden_bias, "bias_moment": bias_moment, "bias_average": bias_average}


@jax.custom_vjp
def low(v):
    return lax.optimization_barrier(v.astype(jnp.bfloat16)).astype(jnp.float32)

@jax.custom_vjp
def low_back(v):
    return v

def low_keep(v):
    return (low(v), None)

def low_pass(kept, grad):
    return (grad,)

def back_keep(v):
    return (v, None)

def back_low(kept, grad):
    return (low(grad),)
low.defvjp(low_keep, low_pass)
low_back.defvjp(back_keep, back_low)
EPSILON = 1e-06
SCALE_SCORE = 0.125
MOMENTUM_RATE = 0.9
DECAY_RATE = 0.0001
AVERAGE_RATE = 0.5
LEARN_BASE = 0.1

def layer_norm(values, gain_row, shift_row):
    center = values - lax.optimization_barrier(jnp.mean(values, axis=-1, keepdims=True))
    spread = lax.optimization_barrier(jnp.mean(center * center, axis=-1, keepdims=True))
    return center * lax.rsqrt(spread + EPSILON) * gain_row + shift_row

def dense(values, matrix):
    return jnp.einsum('...i,ij->...j', values, matrix, precision=lax.Precision.HIGHEST)

def segment_ids(image_lengths, row_len):
    bounds = jnp.cumsum(image_lengths, axis=-1, dtype=jnp.int32)
    places = jnp.arange(row_len, dtype=jnp.int32)
    return lax.optimization_barrier(jnp.sum((bounds[:, None, :] <= places[None, :, None]).astype(jnp.int32), axis=-1, dtype=jnp.int32))

def visibility(segments):
    key_count = segments.shape[-1]
    matching = segments[:, :, None] == segments[:, None, :]
    open_key = segments[:, None, :] != SEGS - 1
    itself = jnp.eye(key_count, dtype=bool)[None]
    return matching & open_key | itself

def block_forward(hidden_in, params, visible):
    attention, upward, downward, vectors, bias_up = params
    groups, length, model_width = hidden_in.shape
    normed = low(layer_norm(hidden_in, vectors[0], vectors[1]))
    queries = low(low_back(dense(normed, attention[0]) + vectors[2]))
    key_rows = low(low_back(dense(normed, attention[1])))
    value_rows = low(low_back(dense(normed, attention[2]) + vectors[3]))
    head_shape = (groups, length, HEADS, HEAD_DIM)
    scores = jnp.einsum('gqhd,gkhd->ghqk', queries.reshape(head_shape), key_rows.reshape(head_shape), precision=lax.Precision.HIGHEST)
    scores = low_back(scores * SCALE_SCORE)
    scores = jnp.where(visible[:, None], scores, -1e+30)
    weights = low(jax.nn.softmax(scores, axis=-1))
    mixture = jnp.einsum('ghqk,gkhd->gqhd', weights, value_rows.reshape(head_shape), precision=lax.Precision.HIGHEST)
    mixture = low(low_back(mixture.reshape(groups, length, model_width)))
    residual = hidden_in + low_back(dense(mixture, attention[3]) + vectors[4])
    normed_two = low(layer_norm(residual, vectors[5], vectors[6]))
    hidden_pre = low_back(dense(normed_two, upward) + bias_up)
    hidden_act = low(jax.nn.gelu(hidden_pre, approximate=False))
    return residual + low_back(dense(hidden_act, downward) + vectors[7])

def forward_all(params, hidden_in, visible):
    for level_index in range(LAYERS):
        hidden_in = block_forward(hidden_in, tuple((param[level_index] for param in params)), visible)
    return hidden_in

def optimizer_step(gradient, master, moment, average, step_rate):
    direction = gradient + DECAY_RATE * master
    moment_new = MOMENTUM_RATE * moment + direction
    master_new = master - step_rate * (direction + MOMENTUM_RATE * moment_new)
    average_new = AVERAGE_RATE * average + (1.0 - AVERAGE_RATE) * master_new
    return (gradient, moment_new, average_new, master_new, master_new.astype(jnp.bfloat16))

def reference(inputs, cotangent, image_lengths, attention_weight, attention_moment, attention_average, up_weight, up_moment, up_average, down_weight, down_moment, down_average, layer_vectors, vector_moment, vector_average, hidden_bias, bias_moment, bias_average):
    masters = (attention_weight, up_weight, down_weight, layer_vectors, hidden_bias)
    rounded = tuple((low(master) for master in masters))
    segments = segment_ids(image_lengths, ROW_LEN)
    group_rows = math.gcd(ROWS, max(1, 2048 // ROW_LEN))
    step_count = ROWS // group_rows

    def regroup(array):
        return array.reshape((step_count, group_rows) + array.shape[1:])

    def accumulate(totals, row_items):
        rows_in, rows_back, rows_seg = row_items
        visible = visibility(rows_seg)

        def forward_rows(params, values):
            return forward_all(params, values, visible)
        result, pullback = jax.vjp(forward_rows, rounded, rows_in)
        grad_params, grad_in = pullback(rows_back)
        totals = jax.tree.map(jnp.add, totals, grad_params)
        return (totals, (result.astype(jnp.bfloat16), grad_in.astype(jnp.bfloat16)))
    zeros = tuple((jnp.zeros_like(master) for master in rounded))
    sources = (regroup(inputs.astype(jnp.float32)), regroup(cotangent.astype(jnp.float32)), regroup(segments))
    grads_total, (results, grads_in) = lax.scan(accumulate, zeros, sources)
    output = results.reshape(ROWS, ROW_LEN, D)
    input_grad = grads_in.reshape(ROWS, ROW_LEN, D)
    step_rate = LEARN_BASE / math.sqrt(TOKENS)
    states = ((attention_weight, attention_moment, attention_average), (up_weight, up_moment, up_average), (down_weight, down_moment, down_average), (layer_vectors, vector_moment, vector_average), (hidden_bias, bias_moment, bias_average))
    outcome = [output, input_grad]
    for member in range(5):
        master, moment, average = states[member]
        outcome.extend(optimizer_step(grads_total[member], master, moment, average, step_rate))
    return tuple(outcome)
```

```python
import functools
import math

import jax
import jax.numpy as jnp
from jax import lax
from jax.experimental import pallas as pl
from jax.experimental.pallas import tpu as pltpu
from jax.sharding import PartitionSpec as P

HEAD_DIM = 64
SEGS = 8


EPSILON = 1e-06
SCALE_SCORE = 0.125
MOMENTUM_RATE = 0.9
DECAY_RATE = 0.0001
AVERAGE_RATE = 0.5
LEARN_BASE = 0.1
VMEM_BYTES = 66500000


def as_sent(shard):
    return jax.tree.map(lambda a: a.astype(jnp.bfloat16) if a.dtype == jnp.float32 else a, shard)


def layer_norm(values, gain_row, shift_row):
    center = values - jnp.mean(values, axis=-1, keepdims=True)
    spread = jnp.mean(center * center, axis=-1, keepdims=True)
    return center * lax.rsqrt(spread + EPSILON) * gain_row + shift_row


def gelu_exact(values):
    return jax.nn.gelu(values, approximate=False)


def project(values, matrix):
    return jnp.einsum("rti,ij->rtj", values, matrix, preferred_element_type=jnp.float32)


def project_back(grad_rows, matrix):
    return jnp.einsum("rtj,ij->rti", grad_rows, matrix, preferred_element_type=jnp.float32)


def outer_sum(values, grad_rows):
    return jnp.einsum("rti,rtj->ij", values, grad_rows, preferred_element_type=jnp.float32)


def column_sum(grad_rows):
    return jnp.sum(grad_rows, axis=(0, 1), dtype=jnp.float32)


def segment_ids(image_lengths, row_len):
    upto = jnp.arange(SEGS)[:, None] <= jnp.arange(SEGS)[None, :]
    bounds = jnp.sum(jnp.where(upto[None], image_lengths[:, :, None], 0), axis=1, dtype=jnp.int32)
    places = jnp.arange(row_len, dtype=jnp.int32)
    return jnp.sum(
        (bounds[:, None, :] <= places[None, :, None]).astype(jnp.int32), axis=-1, dtype=jnp.int32
    )


def visible_block(seg_rows, offset, block_size):
    row_len = seg_rows.shape[0]
    seg_query = seg_rows[offset : offset + block_size]
    matching = seg_query[:, None] == seg_rows[None, :]
    open_key = seg_rows[None, :] != SEGS - 1
    query_place = offset + jnp.arange(block_size, dtype=jnp.int32)
    key_place = jnp.arange(row_len, dtype=jnp.int32)
    return matching & open_key | (query_place[:, None] == key_place[None, :])


def score_block(query_block, key_heads, seg_rows, offset):
    scores = (
        jnp.einsum("qhd,khd->hqk", query_block, key_heads, preferred_element_type=jnp.float32)
        * SCALE_SCORE
    )
    allowed = visible_block(seg_rows, offset, query_block.shape[0])
    return jnp.where(allowed[None], scores, -1e30)


def split_heads(row_values):
    return row_values.reshape(row_values.shape[0], row_values.shape[1] // HEAD_DIM, HEAD_DIM)


def attend_row(row_items):
    query_row, key_row, value_row, seg_rows = row_items
    row_len = query_row.shape[0]
    query_heads = split_heads(query_row)
    key_heads = split_heads(key_row)
    value_heads = split_heads(value_row)
    block_size = min(512, row_len)
    outputs = []
    totals = []
    for offset in range(0, row_len, block_size):
        scores = score_block(query_heads[offset : offset + block_size], key_heads, seg_rows, offset)
        top_score = jnp.max(scores, axis=-1, keepdims=True)
        exponent = jnp.exp(scores - top_score)
        denominator = jnp.sum(exponent, axis=-1, keepdims=True)
        probability = (exponent / denominator).astype(jnp.bfloat16)
        outputs.append(
            jnp.einsum("hqk,khd->qhd", probability, value_heads, preferred_element_type=jnp.float32)
        )
        totals.append(top_score[..., 0] + jnp.log(denominator[..., 0]))
    mixture = jnp.concatenate(outputs, axis=0).reshape(query_row.shape).astype(jnp.bfloat16)
    return (mixture, jnp.concatenate(totals, axis=1))


def attend_back(row_items):
    query_row, key_row, value_row, grad_row, log_total, seg_rows = row_items
    row_len = query_row.shape[0]
    query_heads = split_heads(query_row)
    key_heads = split_heads(key_row)
    value_heads = split_heads(value_row)
    grad_heads = split_heads(grad_row)
    block_size = min(512, row_len)
    key_grad = jnp.zeros(key_heads.shape, jnp.float32)
    value_grad = jnp.zeros(value_heads.shape, jnp.float32)
    query_grads = []
    for offset in range(0, row_len, block_size):
        query_block = query_heads[offset : offset + block_size]
        grad_block = grad_heads[offset : offset + block_size]
        scores = score_block(query_block, key_heads, seg_rows, offset)
        probability = jnp.exp(scores - log_total[:, offset : offset + block_size, None])
        prob_low = probability.astype(jnp.bfloat16)
        prob_grad = jnp.einsum(
            "qhd,khd->hqk", grad_block, value_heads, preferred_element_type=jnp.float32
        )
        inner_sum = jnp.sum(probability * prob_grad, axis=-1, keepdims=True)
        score_grad = (probability * (prob_grad - inner_sum)).astype(jnp.bfloat16)
        query_grads.append(
            jnp.einsum("hqk,khd->qhd", score_grad, key_heads, preferred_element_type=jnp.float32)
            * SCALE_SCORE
        )
        key_grad = (
            key_grad
            + jnp.einsum(
                "hqk,qhd->khd", score_grad, query_block, preferred_element_type=jnp.float32
            )
            * SCALE_SCORE
        )
        value_grad = value_grad + jnp.einsum(
            "hqk,qhd->khd", prob_low, grad_block, preferred_element_type=jnp.float32
        )
    flat_shape = query_row.shape
    query_grad = jnp.concatenate(query_grads, axis=0)
    return (
        query_grad.reshape(flat_shape).astype(jnp.bfloat16),
        key_grad.reshape(flat_shape).astype(jnp.bfloat16),
        value_grad.reshape(flat_shape).astype(jnp.bfloat16),
    )


def layer_forward(hidden_in, params, seg_full):
    attention, upward, downward, vectors, bias_up = params
    vector_values = vectors.astype(jnp.float32)
    normed = layer_norm(hidden_in, vector_values[0], vector_values[1]).astype(jnp.bfloat16)
    queries = (project(normed, attention[0]) + vector_values[2]).astype(jnp.bfloat16)
    key_rows = project(normed, attention[1]).astype(jnp.bfloat16)
    value_rows = (project(normed, attention[2]) + vector_values[3]).astype(jnp.bfloat16)
    query_full, key_full, value_full = (
        lax.all_to_all(queries, "seq", split_axis=2, concat_axis=1, tiled=True),
        lax.all_to_all(key_rows, "seq", split_axis=2, concat_axis=1, tiled=True),
        lax.all_to_all(value_rows, "seq", split_axis=2, concat_axis=1, tiled=True),
    )
    mixture, log_total = lax.map(attend_row, (query_full, key_full, value_full, seg_full))
    mixed_tokens = lax.all_to_all(mixture, "seq", split_axis=1, concat_axis=2, tiled=True)
    residual = hidden_in + (project(mixed_tokens, attention[3]) + vector_values[4])
    normed_two = layer_norm(residual, vector_values[5], vector_values[6]).astype(jnp.bfloat16)
    hidden_pre = project(normed_two, upward) + bias_up.astype(jnp.float32)
    hidden_act = gelu_exact(hidden_pre).astype(jnp.bfloat16)
    result = residual + (project(hidden_act, downward) + vector_values[7])
    saved_values = (
        hidden_in,
        normed,
        query_full,
        key_full,
        value_full,
        log_total,
        mixed_tokens,
        residual,
        normed_two,
        hidden_pre,
        hidden_act,
    )
    return (result, saved_values)


def layer_backward(grad_out, params, saved_values, seg_full):
    attention, upward, downward, vectors, bias_up = params
    vector_values = vectors.astype(jnp.float32)
    (
        hidden_in,
        normed,
        query_full,
        key_full,
        value_full,
        log_total,
        mixed_tokens,
        residual,
        normed_two,
        hidden_pre,
        hidden_act,
    ) = saved_values
    grad_mlp = grad_out.astype(jnp.bfloat16)
    grad_down = outer_sum(hidden_act, grad_mlp)
    grad_act = project_back(grad_mlp, downward)
    grad_pre = jax.vjp(gelu_exact, hidden_pre)[1](grad_act)[0].astype(jnp.bfloat16)
    grad_up = outer_sum(normed_two, grad_pre)
    grad_normed_two = project_back(grad_pre, upward)
    norm_pull_two = jax.vjp(layer_norm, residual, vector_values[5], vector_values[6])[1]
    grad_resid_norm, grad_gain_two, grad_shift_two = norm_pull_two(grad_normed_two)
    grad_residual = grad_out + grad_resid_norm
    grad_proj = grad_residual.astype(jnp.bfloat16)
    grad_outproj = outer_sum(mixed_tokens, grad_proj)
    grad_mixed = project_back(grad_proj, attention[3]).astype(jnp.bfloat16)
    grad_heads = lax.all_to_all(grad_mixed, "seq", split_axis=2, concat_axis=1, tiled=True)
    query_grad, key_grad, value_grad = lax.map(
        attend_back, (query_full, key_full, value_full, grad_heads, log_total, seg_full)
    )
    grad_query, grad_key, grad_value = (
        lax.all_to_all(query_grad, "seq", split_axis=1, concat_axis=2, tiled=True),
        lax.all_to_all(key_grad, "seq", split_axis=1, concat_axis=2, tiled=True),
        lax.all_to_all(value_grad, "seq", split_axis=1, concat_axis=2, tiled=True),
    )
    grad_wq = outer_sum(normed, grad_query)
    grad_wk = outer_sum(normed, grad_key)
    grad_wv = outer_sum(normed, grad_value)
    grad_normed = (
        project_back(grad_query, attention[0])
        + project_back(grad_key, attention[1])
        + project_back(grad_value, attention[2])
    )
    norm_pull_one = jax.vjp(layer_norm, hidden_in, vector_values[0], vector_values[1])[1]
    grad_in_norm, grad_gain_one, grad_shift_one = norm_pull_one(grad_normed)
    grad_in = grad_residual + grad_in_norm
    attention_terms = jnp.stack([grad_wq, grad_wk, grad_wv, grad_outproj])
    vector_terms = jnp.stack(
        [
            grad_gain_one,
            grad_shift_one,
            column_sum(grad_query),
            column_sum(grad_value),
            column_sum(grad_proj),
            grad_gain_two,
            grad_shift_two,
            column_sum(grad_mlp),
        ]
    )
    return (grad_in, (attention_terms, grad_up, grad_down, vector_terms, column_sum(grad_pre)))


def fold_terms(terms, dims, dp_count, seq_count):
    folded = []
    for member in range(len(terms)):
        term = terms[member]
        place = dims[member]
        shape = term.shape
        leading = math.prod(shape[:place])
        owned = shape[place] // (dp_count * seq_count)
        trailing = owned * math.prod(shape[place + 1 :])
        folded.append(term.reshape(leading, dp_count, seq_count, trailing))
    return tuple(folded)


def unfold_terms(received, terms, dims, dp_count, seq_count):
    results = []
    for member in range(len(terms)):
        shape = terms[member].shape
        place = dims[member]
        owned_shape = shape[:place] + (shape[place] // (dp_count * seq_count),) + shape[place + 1 :]
        results.append(jnp.sum(received[member], axis=(1, 2)).reshape(owned_shape))
    return tuple(results)


def optimizer_step(gradient, master, moment, average, step_rate):
    direction = gradient + DECAY_RATE * master
    moment_new = MOMENTUM_RATE * moment + direction
    master_new = master - step_rate * (direction + MOMENTUM_RATE * moment_new)
    average_new = AVERAGE_RATE * average + (1.0 - AVERAGE_RATE) * master_new
    return (gradient, moment_new, average_new, master_new, master_new.astype(jnp.bfloat16))


def plain_step(inputs, cotangent, image_lengths, masters):
    layer_count = masters[0].shape[0]
    dp_count = lax.axis_size("dp")
    seq_count = lax.axis_size("seq")
    seg_full = segment_ids(image_lengths, inputs.shape[1] * seq_count)

    def gather_layer(level_index):
        pieces = tuple((master[level_index].astype(jnp.bfloat16) for master in masters))
        return (
            lax.all_gather(pieces[0], ("dp", "seq"), axis=1, tiled=True),
            lax.all_gather(pieces[1], ("dp", "seq"), axis=0, tiled=True),
            lax.all_gather(pieces[2], ("dp", "seq"), axis=0, tiled=True),
            lax.all_gather(pieces[3], ("dp", "seq"), axis=1, tiled=True),
            lax.all_gather(pieces[4], ("dp", "seq"), axis=0, tiled=True),
        )

    hidden = inputs.astype(jnp.float32)
    kept_params = []
    kept_saved = []
    for level_index in range(layer_count):
        params = gather_layer(level_index)
        hidden, saved_values = layer_forward(hidden, params, seg_full)
        kept_params.append(params)
        kept_saved.append(saved_values)
    output = hidden.astype(jnp.bfloat16)
    stack_dims = (2, 1, 1, 2, 1)
    grad_hidden = cotangent.astype(jnp.float32)
    layer_terms = [None] * layer_count
    for level_index in reversed(range(layer_count)):
        params = kept_params[level_index]
        grad_hidden, terms_here = layer_backward(
            grad_hidden, params, kept_saved[level_index], seg_full
        )
        layer_terms[level_index] = terms_here
    stacked = tuple(
        (jnp.stack([terms_here[member] for terms_here in layer_terms]) for member in range(5))
    )
    folded = fold_terms(stacked, stack_dims, dp_count, seq_count)
    received = jax.tree.map(
        lambda part, own: part.astype(own.dtype),
        lax.all_to_all(
            lax.all_to_all(as_sent(folded), "dp", split_axis=1, concat_axis=1, tiled=True),
            "seq",
            split_axis=2,
            concat_axis=2,
            tiled=True,
        ),
        folded,
    )
    reduced = unfold_terms(received, stacked, stack_dims, dp_count, seq_count)
    return (output, grad_hidden.astype(jnp.bfloat16), *reduced)


MESH = pl.DeviceIdType.MESH
F32 = jnp.float32
BF16 = jnp.bfloat16
KEYS = 896
QBLOCK = 256


def nt(left, right):
    return lax.dot_general(left, right, (((1,), (1,)), ((), ())), preferred_element_type=F32)


def nn(left, right):
    return lax.dot_general(left, right, (((1,), (0,)), ((), ())), preferred_element_type=F32)


def tn(left, right):
    return lax.dot_general(left, right, (((0,), (0,)), ((), ())), preferred_element_type=F32)


def norm_parts(values):
    center = values - jnp.mean(values, axis=-1, keepdims=True)
    scale = lax.rsqrt(jnp.mean(center * center, axis=-1, keepdims=True) + EPSILON)
    return center * scale, scale


def norm_back(values, grad, gain):
    unit, scale = norm_parts(values)
    pulled = grad * gain
    first = jnp.mean(pulled, axis=-1, keepdims=True)
    second = jnp.mean(pulled * unit, axis=-1, keepdims=True)
    result = scale * (pulled - first - unit * second)
    return (
        result,
        jnp.sum(grad * unit, axis=0, keepdims=True),
        jnp.sum(grad, axis=0, keepdims=True),
    )


SEMS = 400


def step_kernel(NZ, x_in, cot_in, lens, aw, uw, dw, lv, hb, *rest):
    (out, gin, gA, gU, gD, gV, gB) = rest[:7]
    (
        w1, w2, w3, w4, stg, rsl, gm, a, b, qh, kk, vv, kT, vT, oh, ofull, goh, gos, gpo, lse,
        x1, xs, hact, gpb, segc, segr, facc, gq, gw1, gw2, gw3, gw4, gw5, xl1, xl2, xl3, xl4, xl5,
        zl1, zl2, zl3, zl4, zl5, ps1, ps2, ps3, ps5, pl1, pl2, pl3, pl5, tt, V, vg, snd, rcv,
        credx, credz,
    ) = rest[7:]
    W = {1: w1, 2: w2, 3: w3, 4: w4}
    GW = {1: gw1, 2: gw2, 3: gw3, 4: gw4, 5: gw5}
    XL = {1: xl1, 2: xl2, 3: xl3, 4: xl4, 5: xl5}
    ZL = {1: zl1, 2: zl2, 3: zl3, 4: zl4, 5: zl5}
    PS = {1: ps1, 2: ps2, 3: ps3, 5: ps5}
    PL = {1: pl1, 2: pl2, 3: pl3, 5: pl5}
    S = 4
    T, D = x_in.shape[1], x_in.shape[2]
    R = aw.shape[2]
    CH = R * S
    DP = NZ * 2
    FJ = hb.shape[1]

    d = lax.axis_index("dp")
    s = lax.axis_index("seq")
    z, x = d // 2, d % 2
    y, c = s // 2, s % 2
    xp = 1 - x

    def xor(k):
        return ((y + k // 2) % 2) * 2 + (c + k % 2) % 2

    def dev(dd, ss):
        return {"dp": dd, "seq": ss}

    core_peer, y_peer, x_peer = dev(d, xor(1)), dev(d, xor(2)), dev(z * 2 + xp, s)

    def zdev(dz):
        return dev(((z + dz) % NZ) * 2 + x, s)

    count = [0]

    def sems(n):
        first = count[0]
        count[0] += n
        assert count[0] <= SEMS
        return first

    def rc(src, dst, device, i):
        return pltpu.make_async_remote_copy(
            src_ref=src, dst_ref=dst, send_sem=snd.at[i], recv_sem=rcv.at[i],
            device_id=device, device_id_type=MESH,
        )

    pending = []
    sent_weights = []

    def flush():
        for copy in pending:
            copy.wait_send()
        pending.clear()

    def rows(i):
        return pl.ds(pl.multiple_of(i * T, T), T)

    def chunk(i):
        return pl.ds(pl.multiple_of(i * CH, CH), CH)

    class Gather:
        def __init__(self, view):
            i = sems(3)
            own, across = view.at[rows(s)], view.at[rows(xor(2))]
            self.c1 = rc(own, own, core_peer, i)
            self.c2 = rc(own, own, y_peer, i + 1)
            self.c3 = rc(across, across, core_peer, i + 2)

        def start(self):
            self.c2.start()
            self.c1.start()

        def core(self):
            self.c1.wait_recv()

        def forward(self):
            self.c2.wait_recv()
            self.c3.start()

        def last(self):
            self.c3.wait_recv()

        def done(self):
            pending.extend([self.c1, self.c2, self.c3])

    ag_sems = {}

    def ag_start(g, l):
        zi, xi = sems(NZ), sems(NZ)
        ag_sems[g, l] = (zi, xi)
        own = W[g].at[l, chunk(d)]
        for dz in range(1, NZ):
            rc(own, own, zdev(dz), zi + dz).start()
            sent_weights.append((g, zi + dz))

    def ag_forward(g, l):
        zi, xi = ag_sems[g, l]
        for dz in range(NZ):
            part = W[g].at[l, chunk(((z - dz + NZ) % NZ) * 2 + x)]
            if dz:
                rc(part, part, zdev(dz), zi + dz).wait_recv()
            rc(part, part, x_peer, xi + dz).start()
            sent_weights.append((g, xi + dz))

    def ag_done(g, l):
        xi = ag_sems[g, l][1]
        for dz in range(NZ):
            part = W[g].at[l, chunk(dz)]
            rc(part, part, x_peer, xi + dz).wait_recv()

    red_sems = {}

    def x_copies(g, l):
        i = red_sems[g, l]
        return [rc(GW[g].at[chunk(zi * 2 + xp)], XL[g].at[zi], x_peer, i + zi) for zi in range(NZ)]

    def z_copies(g, l):
        i = red_sems[g, l] + NZ
        return [
            rc(GW[g].at[chunk(((z + dz) % NZ) * 2 + x)], ZL[g].at[dz - 1], zdev(dz), i + dz)
            for dz in range(1, NZ)
        ]

    def s_copies(g, l):
        i = red_sems[g, l] + 2 * NZ
        return [
            rc(PS[g].at[(s + ds) % S], PL[g].at[s], dev(d, (s + ds) % S), i + ds)
            for ds in range(1, S)
        ]

    def red_x(g, l):
        if l == 0 and g != 5:
            pl.semaphore_wait(credx.at[g], 1)
        red_sems[g, l] = sems(2 * NZ + S)
        for copy in x_copies(g, l):
            copy.start()

    def red_z(g, l):
        for zi, copy in enumerate(x_copies(g, l)):
            copy.wait_recv()
            mine = chunk(zi * 2 + x)
            GW[g][mine] = (GW[g][mine].astype(F32) + XL[g][zi].astype(F32)).astype(BF16)
        if l == 1 and g != 5:
            pl.semaphore_signal(credx.at[g], 1, device_id=x_peer, device_id_type=MESH)
        if l == 0 and g != 5:
            pl.semaphore_wait(credz.at[g], NZ - 1)
        for copy in z_copies(g, l):
            copy.start()

    def red_sum(g, l):
        total = GW[g][chunk(d)].astype(F32)
        for k, copy in enumerate(z_copies(g, l)):
            copy.wait_recv()
            total = total + ZL[g][k].astype(F32)
        for copy in x_copies(g, l) + z_copies(g, l):
            copy.wait_send()
        if l == 1 and g != 5:
            for dz in range(1, NZ):
                pl.semaphore_signal(credz.at[g], 1, device_id=zdev(dz), device_id_type=MESH)
        if g == 4:
            gD[l] = total
            return
        if g == 5:
            tt[0:CH, :] = total
        wide = total.shape[1]
        for k in range(S):
            piece = jnp.concatenate(
                [total[R * k : R * (k + 1)], jnp.zeros((PS[g].shape[1] - R, wide), F32)], axis=0
            )
            PS[g][k] = piece.astype(BF16)
        PL[g][s] = PS[g][s]
        for copy in s_copies(g, l):
            copy.start()

    def red_write(g, l):
        for copy in s_copies(g, l):
            copy.wait_recv()
        parts = [PL[g][k].astype(F32)[0:R] for k in range(S)]
        if g == 1:
            gA[l, 0] = jnp.concatenate([p[:, 0:192] for p in parts], axis=1)
            gA[l, 1] = jnp.concatenate(
                [q for p in parts for q in (p[:, 256:384], p[:, 192:256])], axis=1
            )
            gA[l, 2] = jnp.concatenate([p[:, 384:576] for p in parts], axis=1)
        elif g == 2:
            gA[l, 3] = parts[0] + parts[1] + parts[2] + parts[3]
        elif g == 3:
            gU[l] = jnp.concatenate(
                [parts[k][:, FJ * i : FJ * (i + 1)] for i in range(DP) for k in range(S)], axis=1
            )
        else:
            biases = jnp.transpose(tt[...])
            tt[0:R, :] = parts[0] + parts[1] + parts[2] + parts[3]
            vectors = jnp.transpose(tt[...])
            for k in range(2):
                gV[k] = vectors[16 * k : 16 * k + 8, 0:R]
                gB[k : k + 1, :] = biases[16 * k + 8 : 16 * k + 9, 0:CH]
        for copy in s_copies(g, l):
            copy.wait_send()

    parity = [0]

    class Scatter:
        def __init__(self):
            i = sems(3)
            base = parity[0] * 3
            parity[0] = 1 - parity[0]
            self.base = base
            self.r0 = rc(stg.at[0:T], rsl.at[base], core_peer, i)
            self.r1 = rc(stg.at[T : 2 * T], rsl.at[base + 1], core_peer, i + 1)
            self.r2 = rc(stg.at[2 * T : 3 * T], rsl.at[base + 2], y_peer, i + 2)

        def send_core(self, j):
            k = 0 if j == 3 else 1
            stg[T * k : T * (k + 1)] = facc[T * j : T * (j + 1)].astype(BF16)
            (self.r0 if j == 3 else self.r1).start()

        def send_y(self):
            self.r0.wait_recv()
            stg[2 * T : 3 * T] = (
                facc[2 * T : 3 * T] + rsl[self.base].astype(F32)
            ).astype(BF16)
            self.r2.start()

        def finish(self):
            self.r1.wait_recv()
            self.r2.wait_recv()
            total = facc[0:T] + rsl[self.base + 1].astype(F32) + rsl[self.base + 2].astype(F32)
            for copy in (self.r0, self.r1, self.r2):
                copy.wait_send()
            return total

    barrier = pltpu.get_barrier_semaphore()
    greeted = [core_peer, y_peer, dev(d, xor(3)), x_peer] + [zdev(dz) for dz in range(1, NZ)]
    for device in greeted:
        pl.semaphore_signal(barrier, inc=1, device_id=device, device_id_type=MESH)

    tt[...] = jnp.zeros_like(tt)
    tt[64:72, 0:R] = lv[0]
    tt[72:80, 0:R] = lv[1]
    tt[80:82, 0:CH] = hb[...]
    turned = jnp.transpose(tt[...])
    lane128 = lax.broadcasted_iota(jnp.int32, (1, 128), 1)
    vec_cols = jnp.where(lane128 < 80, turned[0:R, :], 0.0)[:, 64:128]
    bias_cols = jnp.where((lane128 >= 80) & (lane128 < 82), turned[0:CH, :], 0.0)
    for k in range(S):
        o = 192 * k
        two = []
        for l in range(2):
            wq, wk, wv = aw[l, 0], aw[l, 1], aw[l, 2]
            tail = vec_cols if l == 0 else jnp.zeros((R, 64), F32)
            two.append(
                jnp.concatenate(
                    [wq[:, o : o + 192], wk[:, o + 128 : o + 192], wk[:, o : o + 128],
                     wv[:, o : o + 192], tail],
                    axis=1,
                )
            )
        stg[144 * k : 144 * k + 48, 0:640] = jnp.concatenate(two, axis=0).astype(BF16)
    gm[0, rows(s)] = x_in[0]

    pl.semaphore_wait(barrier, len(greeted))

    def piece_rows(k):
        return pl.multiple_of(k * 144, 16)

    i = sems(S)
    pieces1 = []
    for ds in (2, 3, 1):
        to = xor(ds)
        copy = rc(stg.at[pl.ds(piece_rows(to), 48), 0:640], rsl.at[s, 0:48, 0:640], dev(d, to), i + ds)
        copy.start()
        pieces1.append(copy)
    gather_x = Gather(gm.at[0])
    gather_x.start()
    for k in range(S):
        two = [
            jnp.concatenate(
                [uw[l][:, (m * S + k) * FJ : (m * S + k + 1) * FJ] for m in range(DP)], axis=1
            )
            for l in range(2)
        ]
        stg[144 * k + 48 : 144 * k + 96, :] = jnp.concatenate([aw[0, 3], aw[1, 3]], axis=0).astype(BF16)
        stg[144 * k + 96 : 144 * k + 144, :] = jnp.concatenate(two, axis=0).astype(BF16)
    i = sems(S)
    pieces2 = []
    for ds in (2, 3, 1):
        to = xor(ds)
        copy = rc(
            stg.at[pl.ds(pl.multiple_of(piece_rows(to) + 48, 16), 96), :],
            rsl.at[s, 48:144, :], dev(d, to), i + ds,
        )
        copy.start()
        pieces2.append(copy)
    rsl[s, 0:48, 0:640] = stg[pl.ds(piece_rows(s), 48), 0:640]
    rsl[s, 48:144, :] = stg[pl.ds(pl.multiple_of(piece_rows(s) + 48, 16), 96), :]
    vg[...] = jnp.zeros_like(vg)
    for l in range(2):
        w4[l, chunk(d)] = dw[l].astype(BF16)
    for copy in pieces1:
        copy.wait_recv()
    got = [rsl[k, 0:48, 0:640].astype(F32) for k in range(S)]
    for l in range(2):
        full = jnp.concatenate([g[R * l : R * (l + 1)] for g in got], axis=0)
        if l == 0:
            full = jnp.concatenate([full[:, 0:512], full[:, 512:640] + bias_cols], axis=1)
        w1[l, chunk(d)] = full.astype(BF16)
    ag_start(1, 0)

    bounds = []
    running = jnp.int32(0)
    for k in range(SEGS):
        running = running + lens[0, k]
        bounds.append(running)
    N = S * T

    def segments(shape, dim):
        place = lax.broadcasted_iota(jnp.int32, shape, dim)
        seg = jnp.zeros(shape, jnp.int32)
        for bound in bounds:
            seg = seg + jnp.where(place >= bound, 1, 0)
        return jnp.where(seg == SEGS - 1, SEGS + place, seg)

    segr[...] = segments((8, N), 1)
    segc[...] = segments((N, 128), 0)

    for copy in pieces2:
        copy.wait_recv()
    for g, at in ((2, 48), (3, 96)):
        got = [rsl[k, at : at + 48, :].astype(F32) for k in range(S)]
        for l in range(2):
            W[g][l, chunk(d)] = jnp.concatenate(
                [part[R * l : R * (l + 1)] for part in got], axis=0
            ).astype(BF16)
    for copy in pieces1 + pieces2:
        copy.wait_send()
    ag_start(2, 0)
    ag_forward(1, 0)
    ag_start(3, 0)
    gather_x.core()
    gather_x.forward()
    gm[1, rows(s)] = cot_in[0]
    ag_done(1, 0)
    V[...] = jnp.transpose(w1[0, :, 512:640].astype(F32))[64:96]
    gather_x.last()
    gather_x.done()

    def vec(l, k):
        return V[8 * l + k : 8 * l + k + 1, :]

    def own_heads(row):
        total = jnp.zeros((1, 192), F32)
        for k in range(S):
            total = total + jnp.where(s == k, row[:, 192 * k : 192 * (k + 1)], 0.0)
        return total

    def at_heads(part):
        total = jnp.zeros((1, D), F32)
        for k in range(S):
            spread = [jnp.zeros((1, 192), F32)] * S
            spread[k] = part
            total = total + jnp.where(s == k, jnp.concatenate(spread, axis=1), 0.0)
        return total

    low = lax.broadcasted_iota(jnp.int32, (T, 128), 1) < 64
    low_rows = lax.broadcasted_iota(jnp.int32, (128, QBLOCK), 0) < 64

    def project_heads(l):
        bias = jnp.concatenate(
            [own_heads(vec(l, 2)), jnp.zeros((1, 192), F32), own_heads(vec(l, 3)), jnp.zeros((1, 64), F32)],
            axis=1,
        )

        @pl.loop(0, S)
        def _(i):
            r = rows(i)
            if l == 0:
                unit, _ = norm_parts(gm[0, r].astype(F32))
                a[0, r] = (unit * vec(0, 0) + vec(0, 1)).astype(BF16)
            full = (nn(a[l, r], w1[l]) + bias).astype(BF16).astype(F32)
            t0, t1, t2, t3, t4 = (full[:, 128 * j : 128 * (j + 1)] for j in range(5))
            t1r = pltpu.roll(t1, 64, 1)
            v4 = jnp.where(low, t4, 0.0)
            qh[l, 0, r] = (jnp.where(low, t0, 0.0) * SCALE_SCORE).astype(BF16)
            qh[l, 1, r] = (jnp.where(low, 0.0, t0) * SCALE_SCORE).astype(BF16)
            qh[l, 2, r] = (jnp.where(low, t1, 0.0) * SCALE_SCORE).astype(BF16)
            kk[l, 0, r] = t2.astype(BF16)
            kk[l, 1, r] = t1r.astype(BF16)
            vv[l, 0, r] = t3.astype(BF16)
            vv[l, 1, r] = v4.astype(BF16)
            kT[l, 0, :, r] = jnp.transpose(t2).astype(BF16)
            kT[l, 1, :, r] = jnp.transpose(t1r).astype(BF16)
            vT[0, :, r] = jnp.transpose(t3).astype(BF16)
            vT[1, :, r] = jnp.transpose(v4).astype(BF16)

    def query_block(qb):
        q = pl.ds(pl.multiple_of(qb * QBLOCK, QBLOCK), QBLOCK)
        k = pl.ds(pl.multiple_of((qb // 2) * (N - KEYS), 128), KEYS)
        return q, k

    def attend(l, points):
        @pl.loop(0, N // QBLOCK)
        def _(qb):
            for at, action in points.items():
                pl.when(qb == at)(action)
            q, k = query_block(qb)
            allowed = jnp.concatenate([segc[k, :]] * 2, axis=1) == segr[0:1, q]
            parts = []
            for h in range(3):
                scores = jnp.where(allowed, nt(kk[l, h // 2, k], qh[l, h, q]), -1e30)
                top = jnp.max(scores, axis=0, keepdims=True)
                grown = jnp.exp(scores - top)
                total = jnp.sum(grown, axis=0, keepdims=True)
                lse[l, h : h + 1, q] = top + jnp.log(total)
                parts.append(nn(vT[h // 2, :, k], grown.astype(BF16)) / total)
            oh[l, q, 0:128] = jnp.transpose(jnp.where(low_rows, parts[0], parts[1])).astype(BF16)
            oh[l, q, 128:256] = jnp.transpose(parts[2]).astype(BF16)

    def attend_grad(l, points):
        facc[:, 0:512] = jnp.zeros((N, 512), F32)

        @pl.loop(0, N // QBLOCK)
        def _(qb):
            for at, action in points.items():
                pl.when(qb == at)(action)
            q, k = query_block(qb)
            allowed = jnp.concatenate([segc[k, :]] * 2, axis=1) == segr[0:1, q]
            tiles = [goh[q, 0:128], goh[q, 128:256]]
            inner = [
                jnp.transpose(tiles[j].astype(F32) * oh[l, q, 128 * j : 128 * (j + 1)].astype(F32))
                for j in range(2)
            ]
            inner = [
                jnp.sum(inner[0][0:64], axis=0, keepdims=True),
                jnp.sum(inner[0][64:128], axis=0, keepdims=True),
                jnp.sum(inner[1], axis=0, keepdims=True),
            ]
            t0 = tiles[0].astype(F32)
            heads = [
                jnp.where(low, t0, 0.0).astype(BF16),
                jnp.where(low, 0.0, t0).astype(BF16),
                tiles[1],
            ]
            parts = []
            for h in range(3):
                p = h // 2
                queries = qh[l, h, q]
                scores = jnp.where(allowed, nt(kk[l, p, k], queries), -1e30)
                prob = jnp.exp(scores - lse[l, h : h + 1, q])
                grad = nt(vv[l, p, k], heads[h])
                grad = (prob * (grad - inner[h])).astype(BF16)
                facc[k, 256 + 128 * p : 384 + 128 * p] += nn(prob.astype(BF16), heads[h])
                facc[k, 128 * p : 128 * (p + 1)] += nn(grad, queries)
                parts.append(nn(kT[l, p, :, k], grad) * SCALE_SCORE)
            gq[q, 0:128] = jnp.transpose(jnp.where(low_rows, parts[0], parts[1])).astype(BF16)
            gq[q, 128:256] = jnp.transpose(jnp.where(low_rows, parts[2], 0.0)).astype(BF16)

        @pl.loop(0, S)
        def _(i):
            r = rows(i)
            other = pltpu.roll(facc[r, 128:256], 64, 1)
            gq[r, 128:256] = (gq[r, 128:256].astype(F32) + other).astype(BF16)
            gq[r, 256:384] = facc[r, 0:128].astype(BF16)
            gq[r, 384:512] = facc[r, 256:384].astype(BF16)
            gq[r, 512:640] = facc[r, 384:512].astype(BF16)

    def exchange(source, target):
        i = sems(S)
        copies = []
        for ds in (2, 3, 1):
            to = xor(ds)
            part = source(to)
            copies.append(rc(part, target(s), dev(d, to), i + ds))
        for copy in copies:
            copy.start()
        return copies

    def mlp_forward(l, gather):
        scatter = Scatter()

        @pl.loop(0, S)
        def _(k):
            pl.when(k == 1)(gather.core)
            pl.when(k == 2)(gather.forward)
            pl.when(k == 3)(gather.last)
            r = rows(((y + k // 2) % 2) * 2 + (c + k % 2) % 2)
            pre = nn(b[l, r], w3[l]) + V[16 + l : 17 + l, :]
            cdf = 0.5 * (1.0 + lax.erf(pre * 0.7071067811865476))
            density = jnp.exp(-0.5 * pre * pre) * 0.3989422804014327
            act = (pre * cdf).astype(BF16)
            hact[l, r] = act
            gpb[l, r] = (cdf + pre * density).astype(BF16)
            facc[rows(k)] = nn(act, w4[l])
            pl.when(k == 1)(lambda: scatter.send_core(1))
            pl.when(k == 3)(lambda: scatter.send_core(3))

        gather.done()
        scatter.send_y()
        return scatter

    def mlp_backward(l, gather):
        scatter = Scatter()
        @pl.loop(0, S, init_carry=jnp.zeros((1, D), F32))
        def bias_grad(i, carry):
            if gather is None:
                k = S - 1 - i
            else:
                k = i
                pl.when(k == 1)(gather.core)
                pl.when(k == 2)(gather.forward)
                pl.when(k == 3)(gather.last)
            r = rows(((y + k // 2) % 2) * 2 + (c + k % 2) % 2)
            grad_act = nt(gm[l, r], w4[l])
            grad_pre = (grad_act * gpb[l, r].astype(F32)).astype(BF16)
            gpb[l, r] = grad_pre
            facc[rows(k)] = nt(grad_pre, w3[l])
            pl.when(k == 1)(lambda: scatter.send_core(1))
            pl.when(k == 3)(lambda: scatter.send_core(3))
            if gather is None:
                pl.when(k == 2)(scatter.send_y)
            return carry + jnp.sum(grad_pre.astype(F32), axis=0, keepdims=True)

        vg[16 * l + 8 : 16 * l + 9, :] = bias_grad
        if gather is not None:
            gather.done()
            scatter.send_y()
        return scatter

    def weight_grad(g, left, right):
        @pl.loop(0, 2)
        def _(i):
            m = pl.ds(pl.multiple_of(i * 384, 384), 384)
            GW[g][m, :] = tn(left(m), right()).astype(BF16)

    def heads_input_grad(l):
        scatter = Scatter()

        @pl.loop(0, S)
        def _(i):
            k = S - 1 - i
            r = rows(((y + k // 2) % 2) * 2 + (c + k % 2) % 2)
            facc[rows(k)] = nt(gq[r], w1[l])
            pl.when(k == 1)(lambda: scatter.send_core(1))
            pl.when(k == 3)(lambda: scatter.send_core(3))
            pl.when(k == 2)(scatter.send_y)

        return scatter

    def column(values):
        return jnp.sum(values.astype(F32), axis=0, keepdims=True)

    gather_cot = Gather(gm.at[1])
    gather_b = {}
    later = [
        lambda: (ag_forward(2, 0), ag_start(4, 0)),
        lambda: (ag_forward(3, 0), ag_start(1, 1)),
        lambda: (ag_forward(4, 0), ag_start(2, 1)),
        lambda: (ag_forward(1, 1), ag_start(3, 1)),
        lambda: (ag_forward(2, 1), ag_start(4, 1)),
        lambda: ag_forward(3, 1),
        lambda: ag_forward(4, 1),
    ]

    def do_later():
        later.pop(0)()

    for l in range(2):
        project_heads(l)
        if l == 0:
            gather_cot.start()
        do_later()
        if l == 0:
            def point():
                do_later()
                gather_cot.core()
                gather_cot.forward()
            attend(l, {2: point})
            gather_cot.last()
            gather_cot.done()
        else:
            attend(l, {2: do_later})
        copies = exchange(lambda to: oh.at[l, rows(to)], lambda me: goh.at[rows(me)])
        goh[rows(s)] = oh[l, rows(s)]
        pending.extend(copies)
        ag_done(2, l)
        for copy in copies:
            copy.wait_recv()
        ofull[l] = jnp.concatenate([goh[T * k : T * (k + 1)].astype(F32)[:, 0:192] for k in range(S)], axis=1).astype(BF16)
        before = x_in[0].astype(F32) if l == 0 else xs[...]
        middle = before + (nn(ofull[l], w2[l]) + vec(l, 4))
        x1[l] = middle
        unit, _ = norm_parts(middle)
        b[l, rows(s)] = (unit * vec(l, 5) + vec(l, 6)).astype(BF16)
        gather_b[l] = Gather(b.at[l])
        gather_b[l].start()
        if l == 0:
            do_later()
        ag_done(3, l)
        ag_done(4, l)
        scatter = mlp_forward(l, gather_b[l])
        if l == 0:
            do_later()
        after = x1[l] + (scatter.finish() + vec(l, 7))
        flush()
        if l == 0:
            xs[...] = after
            unit, _ = norm_parts(after)
            a[1, rows(s)] = (unit * vec(1, 0) + vec(1, 1)).astype(BF16)
            gather_a = Gather(a.at[1])
            gather_a.start()
            do_later()
            ag_done(1, 1)
            gather_a.core()
            gather_a.forward()
            gather_a.last()
            gather_a.done()
            do_later()
            later.insert(0, lambda: None)
        else:
            out[0] = after.astype(BF16)

    grad = cot_in[0].astype(F32)
    gather = None
    for l in (1, 0):
        first = l == 1
        scatter = mlp_backward(l, gather)
        if not first:
            red_write(2, 1)
            red_write(3, 1)
            red_sum(1, 1)
        vg[16 * l + 7 : 16 * l + 8, :] = column(gm[l, rows(s)])
        weight_grad(4, lambda m: hact[l, :, m], lambda: gm[l])
        red_x(4, l)
        weight_grad(3, lambda m: b[l, :, m], lambda: gpb[l])
        red_x(3, l)
        grad_b = scatter.finish()
        grad_x1, gain, shift = norm_back(x1[l], grad_b, vec(l, 5))
        if first:
            grad_x1 = grad_x1 + cot_in[0].astype(F32)
        else:
            grad_x1 = grad_x1 + xs[...]
        x1[l] = grad_x1
        vg[16 * l + 5 : 16 * l + 6, :] = gain
        vg[16 * l + 6 : 16 * l + 7, :] = shift
        gpo[...] = grad_x1.astype(BF16)
        vg[16 * l + 4 : 16 * l + 5, :] = column(gpo[...])
        flush()
        back = nt(gpo[...], w2[l])
        for k in range(S):
            gos[k] = jnp.concatenate(
                [back[:, 192 * k : 192 * (k + 1)], jnp.zeros((T, 64), F32)], axis=1
            ).astype(BF16)
        copies = exchange(lambda to: gos.at[to], lambda me: goh.at[rows(me)])
        goh[rows(s)] = gos[s]
        pending.extend(copies)
        if not first:
            red_write(1, 1)
        weight_grad(2, lambda m: ofull[l, :, m], lambda: gpo[...])
        red_x(2, l)
        red_z(4, l)
        for copy in copies:
            copy.wait_recv()

        def point_a():
            red_z(3, l)

        def point_b():
            red_z(2, l)

        attend_grad(l, {2: point_a, 3: point_b})
        sums = column(gq[...])
        vg[16 * l + 2 : 16 * l + 3, :] = at_heads(sums[:, 0:192])
        vg[16 * l + 3 : 16 * l + 4, :] = at_heads(sums[:, 384:576])
        scatter = heads_input_grad(l)
        weight_grad(1, lambda m: a[l, :, m], lambda: gq[...])
        red_x(1, l)
        red_sum(4, l)
        grad_a = scatter.finish()
        before = xs[...] if first else x_in[0].astype(F32)
        grad, gain, shift = norm_back(before, grad_a, vec(l, 0))
        grad = grad + x1[l]
        vg[16 * l : 16 * l + 1, :] = gain
        vg[16 * l + 1 : 16 * l + 2, :] = shift
        flush()
        if first:
            xs[...] = grad
            gm[0, rows(s)] = grad.astype(BF16)
            gather = Gather(gm.at[0])
            gather.start()
            red_sum(3, 1)
            red_sum(2, 1)
            red_z(1, 1)
        else:
            gin[0] = grad.astype(BF16)

    gw5[...] = jnp.transpose(vg[...]).astype(BF16)
    red_x(5, 0)
    red_sum(3, 0)
    red_sum(2, 0)
    red_z(1, 0)
    red_z(5, 0)
    red_write(3, 0)
    red_write(2, 0)
    red_sum(1, 0)
    red_sum(5, 0)
    red_write(1, 0)
    red_write(5, 0)
    flush()
    for g, i in sent_weights:
        part = W[g].at[0, 0:CH]
        rc(part, part, x_peer, i).wait_send()


def fused_step(inputs, cotangent, image_lengths, attention, upward, downward, vectors, bias_up):
    DP = lax.axis_size("dp")
    S = lax.axis_size("seq")
    NZ = DP // 2
    L = attention.shape[0]
    T, D = inputs.shape[1], inputs.shape[2]
    N = S * T
    R = attention.shape[2]
    CH = R * S
    RP = (R + 15) // 16 * 16
    FJ = bias_up.shape[1]
    vmem = pl.BlockSpec(memory_space=pltpu.VMEM)
    V = pltpu.VMEM
    widths = {1: 640, 2: D, 3: D, 4: D, 5: 128}
    scratch = [
        V((L, D, 640), BF16), V((L, D, D), BF16), V((L, D, D), BF16), V((L, D, D), BF16),
        V((3 * T, D), BF16),
        V((6, T, D), BF16),
        V((L, N, D), BF16), V((L, N, D), BF16), V((L, N, D), BF16),
        V((L, 3, N, 128), BF16), V((L, 2, N, 128), BF16), V((L, 2, N, 128), BF16),
        V((L, 2, 128, N), BF16), V((2, 128, N), BF16),
        V((L, N, 256), BF16), V((L, T, D), BF16),
        V((N, 256), BF16), V((S, T, 256), BF16), V((T, D), BF16),
        V((L, 8, N), F32),
        V((L, T, D), F32), V((T, D), F32),
        V((L, N, D), BF16), V((L, N, D), BF16),
        V((N, 128), jnp.int32), V((8, N), jnp.int32),
        V((N, D), F32),
        V((N, 640), BF16),
        *[V((D, widths[g]), BF16) for g in range(1, 6)],
        *[V((NZ, CH, widths[g]), BF16) for g in range(1, 6)],
        *[V((NZ - 1, CH, widths[g]), BF16) for g in range(1, 6)],
        *[V((S, RP, widths[g]), BF16) for g in (1, 2, 3, 5)],
        *[V((S, RP, widths[g]), BF16) for g in (1, 2, 3, 5)],
        V((128, 128), F32), V((32, D), F32), V((128, D), F32),
        pltpu.SemaphoreType.DMA((SEMS,)), pltpu.SemaphoreType.DMA((SEMS,)),
        pltpu.SemaphoreType.REGULAR((8,)), pltpu.SemaphoreType.REGULAR((8,)),
    ]
    return pl.pallas_call(
        functools.partial(step_kernel, NZ),
        out_shape=(
            jax.ShapeDtypeStruct(inputs.shape, BF16),
            jax.ShapeDtypeStruct(inputs.shape, BF16),
            jax.ShapeDtypeStruct(attention.shape, F32),
            jax.ShapeDtypeStruct(upward.shape, F32),
            jax.ShapeDtypeStruct(downward.shape, F32),
            jax.ShapeDtypeStruct(vectors.shape, F32),
            jax.ShapeDtypeStruct(bias_up.shape, F32),
        ),
        in_specs=[vmem, vmem, pl.BlockSpec(memory_space=pltpu.SMEM)] + [vmem] * 5,
        out_specs=(vmem,) * 7,
        scratch_shapes=scratch,
        compiler_params=pltpu.CompilerParams(
            collective_id=0, has_side_effects=True, vmem_limit_bytes=VMEM_BYTES
        ),
    )(inputs, cotangent, image_lengths, attention, upward, downward, vectors, bias_up)


def fits_fused(inputs, attention, upward, bias_up, dp_count, seq_count):
    own_rows, width = attention.shape[2], attention.shape[3]
    return (
        seq_count == 4
        and dp_count == 8
        and inputs.shape == (1, QBLOCK, 768)
        and width == 768
        and own_rows % 8 == 0
        and upward.shape[2] == seq_count * width
        and bias_up.shape[1] % 16 == 0
    )


def per_device(
    inputs,
    cotangent,
    image_lengths,
    attention_weight,
    attention_moment,
    attention_average,
    up_weight,
    up_moment,
    up_average,
    down_weight,
    down_moment,
    down_average,
    layer_vectors,
    vector_moment,
    vector_average,
    hidden_bias,
    bias_moment,
    bias_average,
):
    masters = (attention_weight, up_weight, down_weight, layer_vectors, hidden_bias)
    dp_count = lax.axis_size("dp")
    seq_count = lax.axis_size("seq")
    if fits_fused(inputs, attention_weight, up_weight, hidden_bias, dp_count, seq_count):
        output, input_grad, *reduced = fused_step(inputs, cotangent, image_lengths, *masters)
    else:
        output, input_grad, *reduced = plain_step(inputs, cotangent, image_lengths, masters)
    total_tokens = inputs.shape[0] * inputs.shape[1] * dp_count * seq_count
    step_rate = LEARN_BASE / math.sqrt(total_tokens)
    states = (
        (attention_weight, attention_moment, attention_average),
        (up_weight, up_moment, up_average),
        (down_weight, down_moment, down_average),
        (layer_vectors, vector_moment, vector_average),
        (hidden_bias, bias_moment, bias_average),
    )
    outcome = [output, input_grad]
    for member in range(5):
        master, moment, average = states[member]
        outcome.extend(optimizer_step(reduced[member], master, moment, average, step_rate))
    return tuple(outcome)


def solution(mesh):
    placed = (
        P("dp", "seq", None),
        P("dp", "seq", None),
        P("dp", None),
        P(None, None, ("dp", "seq"), None),
        P(None, None, ("dp", "seq"), None),
        P(None, None, ("dp", "seq"), None),
        P(None, ("dp", "seq"), None),
        P(None, ("dp", "seq"), None),
        P(None, ("dp", "seq"), None),
        P(None, ("dp", "seq"), None),
        P(None, ("dp", "seq"), None),
        P(None, ("dp", "seq"), None),
        P(None, None, ("dp", "seq")),
        P(None, None, ("dp", "seq")),
        P(None, None, ("dp", "seq")),
        P(None, ("dp", "seq")),
        P(None, ("dp", "seq")),
        P(None, ("dp", "seq")),
    )
    return jax.shard_map(
        per_device,
        mesh=mesh,
        in_specs=placed,
        out_specs=(
            P("dp", "seq", None),
            P("dp", "seq", None),
            P(None, None, ("dp", "seq"), None),
            P(None, None, ("dp", "seq"), None),
            P(None, None, ("dp", "seq"), None),
            P(None, None, ("dp", "seq"), None),
            P(None, None, ("dp", "seq"), None),
            P(None, ("dp", "seq"), None),
            P(None, ("dp", "seq"), None),
            P(None, ("dp", "seq"), None),
            P(None, ("dp", "seq"), None),
            P(None, ("dp", "seq"), None),
            P(None, ("dp", "seq"), None),
            P(None, ("dp", "seq"), None),
            P(None, ("dp", "seq"), None),
            P(None, ("dp", "seq"), None),
            P(None, ("dp", "seq"), None),
            P(None, None, ("dp", "seq")),
            P(None, None, ("dp", "seq")),
            P(None, None, ("dp", "seq")),
            P(None, None, ("dp", "seq")),
            P(None, None, ("dp", "seq")),
            P(None, ("dp", "seq")),
            P(None, ("dp", "seq")),
            P(None, ("dp", "seq")),
            P(None, ("dp", "seq")),
            P(None, ("dp", "seq")),
        ),
        check_vma=False,
    )
```

```python
import functools
import math

import jax
import jax.numpy as jnp
from jax import lax
from jax.experimental import pallas as pl
from jax.experimental.pallas import tpu as pltpu
from jax.sharding import PartitionSpec as P

HEAD_DIM = 64
SEGS = 8


EPSILON = 1e-06
SCALE_SCORE = 0.125
MOMENTUM_RATE = 0.9
DECAY_RATE = 0.0001
AVERAGE_RATE = 0.5
LEARN_BASE = 0.1
VMEM_BYTES = 66900000


def as_sent(shard):
    return jax.tree.map(lambda a: a.astype(jnp.bfloat16) if a.dtype == jnp.float32 else a, shard)


def layer_norm(values, gain_row, shift_row):
    center = values - jnp.mean(values, axis=-1, keepdims=True)
    spread = jnp.mean(center * center, axis=-1, keepdims=True)
    return center * lax.rsqrt(spread + EPSILON) * gain_row + shift_row


def gelu_exact(values):
    return jax.nn.gelu(values, approximate=False)


def project(values, matrix):
    return jnp.einsum("rti,ij->rtj", values, matrix, preferred_element_type=jnp.float32)


def project_back(grad_rows, matrix):
    return jnp.einsum("rtj,ij->rti", grad_rows, matrix, preferred_element_type=jnp.float32)


def outer_sum(values, grad_rows):
    return jnp.einsum("rti,rtj->ij", values, grad_rows, preferred_element_type=jnp.float32)


def column_sum(grad_rows):
    return jnp.sum(grad_rows, axis=(0, 1), dtype=jnp.float32)


def segment_ids(image_lengths, row_len):
    upto = jnp.arange(SEGS)[:, None] <= jnp.arange(SEGS)[None, :]
    bounds = jnp.sum(jnp.where(upto[None], image_lengths[:, :, None], 0), axis=1, dtype=jnp.int32)
    places = jnp.arange(row_len, dtype=jnp.int32)
    return jnp.sum(
        (bounds[:, None, :] <= places[None, :, None]).astype(jnp.int32), axis=-1, dtype=jnp.int32
    )


def visible_block(seg_rows, offset, block_size):
    row_len = seg_rows.shape[0]
    seg_query = seg_rows[offset : offset + block_size]
    matching = seg_query[:, None] == seg_rows[None, :]
    open_key = seg_rows[None, :] != SEGS - 1
    query_place = offset + jnp.arange(block_size, dtype=jnp.int32)
    key_place = jnp.arange(row_len, dtype=jnp.int32)
    return matching & open_key | (query_place[:, None] == key_place[None, :])


def score_block(query_block, key_heads, seg_rows, offset):
    scores = (
        jnp.einsum("qhd,khd->hqk", query_block, key_heads, preferred_element_type=jnp.float32)
        * SCALE_SCORE
    )
    allowed = visible_block(seg_rows, offset, query_block.shape[0])
    return jnp.where(allowed[None], scores, -1e30)


def split_heads(row_values):
    return row_values.reshape(row_values.shape[0], row_values.shape[1] // HEAD_DIM, HEAD_DIM)


def attend_row(row_items):
    query_row, key_row, value_row, seg_rows = row_items
    row_len = query_row.shape[0]
    query_heads = split_heads(query_row)
    key_heads = split_heads(key_row)
    value_heads = split_heads(value_row)
    block_size = min(512, row_len)
    outputs = []
    totals = []
    for offset in range(0, row_len, block_size):
        scores = score_block(query_heads[offset : offset + block_size], key_heads, seg_rows, offset)
        top_score = jnp.max(scores, axis=-1, keepdims=True)
        exponent = jnp.exp(scores - top_score)
        denominator = jnp.sum(exponent, axis=-1, keepdims=True)
        probability = (exponent / denominator).astype(jnp.bfloat16)
        outputs.append(
            jnp.einsum("hqk,khd->qhd", probability, value_heads, preferred_element_type=jnp.float32)
        )
        totals.append(top_score[..., 0] + jnp.log(denominator[..., 0]))
    mixture = jnp.concatenate(outputs, axis=0).reshape(query_row.shape).astype(jnp.bfloat16)
    return (mixture, jnp.concatenate(totals, axis=1))


def attend_back(row_items):
    query_row, key_row, value_row, grad_row, log_total, seg_rows = row_items
    row_len = query_row.shape[0]
    query_heads = split_heads(query_row)
    key_heads = split_heads(key_row)
    value_heads = split_heads(value_row)
    grad_heads = split_heads(grad_row)
    block_size = min(512, row_len)
    key_grad = jnp.zeros(key_heads.shape, jnp.float32)
    value_grad = jnp.zeros(value_heads.shape, jnp.float32)
    query_grads = []
    for offset in range(0, row_len, block_size):
        query_block = query_heads[offset : offset + block_size]
        grad_block = grad_heads[offset : offset + block_size]
        scores = score_block(query_block, key_heads, seg_rows, offset)
        probability = jnp.exp(scores - log_total[:, offset : offset + block_size, None])
        prob_low = probability.astype(jnp.bfloat16)
        prob_grad = jnp.einsum(
            "qhd,khd->hqk", grad_block, value_heads, preferred_element_type=jnp.float32
        )
        inner_sum = jnp.sum(probability * prob_grad, axis=-1, keepdims=True)
        score_grad = (probability * (prob_grad - inner_sum)).astype(jnp.bfloat16)
        query_grads.append(
            jnp.einsum("hqk,khd->qhd", score_grad, key_heads, preferred_element_type=jnp.float32)
            * SCALE_SCORE
        )
        key_grad = (
            key_grad
            + jnp.einsum(
                "hqk,qhd->khd", score_grad, query_block, preferred_element_type=jnp.float32
            )
            * SCALE_SCORE
        )
        value_grad = value_grad + jnp.einsum(
            "hqk,qhd->khd", prob_low, grad_block, preferred_element_type=jnp.float32
        )
    flat_shape = query_row.shape
    query_grad = jnp.concatenate(query_grads, axis=0)
    return (
        query_grad.reshape(flat_shape).astype(jnp.bfloat16),
        key_grad.reshape(flat_shape).astype(jnp.bfloat16),
        value_grad.reshape(flat_shape).astype(jnp.bfloat16),
    )


def layer_forward(hidden_in, params, seg_full):
    attention, upward, downward, vectors, bias_up = params
    vector_values = vectors.astype(jnp.float32)
    normed = layer_norm(hidden_in, vector_values[0], vector_values[1]).astype(jnp.bfloat16)
    queries = (project(normed, attention[0]) + vector_values[2]).astype(jnp.bfloat16)
    key_rows = project(normed, attention[1]).astype(jnp.bfloat16)
    value_rows = (project(normed, attention[2]) + vector_values[3]).astype(jnp.bfloat16)
    query_full, key_full, value_full = (
        lax.all_to_all(queries, "seq", split_axis=2, concat_axis=1, tiled=True),
        lax.all_to_all(key_rows, "seq", split_axis=2, concat_axis=1, tiled=True),
        lax.all_to_all(value_rows, "seq", split_axis=2, concat_axis=1, tiled=True),
    )
    mixture, log_total = lax.map(attend_row, (query_full, key_full, value_full, seg_full))
    mixed_tokens = lax.all_to_all(mixture, "seq", split_axis=1, concat_axis=2, tiled=True)
    residual = hidden_in + (project(mixed_tokens, attention[3]) + vector_values[4])
    normed_two = layer_norm(residual, vector_values[5], vector_values[6]).astype(jnp.bfloat16)
    hidden_pre = project(normed_two, upward) + bias_up.astype(jnp.float32)
    hidden_act = gelu_exact(hidden_pre).astype(jnp.bfloat16)
    result = residual + (project(hidden_act, downward) + vector_values[7])
    saved_values = (
        hidden_in,
        normed,
        query_full,
        key_full,
        value_full,
        log_total,
        mixed_tokens,
        residual,
        normed_two,
        hidden_pre,
        hidden_act,
    )
    return (result, saved_values)


def layer_backward(grad_out, params, saved_values, seg_full):
    attention, upward, downward, vectors, bias_up = params
    vector_values = vectors.astype(jnp.float32)
    (
        hidden_in,
        normed,
        query_full,
        key_full,
        value_full,
        log_total,
        mixed_tokens,
        residual,
        normed_two,
        hidden_pre,
        hidden_act,
    ) = saved_values
    grad_mlp = grad_out.astype(jnp.bfloat16)
    grad_down = outer_sum(hidden_act, grad_mlp)
    grad_act = project_back(grad_mlp, downward)
    grad_pre = jax.vjp(gelu_exact, hidden_pre)[1](grad_act)[0].astype(jnp.bfloat16)
    grad_up = outer_sum(normed_two, grad_pre)
    grad_normed_two = project_back(grad_pre, upward)
    norm_pull_two = jax.vjp(layer_norm, residual, vector_values[5], vector_values[6])[1]
    grad_resid_norm, grad_gain_two, grad_shift_two = norm_pull_two(grad_normed_two)
    grad_residual = grad_out + grad_resid_norm
    grad_proj = grad_residual.astype(jnp.bfloat16)
    grad_outproj = outer_sum(mixed_tokens, grad_proj)
    grad_mixed = project_back(grad_proj, attention[3]).astype(jnp.bfloat16)
    grad_heads = lax.all_to_all(grad_mixed, "seq", split_axis=2, concat_axis=1, tiled=True)
    query_grad, key_grad, value_grad = lax.map(
        attend_back, (query_full, key_full, value_full, grad_heads, log_total, seg_full)
    )
    grad_query, grad_key, grad_value = (
        lax.all_to_all(query_grad, "seq", split_axis=1, concat_axis=2, tiled=True),
        lax.all_to_all(key_grad, "seq", split_axis=1, concat_axis=2, tiled=True),
        lax.all_to_all(value_grad, "seq", split_axis=1, concat_axis=2, tiled=True),
    )
    grad_wq = outer_sum(normed, grad_query)
    grad_wk = outer_sum(normed, grad_key)
    grad_wv = outer_sum(normed, grad_value)
    grad_normed = (
        project_back(grad_query, attention[0])
        + project_back(grad_key, attention[1])
        + project_back(grad_value, attention[2])
    )
    norm_pull_one = jax.vjp(layer_norm, hidden_in, vector_values[0], vector_values[1])[1]
    grad_in_norm, grad_gain_one, grad_shift_one = norm_pull_one(grad_normed)
    grad_in = grad_residual + grad_in_norm
    attention_terms = jnp.stack([grad_wq, grad_wk, grad_wv, grad_outproj])
    vector_terms = jnp.stack(
        [
            grad_gain_one,
            grad_shift_one,
            column_sum(grad_query),
            column_sum(grad_value),
            column_sum(grad_proj),
            grad_gain_two,
            grad_shift_two,
            column_sum(grad_mlp),
        ]
    )
    return (grad_in, (attention_terms, grad_up, grad_down, vector_terms, column_sum(grad_pre)))


def fold_terms(terms, dims, dp_count, seq_count):
    folded = []
    for member in range(len(terms)):
        term = terms[member]
        place = dims[member]
        shape = term.shape
        leading = math.prod(shape[:place])
        owned = shape[place] // (dp_count * seq_count)
        trailing = owned * math.prod(shape[place + 1 :])
        folded.append(term.reshape(leading, dp_count, seq_count, trailing))
    return tuple(folded)


def unfold_terms(received, terms, dims, dp_count, seq_count):
    results = []
    for member in range(len(terms)):
        shape = terms[member].shape
        place = dims[member]
        owned_shape = shape[:place] + (shape[place] // (dp_count * seq_count),) + shape[place + 1 :]
        results.append(jnp.sum(received[member], axis=(1, 2)).reshape(owned_shape))
    return tuple(results)


def optimizer_step(gradient, master, moment, average, step_rate):
    direction = gradient + DECAY_RATE * master
    moment_new = MOMENTUM_RATE * moment + direction
    master_new = master - step_rate * (direction + MOMENTUM_RATE * moment_new)
    average_new = AVERAGE_RATE * average + (1.0 - AVERAGE_RATE) * master_new
    return (gradient, moment_new, average_new, master_new, master_new.astype(jnp.bfloat16))


def plain_step(inputs, cotangent, image_lengths, masters):
    layer_count = masters[0].shape[0]
    dp_count = lax.axis_size("dp")
    seq_count = lax.axis_size("seq")
    seg_full = segment_ids(image_lengths, inputs.shape[1] * seq_count)

    def gather_layer(level_index):
        pieces = tuple((master[level_index].astype(jnp.bfloat16) for master in masters))
        return (
            lax.all_gather(pieces[0], ("dp", "seq"), axis=1, tiled=True),
            lax.all_gather(pieces[1], ("dp", "seq"), axis=0, tiled=True),
            lax.all_gather(pieces[2], ("dp", "seq"), axis=0, tiled=True),
            lax.all_gather(pieces[3], ("dp", "seq"), axis=1, tiled=True),
            lax.all_gather(pieces[4], ("dp", "seq"), axis=0, tiled=True),
        )

    hidden = inputs.astype(jnp.float32)
    kept_params = []
    kept_saved = []
    for level_index in range(layer_count):
        params = gather_layer(level_index)
        hidden, saved_values = layer_forward(hidden, params, seg_full)
        kept_params.append(params)
        kept_saved.append(saved_values)
    output = hidden.astype(jnp.bfloat16)
    stack_dims = (2, 1, 1, 2, 1)
    grad_hidden = cotangent.astype(jnp.float32)
    layer_terms = [None] * layer_count
    for level_index in reversed(range(layer_count)):
        params = kept_params[level_index]
        grad_hidden, terms_here = layer_backward(
            grad_hidden, params, kept_saved[level_index], seg_full
        )
        layer_terms[level_index] = terms_here
    stacked = tuple(
        (jnp.stack([terms_here[member] for terms_here in layer_terms]) for member in range(5))
    )
    folded = fold_terms(stacked, stack_dims, dp_count, seq_count)
    received = jax.tree.map(
        lambda part, own: part.astype(own.dtype),
        lax.all_to_all(
            lax.all_to_all(as_sent(folded), "dp", split_axis=1, concat_axis=1, tiled=True),
            "seq",
            split_axis=2,
            concat_axis=2,
            tiled=True,
        ),
        folded,
    )
    reduced = unfold_terms(received, stacked, stack_dims, dp_count, seq_count)
    return (output, grad_hidden.astype(jnp.bfloat16), *reduced)


MESH = pl.DeviceIdType.MESH
F32 = jnp.float32
BF16 = jnp.bfloat16
KEYS = 896
QBLOCK = 256


def nt(left, right):
    return lax.dot_general(left, right, (((1,), (1,)), ((), ())), preferred_element_type=F32)


def nn(left, right):
    return lax.dot_general(left, right, (((1,), (0,)), ((), ())), preferred_element_type=F32)


def tn(left, right):
    return lax.dot_general(left, right, (((0,), (0,)), ((), ())), preferred_element_type=F32)


def norm_parts(values):
    center = values - jnp.mean(values, axis=-1, keepdims=True)
    scale = lax.rsqrt(jnp.mean(center * center, axis=-1, keepdims=True) + EPSILON)
    return center * scale, scale


def norm_back(values, grad, gain):
    unit, scale = norm_parts(values)
    pulled = grad * gain
    first = jnp.mean(pulled, axis=-1, keepdims=True)
    second = jnp.mean(pulled * unit, axis=-1, keepdims=True)
    result = scale * (pulled - first - unit * second)
    return (
        result,
        jnp.sum(grad * unit, axis=0, keepdims=True),
        jnp.sum(grad, axis=0, keepdims=True),
    )


SEMS = 400


def step_kernel(NZ, x_in, cot_in, lens, aw, uw, dw, lv, hb, *rest):
    (out, gin, gA, gU, gD, gV, gB) = rest[:7]
    (
        w1, w2, w3, w4, stg, rsl, gm, a, b, qh, kk, vv, kT, vT, oh, ofull, goh, gpo, lse,
        x1, xs, xs_out, hact, gpb, segc, segr, facc, gq, gw1, gw2, gw3, gw4, gw5, xl1, xl2, xl3, xl4, xl5,
        zl1, zl2, zl3, zl4, zl5, cl, ps1, ps2, ps3, ps5, pl1, pl2, pl3, pl5, tt, V, vg, snd, rcv,
        credx, credz,
    ) = rest[7:]
    W = {1: w1, 2: w2, 3: w3, 4: w4}
    GW = {1: gw1, 2: gw2, 3: gw3, 4: gw4, 5: gw5}
    XL = {1: xl1, 2: xl2, 3: xl3, 4: xl4, 5: xl5}
    ZL = {1: zl1, 2: zl2, 3: zl3, 4: zl4, 5: zl5}
    PS = {1: ps1, 2: ps2, 3: ps3, 5: ps5}
    PL = {1: pl1, 2: pl2, 3: pl3, 5: pl5}
    S = 4
    T, D = x_in.shape[1], x_in.shape[2]
    R = aw.shape[2]
    CH = R * S
    DP = NZ * 2
    ORDER = (1, NZ - 1) + tuple(range(2, NZ - 1))
    FJ = hb.shape[1]

    d = lax.axis_index("dp")
    s = lax.axis_index("seq")
    z, x = d // 2, d % 2
    y, c = s // 2, s % 2
    xp = 1 - x

    def xor(k):
        return ((y + k // 2) % 2) * 2 + (c + k % 2) % 2

    member = xor

    def dev(dd, ss):
        return {"dp": dd, "seq": ss}

    core_peer, y_peer, x_peer = dev(d, xor(1)), dev(d, xor(2)), dev(z * 2 + xp, s)

    def zdev(dz):
        return dev(((z + dz) % NZ) * 2 + x, s)

    count = [0]

    def sems(n):
        first = count[0]
        count[0] += n
        assert count[0] <= SEMS
        return first

    def rc(src, dst, device, i):
        return pltpu.make_async_remote_copy(
            src_ref=src, dst_ref=dst, send_sem=snd.at[i], recv_sem=rcv.at[i],
            device_id=device, device_id_type=MESH,
        )

    pending = []
    sent_weights = []

    def flush():
        for copy in pending:
            copy.wait_send()
        pending.clear()

    def rows(i):
        return pl.ds(pl.multiple_of(i * T, T), T)

    def chunk(i):
        return pl.ds(pl.multiple_of(i * CH, CH), CH)

    class Gather:
        def __init__(self, view):
            i = sems(3)
            own, across = view.at[rows(s)], view.at[rows(xor(2))]
            self.c1 = rc(own, own, core_peer, i)
            self.c2 = rc(own, own, y_peer, i + 1)
            self.c3 = rc(across, across, core_peer, i + 2)

        def start(self):
            self.c2.start()
            self.c1.start()

        def core(self):
            self.c1.wait_recv()

        def forward(self):
            self.c2.wait_recv()
            self.c3.start()

        def last(self):
            self.c3.wait_recv()

        def done(self):
            pending.extend([self.c1, self.c2, self.c3])

    ag_sems = {}

    def part(g, dd):
        if g == 2:
            return pl.ds(pl.multiple_of(dd * CH + c * (CH // 2), 16), CH // 2)
        return chunk(dd)

    def ag_z(g, l, *steps):
        if (g, l) not in ag_sems:
            ag_sems[g, l] = sems(2 * NZ if g != 2 else 2 * NZ + DP)
        i = ag_sems[g, l]
        own = W[g].at[l, part(g, d)]
        for dz in steps or ORDER:
            rc(own, own, zdev(dz), i + dz).start()
            sent_weights.append((g, i + dz))

    def ag_x(g, l, *steps):
        i = ag_sems[g, l]
        for dz in steps:
            ref = W[g].at[l, part(g, ((z - dz + NZ) % NZ) * 2 + x)]
            if dz:
                rc(ref, ref, zdev(dz), i + dz).wait_recv()
            rc(ref, ref, x_peer, i + NZ + dz).start()
            sent_weights.append((g, i + NZ + dz))

    def ag_done(g, l):
        i = ag_sems[g, l] + NZ
        for dz in range(NZ):
            ref = W[g].at[l, part(g, dz)]
            rc(ref, ref, x_peer, i + dz).wait_recv()

    def ag_core(g, l, start):
        i = ag_sems[g, l] + 2 * NZ
        for k in range(1, DP):
            ref = W[g].at[l, part(g, (d + k) % DP)]
            copy = rc(ref, ref, core_peer, i + k)
            if start:
                copy.start()
                sent_weights.append((g, i + k))
            else:
                copy.wait_recv()

    red_sems = {}

    def x_copy(g, l, dz):
        zi = (z + dz) % NZ
        return rc(
            GW[g].at[part(g, zi * 2 + xp)], XL[g].at[dz], x_peer, red_sems[g, l] + dz
        )

    def z_copy(g, l, dz):
        return rc(
            GW[g].at[part(g, ((z + dz) % NZ) * 2 + x)], ZL[g].at[dz - 1], zdev(dz),
            red_sems[g, l] + NZ + dz,
        )

    def s_copies(g, l):
        i = red_sems[g, l] + 2 * NZ
        return [
            rc(PS[g].at[(s + ds) % S], PL[g].at[s], dev(d, (s + ds) % S), i + ds)
            for ds in range(1, S)
        ]

    def half_copies(l, action):
        i = red_sems[2, l] + 2 * NZ
        for k in range(2):
            to = 2 * c + k
            copy = pltpu.make_async_remote_copy(
                src_ref=PS[2].at[k], dst_ref=PL[2].at[y], send_sem=snd.at[i + k],
                recv_sem=rcv.at[i + y], device_id=dev(d, to), device_id_type=MESH,
            )
            pl.when(to != s)(functools.partial(action, copy))

    def half_arrivals(l):
        i = red_sems[2, l] + 2 * NZ
        for k in range(2):
            copy = rc(PL[2].at[k], PL[2].at[k], core_peer, i + k)
            pl.when(2 * k + s // 2 != s)(lambda copy=copy: copy.wait_recv())

    def core_copies(l):
        i = red_sems[2, l] + 3 * NZ
        other = CH // 2 * (1 - c)
        return [
            rc(
                gw2.at[pl.ds(pl.multiple_of(k * CH + other, 16), CH // 2)], cl.at[k], core_peer, i + k
            )
            for k in range(DP)
        ]

    def red_core(l):
        red_sems[2, l] = sems(3 * NZ + DP)
        for copy in core_copies(l):
            copy.start()

    def red_x(g, l):
        if l == 0 and g != 5:
            pl.semaphore_wait(credx.at[g], 1)
        if g == 2:
            for k, copy in enumerate(core_copies(l)):
                copy.wait_recv()
                gw2[part(2, k)] = (gw2[part(2, k)].astype(F32) + cl[k].astype(F32)).astype(BF16)
        else:
            red_sems[g, l] = sems(2 * NZ + S)
        for dz in ORDER + (0,):
            x_copy(g, l, dz).start()

    def red_z(g, l, *steps):
        for dz in steps or ORDER + (0,):
            x_copy(g, l, dz).wait_recv()
            mine = part(g, ((z + dz) % NZ) * 2 + x)
            GW[g][mine] = (GW[g][mine].astype(F32) + XL[g][dz].astype(F32)).astype(BF16)
            if dz:
                if l == 0 and g != 5 and dz == ORDER[0]:
                    pl.semaphore_wait(credz.at[g], NZ - 1)
                z_copy(g, l, dz).start()
            elif l == 1 and g != 5:
                pl.semaphore_signal(credx.at[g], 1, device_id=x_peer, device_id_type=MESH)

    def red_sum(g, l):
        total = GW[g][part(g, d)].astype(F32)
        for dz in ORDER:
            z_copy(g, l, dz).wait_recv()
            total = total + ZL[g][dz - 1].astype(F32)
        for dz in ORDER:
            z_copy(g, l, dz).wait_send()
        for dz in range(NZ):
            x_copy(g, l, dz).wait_send()
        if g == 2:
            for copy in core_copies(l):
                copy.wait_send()
        if l == 1 and g != 5:
            for dz in range(1, NZ):
                pl.semaphore_signal(credz.at[g], 1, device_id=zdev(dz), device_id_type=MESH)
        if g == 4:
            gD[l] = total
            return
        if g == 5:
            tt[0:CH, :] = total
        wide = total.shape[1]
        pad = jnp.zeros((PS[g].shape[1] - R, wide), F32)
        for k in range(2 if g == 2 else S):
            piece = jnp.concatenate([total[R * k : R * (k + 1)], pad], axis=0)
            PS[g][k] = piece.astype(BF16)
        if g == 2:
            half_copies(l, lambda copy: copy.start())

            @pl.when(s // 2 == c)
            def _():
                PL[2][y] = PS[2][y]
            return
        PL[g][s] = PS[g][s]
        for copy in s_copies(g, l):
            copy.start()

    def red_write(g, l):
        if g == 2:
            half_arrivals(l)
            gA[l, 3] = PL[2][0].astype(F32)[0:R] + PL[2][1].astype(F32)[0:R]
            half_copies(l, lambda copy: copy.wait_send())
            return
        for copy in s_copies(g, l):
            copy.wait_recv()
        parts = [PL[g][k].astype(F32)[0:R] for k in range(S)]
        if g == 1:
            gA[l, 0] = jnp.concatenate([p[:, 0:192] for p in parts], axis=1)
            gA[l, 1] = jnp.concatenate(
                [q for p in parts for q in (p[:, 256:384], p[:, 192:256])], axis=1
            )
            gA[l, 2] = jnp.concatenate([p[:, 384:576] for p in parts], axis=1)
        elif g == 3:
            gU[l] = jnp.concatenate(
                [parts[k][:, FJ * i : FJ * (i + 1)] for i in range(DP) for k in range(S)], axis=1
            )
        else:
            biases = jnp.transpose(tt[...])
            tt[0:R, :] = parts[0] + parts[1] + parts[2] + parts[3]
            vectors = jnp.transpose(tt[...])
            for k in range(2):
                gV[k] = vectors[16 * k : 16 * k + 8, 0:R]
                gB[k : k + 1, :] = biases[16 * k + 8 : 16 * k + 9, 0:CH]
        for copy in s_copies(g, l):
            copy.wait_send()

    parity = [0]

    class Scatter:
        def __init__(self, shifted=False):
            i = sems(3)
            base = parity[0] * 3
            parity[0] = 1 - parity[0]
            self.base = base
            self.shifted = shifted
            self.y_at = 3 * T if shifted else 2 * T
            self.r0 = rc(stg.at[0:T], rsl.at[base], core_peer, i)
            self.r1 = rc(stg.at[T : 2 * T], rsl.at[base + 1], core_peer, i + 1)
            self.r2 = rc(stg.at[self.y_at : self.y_at + T], rsl.at[base + 2], y_peer, i + 2)

        def slot(self, k):
            return rows(1 + k - 2 * (k // 3)) if self.shifted else rows(k)

        def send_core(self, k):
            at = 0 if k == 3 else 1
            stg[T * at : T * (at + 1)] = facc[self.slot(k)].astype(BF16)
            (self.r0 if k == 3 else self.r1).start()

        def send_y(self):
            self.r0.wait_recv()
            stg[self.y_at : self.y_at + T] = (
                facc[self.slot(2)] + rsl[self.base].astype(F32)
            ).astype(BF16)
            self.r2.start()

        def core_sent(self):
            self.r0.wait_send()
            self.r1.wait_send()

        def received(self):
            self.r1.wait_recv()
            self.r2.wait_recv()
            self.r2.wait_send()
            return rsl[self.base + 1].astype(F32) + rsl[self.base + 2].astype(F32)

        def finish(self):
            return facc[self.slot(0)] + self.received()

    barrier = pltpu.get_barrier_semaphore()
    greeted = [core_peer, y_peer, dev(d, xor(3)), x_peer] + [zdev(dz) for dz in range(1, NZ)]
    for device in greeted:
        pl.semaphore_signal(barrier, inc=1, device_id=device, device_id_type=MESH)

    tt[...] = jnp.zeros_like(tt)
    tt[64:72, 0:R] = lv[0]
    tt[72:80, 0:R] = lv[1]
    tt[80:82, 0:CH] = hb[...]
    turned = jnp.transpose(tt[...])
    lane128 = lax.broadcasted_iota(jnp.int32, (1, 128), 1)
    vec_cols = jnp.where(lane128 < 80, turned[0:R, :], 0.0)[:, 64:128]
    bias_cols = jnp.where((lane128 >= 80) & (lane128 < 82), turned[0:CH, :], 0.0)
    for k in range(S):
        o = 192 * k
        two = []
        for l in range(2):
            wq, wk, wv = aw[l, 0], aw[l, 1], aw[l, 2]
            tail = vec_cols if l == 0 else jnp.zeros((R, 64), F32)
            two.append(
                jnp.concatenate(
                    [wq[:, o : o + 192], wk[:, o + 128 : o + 192], wk[:, o : o + 128],
                     wv[:, o : o + 192], tail],
                    axis=1,
                )
            )
        stg[144 * k : 144 * k + 48, 0:640] = jnp.concatenate(two, axis=0).astype(BF16)
    for k in range(S):
        two = [
            jnp.concatenate(
                [uw[l][:, (m * S + k) * FJ : (m * S + k + 1) * FJ] for m in range(DP)], axis=1
            )
            for l in range(2)
        ]
        stg[144 * k + 48 : 144 * k + 96, :] = jnp.concatenate([aw[0, 3], aw[1, 3]], axis=0).astype(BF16)
        stg[144 * k + 96 : 144 * k + 144, :] = jnp.concatenate(two, axis=0).astype(BF16)
    gm[0, rows(s)] = x_in[0]

    pl.semaphore_wait(barrier, len(greeted))

    def piece_rows(k):
        return pl.multiple_of(k * 144, 16)

    def send_pieces(source, target):
        i = sems(S)
        copies = []
        for ds in (2, 3, 1):
            to = xor(ds)
            copies.append(rc(source(to), target, dev(d, to), i + ds))
        for copy in copies:
            copy.start()
        return copies

    pieces1 = send_pieces(
        lambda to: stg.at[pl.ds(piece_rows(to), 48), 0:640], rsl.at[s, 0:48, 0:640]
    )
    pieces2 = send_pieces(
        lambda to: stg.at[pl.ds(pl.multiple_of(piece_rows(to) + 48, 16), 96), :], rsl.at[s, 48:144, :]
    )
    gather_x = Gather(gm.at[0])
    gather_x.start()
    w4[0, chunk(d)] = dw[0].astype(BF16)
    ag_z(4, 0, *ORDER[:2])
    ag_x(4, 0, 0)
    w4[1, chunk(d)] = dw[1].astype(BF16)
    rsl[s, 0:48, 0:640] = stg[pl.ds(piece_rows(s), 48), 0:640]
    rsl[s, 48:144, :] = stg[pl.ds(pl.multiple_of(piece_rows(s) + 48, 16), 96), :]
    vg[...] = jnp.zeros_like(vg)
    for copy in pieces1:
        copy.wait_recv()
    got = [rsl[k, 0:48, 0:640].astype(F32) for k in range(S)]
    for l in range(2):
        full = jnp.concatenate([g[R * l : R * (l + 1)] for g in got], axis=0)
        if l == 0:
            full = jnp.concatenate([full[:, 0:512], full[:, 512:640] + bias_cols], axis=1)
        w1[l, chunk(d)] = full.astype(BF16)
    ag_z(1, 0)
    ag_x(1, 0, 0)
    ag_x(4, 0, ORDER[0])

    bounds = []
    running = jnp.int32(0)
    for k in range(SEGS):
        running = running + lens[0, k]
        bounds.append(running)
    N = S * T

    def segments(shape, dim):
        place = lax.broadcasted_iota(jnp.int32, shape, dim)
        seg = jnp.zeros(shape, jnp.int32)
        for bound in bounds:
            seg = seg + jnp.where(place >= bound, 1, 0)
        return jnp.where(seg == SEGS - 1, SEGS + place, seg)

    segr[...] = segments((8, N), 1)
    segc[...] = segments((N, 128), 0)

    ag_x(1, 0, ORDER[0])
    for copy in pieces2:
        copy.wait_recv()
    for g, at in ((2, 48), (3, 96)):
        got = [rsl[k, at : at + 48, :].astype(F32) for k in range(S)]
        for l in range(2):
            W[g][l, chunk(d)] = jnp.concatenate(
                [piece[R * l : R * (l + 1)] for piece in got], axis=0
            ).astype(BF16)
    for copy in pieces1 + pieces2:
        copy.wait_send()
    ag_x(1, 0, ORDER[1])
    ag_x(1, 0, *ORDER[2:])
    ag_z(2, 0)
    ag_z(3, 0)
    ag_z(4, 0, *ORDER[2:])
    ag_x(2, 0, 0)
    ag_x(4, 0, ORDER[1])
    ag_x(3, 0, 0)
    gather_x.core()
    gather_x.forward()
    gm[1, rows(s)] = cot_in[0]
    ag_done(1, 0)
    V[...] = jnp.transpose(w1[0, :, 512:640].astype(F32))[64:96]
    gather_x.last()
    gather_x.done()

    def vec(l, k):
        return V[8 * l + k : 8 * l + k + 1, :]

    def own_heads(row):
        total = jnp.zeros((1, 192), F32)
        for k in range(S):
            total = total + jnp.where(s == k, row[:, 192 * k : 192 * (k + 1)], 0.0)
        return total

    def at_heads(part):
        total = jnp.zeros((1, D), F32)
        for k in range(S):
            spread = [jnp.zeros((1, 192), F32)] * S
            spread[k] = part
            total = total + jnp.where(s == k, jnp.concatenate(spread, axis=1), 0.0)
        return total

    low = lax.broadcasted_iota(jnp.int32, (T, 128), 1) < 64
    low_rows = lax.broadcasted_iota(jnp.int32, (128, QBLOCK), 0) < 64

    def project_heads(l):
        bias = jnp.concatenate(
            [own_heads(vec(l, 2)), jnp.zeros((1, 192), F32), own_heads(vec(l, 3)), jnp.zeros((1, 64), F32)],
            axis=1,
        )

        @pl.loop(0, S)
        def _(i):
            r = rows(i)
            if l == 0:
                unit, _ = norm_parts(gm[0, r].astype(F32))
                a[0, r] = (unit * vec(0, 0) + vec(0, 1)).astype(BF16)
            full = (nn(a[l, r], w1[l]) + bias).astype(BF16).astype(F32)
            t0, t1, t2, t3, t4 = (full[:, 128 * j : 128 * (j + 1)] for j in range(5))
            t1r = pltpu.roll(t1, 64, 1)
            v4 = jnp.where(low, t4, 0.0)
            qh[l, 0, r] = (jnp.where(low, t0, 0.0) * SCALE_SCORE).astype(BF16)
            qh[l, 1, r] = (jnp.where(low, 0.0, t0) * SCALE_SCORE).astype(BF16)
            qh[l, 2, r] = (jnp.where(low, t1, 0.0) * SCALE_SCORE).astype(BF16)
            kk[l, 0, r] = t2.astype(BF16)
            kk[l, 1, r] = t1r.astype(BF16)
            vv[l, 0, r] = t3.astype(BF16)
            vv[l, 1, r] = v4.astype(BF16)
            kT[l, 0, :, r] = jnp.transpose(t2).astype(BF16)
            kT[l, 1, :, r] = jnp.transpose(t1r).astype(BF16)
            vT[0, :, r] = jnp.transpose(t3).astype(BF16)
            vT[1, :, r] = jnp.transpose(v4).astype(BF16)

    def query_block(qb):
        q = pl.ds(pl.multiple_of(qb * QBLOCK, QBLOCK), QBLOCK)
        k = pl.ds(pl.multiple_of((qb // 2) * (N - KEYS), 128), KEYS)
        return q, k

    def attend(l, points):
        i0 = sems(S)
        order = (2, 3, 1)
        copies = [
            rc(oh.at[l, rows(xor(k))], goh.at[rows(s)], dev(d, xor(k)), i0 + k) for k in order
        ]

        @pl.loop(0, N // QBLOCK)
        def _(i):
            for at, action in points.items():
                pl.when(i == at)(action)
            q, k = query_block(member((2 + i) * (1 - i // 2) + (3 - i) * (i // 2)))
            allowed = jnp.concatenate([segc[k, :]] * 2, axis=1) == segr[0:1, q]
            parts = []
            for h in range(3):
                scores = jnp.where(allowed, nt(kk[l, h // 2, k], qh[l, h, q]), -1e30)
                top = jnp.max(scores, axis=0, keepdims=True)
                grown = jnp.exp(scores - top)
                total = jnp.sum(grown, axis=0, keepdims=True)
                lse[l, h : h + 1, q] = top + jnp.log(total)
                parts.append(nn(vT[h // 2, :, k], grown.astype(BF16)) / total)
            oh[l, q, 0:128] = jnp.transpose(jnp.where(low_rows, parts[0], parts[1])).astype(BF16)
            oh[l, q, 128:256] = jnp.transpose(parts[2]).astype(BF16)
            for at in range(3):
                pl.when(i == at)(copies[at].start)

        goh[rows(s)] = oh[l, rows(s)]
        pending.extend(copies)
        return copies

    def attend_grad(l, copies, points):
        facc[:, 0:512] = jnp.zeros((N, 512), F32)

        @pl.loop(0, N // QBLOCK)
        def _(i):
            for at in range(1, S):
                pl.when(i == at)(copies[at].wait)
            for at, action in points.items():
                pl.when(i == at)(action)
            q, k = query_block(member(i))
            allowed = jnp.concatenate([segc[k, :]] * 2, axis=1) == segr[0:1, q]
            tiles = [goh[q, 0:128], goh[q, 128:256]]
            inner = [
                jnp.transpose(tiles[j].astype(F32) * oh[l, q, 128 * j : 128 * (j + 1)].astype(F32))
                for j in range(2)
            ]
            inner = [
                jnp.sum(inner[0][0:64], axis=0, keepdims=True),
                jnp.sum(inner[0][64:128], axis=0, keepdims=True),
                jnp.sum(inner[1], axis=0, keepdims=True),
            ]
            t0 = tiles[0].astype(F32)
            heads = [
                jnp.where(low, t0, 0.0).astype(BF16),
                jnp.where(low, 0.0, t0).astype(BF16),
                tiles[1],
            ]
            parts = []
            for h in range(3):
                p = h // 2
                queries = qh[l, h, q]
                scores = jnp.where(allowed, nt(kk[l, p, k], queries), -1e30)
                prob = jnp.exp(scores - lse[l, h : h + 1, q])
                grad = nt(vv[l, p, k], heads[h])
                grad = (prob * (grad - inner[h])).astype(BF16)
                facc[k, 256 + 128 * p : 384 + 128 * p] += nn(prob.astype(BF16), heads[h])
                facc[k, 128 * p : 128 * (p + 1)] += nn(grad, queries)
                parts.append(nn(kT[l, p, :, k], grad) * SCALE_SCORE)
            gq[q, 0:128] = jnp.transpose(jnp.where(low_rows, parts[0], parts[1])).astype(BF16)
            gq[q, 128:256] = jnp.transpose(jnp.where(low_rows, parts[2], 0.0)).astype(BF16)

        @pl.loop(0, S)
        def _(i):
            r = rows(i)
            other = pltpu.roll(facc[r, 128:256], 64, 1)
            gq[r, 128:256] = (gq[r, 128:256].astype(F32) + other).astype(BF16)
            gq[r, 256:384] = facc[r, 0:128].astype(BF16)
            gq[r, 384:512] = facc[r, 256:384].astype(BF16)
            gq[r, 512:640] = facc[r, 384:512].astype(BF16)

    def exchange(source, target):
        i = sems(S)
        copies = {}
        for ds in (2, 3, 1):
            to = xor(ds)
            copies[ds] = rc(source(to), target(s), dev(d, to), i + ds)
            copies[ds].start()
        return copies

    def mlp_up(l, gather, points):
        @pl.loop(0, S)
        def _(k):
            pl.when(k == 1)(gather.core)
            pl.when(k == 2)(gather.forward)
            pl.when(k == 3)(gather.last)
            for at, action in points.items():
                pl.when(k == at)(action)
            r = rows(member(k))
            pre = nn(b[l, r], w3[l]) + V[16 + l : 17 + l, :]
            cdf = 0.5 * (1.0 + lax.erf(pre * 0.7071067811865476))
            density = jnp.exp(-0.5 * pre * pre) * 0.3989422804014327
            hact[l, r] = (pre * cdf).astype(BF16)
            gpb[l, r] = (cdf + pre * density).astype(BF16)

        gather.done()

    def scatter_rows(term, shifted=False, across=True):
        scatter = Scatter(shifted)

        @pl.loop(0, S)
        def _(i):
            k = S - 1 - i
            facc[scatter.slot(k)] = term(rows(member(k)))
            pl.when(k == 1)(lambda: scatter.send_core(1))
            pl.when(k == 3)(lambda: scatter.send_core(3))
            if across:
                pl.when(k == 2)(scatter.send_y)

        return scatter

    def mlp_backward(l, gather, points):
        scatter = Scatter()

        @pl.loop(0, S, init_carry=jnp.zeros((1, D), F32))
        def bias_grad(i, carry):
            if gather is None:
                k = S - 1 - i
            else:
                k = i
                pl.when(k == 1)(gather.core)
                pl.when(k == 2)(gather.forward)
                pl.when(k == 3)(gather.last)
            for at, action in points.items():
                pl.when(i == at)(action)
            r = rows(member(k))
            grad_act = nt(gm[l, r], w4[l])
            grad_pre = (grad_act * gpb[l, r].astype(F32)).astype(BF16)
            gpb[l, r] = grad_pre
            facc[rows(k)] = nt(grad_pre, w3[l])
            pl.when(k == 1)(lambda: scatter.send_core(1))
            pl.when(k == 3)(lambda: scatter.send_core(3))
            if gather is None:
                pl.when(k == 2)(scatter.send_y)
            return carry + jnp.sum(grad_pre.astype(F32), axis=0, keepdims=True)

        vg[16 * l + 8 : 16 * l + 9, :] = bias_grad
        if gather is not None:
            gather.done()
            scatter.send_y()
        return scatter

    def weight_grad(g, left, right):
        @pl.loop(0, 2)
        def _(i):
            m = pl.ds(pl.multiple_of(i * 384, 384), 384)
            GW[g][m, :] = tn(left(m), right()).astype(BF16)

    def column(values):
        return jnp.sum(values.astype(F32), axis=0, keepdims=True)

    gather_cot = Gather(gm.at[1])
    last = ORDER[2:]
    for l in range(2):
        project_heads(l)
        if l == 0:
            gather_cot.start()
            ag_x(2, 0, *ORDER[:2])

            def core_stage():
                ag_done(2, 0)
                ag_core(2, 0, True)
                ag_x(3, 0, ORDER[0])

            copies = attend(0, {1: lambda: ag_x(2, 0, *last), 3: core_stage})
        else:

            def core_stage():
                ag_done(2, 1)
                ag_core(2, 1, True)

            copies = attend(1, {1: lambda: ag_x(3, 1, *last), 2: core_stage, 3: lambda: ag_x(4, 1, 0, ORDER[0])})
        for copy in copies:
            copy.wait_recv()
        ag_core(2, l, False)
        ofull[l] = jnp.concatenate(
            [goh[T * k : T * (k + 1)].astype(F32)[:, 0:192] for k in range(S)], axis=1
        ).astype(BF16)
        before = x_in[0].astype(F32) if l == 0 else xs[...]
        middle = before + (nn(ofull[l], w2[l]) + vec(l, 4))
        x1[l] = middle
        unit, _ = norm_parts(middle)
        b[l, rows(s)] = (unit * vec(l, 5) + vec(l, 6)).astype(BF16)
        gather_b = Gather(b.at[l])
        gather_b.start()
        if l == 0:
            gather_cot.core()
            gather_cot.forward()
            ag_z(1, 1)
            ag_z(2, 1)
            ag_x(3, 0, *ORDER[1:])
            gather_cot.last()
            gather_cot.done()
        else:
            ag_x(4, 1, ORDER[1])
        ag_done(3, l)
        if l == 0:
            mlp_up(0, gather_b, {1: lambda: ag_x(4, 0, *last)})
            ag_z(3, 1)
            ag_z(4, 1)
        else:
            mlp_up(1, gather_b, {2: lambda: ag_x(4, 1, *last)})
        ag_done(4, l)
        if l == 1:
            break
        scatter = scatter_rows(lambda r: nn(hact[0, r], w4[0]))
        ag_x(1, 1, 0, *ORDER)
        after = x1[0] + (scatter.finish() + vec(0, 7))
        scatter.core_sent()
        flush()
        xs[...] = after
        unit, _ = norm_parts(after)
        a[1, rows(s)] = (unit * vec(1, 0) + vec(1, 1)).astype(BF16)
        gather_a = Gather(a.at[1])
        gather_a.start()
        ag_x(2, 1, 0, *ORDER)
        ag_x(3, 1, 0, ORDER[0])
        ag_done(1, 1)
        gather_a.core()
        gather_a.forward()
        ag_x(3, 1, ORDER[1])
        gather_a.last()
        gather_a.done()

    gather = None
    for l in (1, 0):
        first = l == 1
        if first:
            scatter = mlp_backward(1, None, {})
        else:
            scatter = mlp_backward(0, gather, {})
        vg[16 * l + 7 : 16 * l + 8, :] = column(gm[l, rows(s)])
        weight_grad(4, lambda m: hact[l, :, m], lambda: gm[l])
        red_x(4, l)
        weight_grad(3, lambda m: b[l, :, m], lambda: gpb[l])
        red_x(3, l)
        if first:
            scatter.core_sent()
            scatter_out = scatter_rows(lambda r: nn(hact[1, r], w4[1]), True, False)
            red_z(4, 1, ORDER[0])
        else:
            red_sum(2, 1)
            red_write(3, 1)
            red_sum(1, 1)
            red_z(4, 0, ORDER[0])
        grad_b = scatter.finish()
        grad_x1, gain, shift = norm_back(x1[l], grad_b, vec(l, 5))
        grad_x1 = grad_x1 + (cot_in[0].astype(F32) if first else xs[...])
        if first:
            xs_out[...] = x1[1] + facc[scatter_out.slot(0)]
        x1[l] = grad_x1
        gpo[...] = grad_x1.astype(BF16)
        flush()
        back = nt(gpo[...], w2[l])
        for k in range(S):
            gq[rows(k), 0:256] = jnp.concatenate(
                [back[:, 192 * k : 192 * (k + 1)], jnp.zeros((T, 64), F32)], axis=1
            ).astype(BF16)
        copies = exchange(lambda to: gq.at[rows(to), 0:256], lambda me: goh.at[rows(me)])
        goh[rows(s)] = gq[rows(s), 0:256]
        vg[16 * l + 5 : 16 * l + 6, :] = gain
        vg[16 * l + 6 : 16 * l + 7, :] = shift
        vg[16 * l + 4 : 16 * l + 5, :] = column(gpo[...])
        if first:
            scatter_out.send_y()
        red_z(4, l, ORDER[1])
        attend_grad(
            l,
            copies,
            {
                1: lambda: red_z(4, l, *last),
                2: lambda: (red_z(4, l, 0), None if first else red_write(1, 1))[1],
                3: lambda: red_z(3, l, ORDER[0]),
            },
        )
        sums = column(gq[...])
        vg[16 * l + 2 : 16 * l + 3, :] = at_heads(sums[:, 0:192])
        vg[16 * l + 3 : 16 * l + 4, :] = at_heads(sums[:, 384:576])
        if first:
            out[0] = (xs_out[...] + (scatter_out.received() + vec(1, 7))).astype(BF16)
            scatter_out.core_sent()
        else:
            scatter.core_sent()
        scatter = scatter_rows(lambda r: nt(gq[r], w1[l]))
        weight_grad(1, lambda m: a[l, :, m], lambda: gq[...])
        red_x(1, l)
        weight_grad(2, lambda m: ofull[l, :, m], lambda: gpo[...])
        red_core(l)
        red_z(3, l, ORDER[1])
        red_x(2, l)
        if not first:
            red_write(2, 1)
        red_z(3, l, *last)
        grad_a = scatter.finish()
        scatter.core_sent()
        before = xs[...] if first else x_in[0].astype(F32)
        grad, gain, shift = norm_back(before, grad_a, vec(l, 0))
        grad = grad + x1[l]
        vg[16 * l : 16 * l + 1, :] = gain
        vg[16 * l + 1 : 16 * l + 2, :] = shift
        flush()
        if first:
            xs[...] = grad
            gm[0, rows(s)] = grad.astype(BF16)
            gather = Gather(gm.at[0])
            gather.start()
        else:
            gin[0] = grad.astype(BF16)
            gw5[...] = jnp.transpose(vg[...]).astype(BF16)
            red_x(5, 0)
        red_z(3, l, 0)
        red_z(1, l, *ORDER[:2])
        red_sum(4, l)
        red_z(1, l, *last)
        red_z(1, l, 0)
        if first:
            red_z(2, 1)
            red_sum(3, 1)

    red_z(5, 0)
    red_z(2, 0)
    red_sum(3, 0)
    red_sum(1, 0)
    red_sum(5, 0)
    red_write(3, 0)
    red_sum(2, 0)
    red_write(1, 0)
    red_write(5, 0)
    red_write(2, 0)
    flush()
    for g, i in sent_weights:
        ref = W[g].at[0, part(g, 0)]
        rc(ref, ref, x_peer, i).wait_send()


def fused_step(inputs, cotangent, image_lengths, attention, upward, downward, vectors, bias_up):
    DP = lax.axis_size("dp")
    S = lax.axis_size("seq")
    NZ = DP // 2
    L = attention.shape[0]
    T, D = inputs.shape[1], inputs.shape[2]
    N = S * T
    R = attention.shape[2]
    CH = R * S
    RP = (R + 15) // 16 * 16
    FJ = bias_up.shape[1]
    vmem = pl.BlockSpec(memory_space=pltpu.VMEM)
    V = pltpu.VMEM
    widths = {1: 640, 2: D, 3: D, 4: D, 5: 128}
    scratch = [
        V((L, D, 640), BF16), V((L, D, D), BF16), V((L, D, D), BF16), V((L, D, D), BF16),
        V((4 * T, D), BF16),
        V((6, T, D), BF16),
        V((L, N, D), BF16), V((L, N, D), BF16), V((L, N, D), BF16),
        V((L, 3, N, 128), BF16), V((L, 2, N, 128), BF16), V((L, 2, N, 128), BF16),
        V((L, 2, 128, N), BF16), V((2, 128, N), BF16),
        V((L, N, 256), BF16), V((L, T, D), BF16),
        V((N, 256), BF16), V((T, D), BF16),
        V((L, 8, N), F32),
        V((L, T, D), F32), V((T, D), F32), V((T, D), F32),
        V((L, N, D), BF16), V((L, N, D), BF16),
        V((N, 128), jnp.int32), V((8, N), jnp.int32),
        V((N, D), F32),
        V((N, 640), BF16),
        *[V((D, widths[g]), BF16) for g in range(1, 6)],
        *[V((NZ, CH // 2 if g == 2 else CH, widths[g]), BF16) for g in range(1, 6)],
        *[V((NZ - 1, CH // 2 if g == 2 else CH, widths[g]), BF16) for g in range(1, 6)],
        V((DP, CH // 2, D), BF16),
        *[V((2 if g == 2 else S, RP, widths[g]), BF16) for g in (1, 2, 3, 5)],
        *[V((2 if g == 2 else S, RP, widths[g]), BF16) for g in (1, 2, 3, 5)],
        V((128, 128), F32), V((32, D), F32), V((128, D), F32),
        pltpu.SemaphoreType.DMA((SEMS,)), pltpu.SemaphoreType.DMA((SEMS,)),
        pltpu.SemaphoreType.REGULAR((8,)), pltpu.SemaphoreType.REGULAR((8,)),
    ]
    return pl.pallas_call(
        functools.partial(step_kernel, NZ),
        out_shape=(
            jax.ShapeDtypeStruct(inputs.shape, BF16),
            jax.ShapeDtypeStruct(inputs.shape, BF16),
            jax.ShapeDtypeStruct(attention.shape, F32),
            jax.ShapeDtypeStruct(upward.shape, F32),
            jax.ShapeDtypeStruct(downward.shape, F32),
            jax.ShapeDtypeStruct(vectors.shape, F32),
            jax.ShapeDtypeStruct(bias_up.shape, F32),
        ),
        in_specs=[vmem, vmem, pl.BlockSpec(memory_space=pltpu.SMEM)] + [vmem] * 5,
        out_specs=(vmem,) * 7,
        scratch_shapes=scratch,
        compiler_params=pltpu.CompilerParams(
            collective_id=0, has_side_effects=True, vmem_limit_bytes=VMEM_BYTES
        ),
    )(inputs, cotangent, image_lengths, attention, upward, downward, vectors, bias_up)


def fits_fused(inputs, attention, upward, bias_up, dp_count, seq_count):
    own_rows, width = attention.shape[2], attention.shape[3]
    return (
        seq_count == 4
        and dp_count == 8
        and inputs.shape == (1, QBLOCK, 768)
        and width == 768
        and own_rows % 8 == 0
        and upward.shape[2] == seq_count * width
        and bias_up.shape[1] % 16 == 0
    )


def update_kernel(rate, *refs):
    for member in range(5):
        gradient, master, moment, average = (refs[5 * k + member][...] for k in range(4))
        results = optimizer_step(gradient, master, moment, average, rate)
        for k in range(5):
            refs[22 + 5 * member + k][...] = results[k]
    for k in range(2):
        refs[47 + k][...] = refs[20 + k][...]


def fused_update(rate, output, input_grad, reduced, masters, moments, averages):
    attention, upward, downward, vectors, bias_up = masters
    halves = [
        pl.BlockSpec((1, 2) + attention.shape[2:], lambda l, i: (l, i, 0, 0)),
        pl.BlockSpec((1, upward.shape[1], upward.shape[2] // 2), lambda l, i: (l, 0, i)),
        pl.BlockSpec((1, downward.shape[1] // 2, downward.shape[2]), lambda l, i: (l, i, 0)),
        pl.BlockSpec((1,) + vectors.shape[1:], lambda l, i: (l, 0, 0)),
        pl.BlockSpec(bias_up.shape, lambda l, i: (0, 0)),
    ]
    tokens = pl.BlockSpec(
        (1, output.shape[1] // 4, output.shape[2]), lambda l, i: (0, 2 * l + i, 0)
    )
    outs, specs = [], []
    for member in range(5):
        for k in range(5):
            outs.append(jax.ShapeDtypeStruct(masters[member].shape, BF16 if k == 4 else F32))
            specs.append(halves[member])
    outs += [jax.ShapeDtypeStruct(output.shape, BF16)] * 2
    results = pl.pallas_call(
        functools.partial(update_kernel, rate),
        grid=(2, 2),
        out_shape=outs,
        in_specs=halves * 4 + [tokens] * 2,
        out_specs=specs + [tokens] * 2,
        compiler_params=pltpu.CompilerParams(vmem_limit_bytes=VMEM_BYTES),
    )(*reduced, *masters, *moments, *averages, output, input_grad)
    return tuple(results[25:]) + tuple(results[:25])


def per_device(
    inputs,
    cotangent,
    image_lengths,
    attention_weight,
    attention_moment,
    attention_average,
    up_weight,
    up_moment,
    up_average,
    down_weight,
    down_moment,
    down_average,
    layer_vectors,
    vector_moment,
    vector_average,
    hidden_bias,
    bias_moment,
    bias_average,
):
    masters = (attention_weight, up_weight, down_weight, layer_vectors, hidden_bias)
    dp_count = lax.axis_size("dp")
    seq_count = lax.axis_size("seq")
    if fits_fused(inputs, attention_weight, up_weight, hidden_bias, dp_count, seq_count):
        output, input_grad, *reduced = fused_step(inputs, cotangent, image_lengths, *masters)
        moments = (attention_moment, up_moment, down_moment, vector_moment, bias_moment)
        averages = (attention_average, up_average, down_average, vector_average, bias_average)
        rate = LEARN_BASE / math.sqrt(inputs.shape[0] * inputs.shape[1] * dp_count * seq_count)
        return fused_update(rate, output, input_grad, reduced, masters, moments, averages)
    else:
        output, input_grad, *reduced = plain_step(inputs, cotangent, image_lengths, masters)
    total_tokens = inputs.shape[0] * inputs.shape[1] * dp_count * seq_count
    step_rate = LEARN_BASE / math.sqrt(total_tokens)
    states = (
        (attention_weight, attention_moment, attention_average),
        (up_weight, up_moment, up_average),
        (down_weight, down_moment, down_average),
        (layer_vectors, vector_moment, vector_average),
        (hidden_bias, bias_moment, bias_average),
    )
    outcome = [output, input_grad]
    for member in range(5):
        master, moment, average = states[member]
        outcome.extend(optimizer_step(reduced[member], master, moment, average, step_rate))
    return tuple(outcome)


def solution(mesh):
    placed = (
        P("dp", "seq", None),
        P("dp", "seq", None),
        P("dp", None),
        P(None, None, ("dp", "seq"), None),
        P(None, None, ("dp", "seq"), None),
        P(None, None, ("dp", "seq"), None),
        P(None, ("dp", "seq"), None),
        P(None, ("dp", "seq"), None),
        P(None, ("dp", "seq"), None),
        P(None, ("dp", "seq"), None),
        P(None, ("dp", "seq"), None),
        P(None, ("dp", "seq"), None),
        P(None, None, ("dp", "seq")),
        P(None, None, ("dp", "seq")),
        P(None, None, ("dp", "seq")),
        P(None, ("dp", "seq")),
        P(None, ("dp", "seq")),
        P(None, ("dp", "seq")),
    )
    return jax.shard_map(
        per_device,
        mesh=mesh,
        in_specs=placed,
        out_specs=(
            P("dp", "seq", None),
            P("dp", "seq", None),
            P(None, None, ("dp", "seq"), None),
            P(None, None, ("dp", "seq"), None),
            P(None, None, ("dp", "seq"), None),
            P(None, None, ("dp", "seq"), None),
            P(None, None, ("dp", "seq"), None),
            P(None, ("dp", "seq"), None),
            P(None, ("dp", "seq"), None),
            P(None, ("dp", "seq"), None),
            P(None, ("dp", "seq"), None),
            P(None, ("dp", "seq"), None),
            P(None, ("dp", "seq"), None),
            P(None, ("dp", "seq"), None),
            P(None, ("dp", "seq"), None),
            P(None, ("dp", "seq"), None),
            P(None, ("dp", "seq"), None),
            P(None, None, ("dp", "seq")),
            P(None, None, ("dp", "seq")),
            P(None, None, ("dp", "seq")),
            P(None, None, ("dp", "seq")),
            P(None, None, ("dp", "seq")),
            P(None, ("dp", "seq")),
            P(None, ("dp", "seq")),
            P(None, ("dp", "seq")),
            P(None, ("dp", "seq")),
            P(None, ("dp", "seq")),
        ),
        check_vma=False,
    )
```

```python
import functools
import math

import jax
import jax.numpy as jnp
from jax import lax
from jax.experimental import pallas as pl
from jax.experimental.pallas import tpu as pltpu
from jax.sharding import PartitionSpec as P

HEAD_DIM = 64
SEGS = 8


EPSILON = 1e-06
SCALE_SCORE = 0.125
MOMENTUM_RATE = 0.9
DECAY_RATE = 0.0001
AVERAGE_RATE = 0.5
LEARN_BASE = 0.1
VMEM_BYTES = 66900000


def as_sent(shard):
    return jax.tree.map(lambda a: a.astype(jnp.bfloat16) if a.dtype == jnp.float32 else a, shard)


def layer_norm(values, gain_row, shift_row):
    center = values - jnp.mean(values, axis=-1, keepdims=True)
    spread = jnp.mean(center * center, axis=-1, keepdims=True)
    return center * lax.rsqrt(spread + EPSILON) * gain_row + shift_row


def gelu_exact(values):
    return jax.nn.gelu(values, approximate=False)


def project(values, matrix):
    return jnp.einsum("rti,ij->rtj", values, matrix, preferred_element_type=jnp.float32)


def project_back(grad_rows, matrix):
    return jnp.einsum("rtj,ij->rti", grad_rows, matrix, preferred_element_type=jnp.float32)


def outer_sum(values, grad_rows):
    return jnp.einsum("rti,rtj->ij", values, grad_rows, preferred_element_type=jnp.float32)


def column_sum(grad_rows):
    return jnp.sum(grad_rows, axis=(0, 1), dtype=jnp.float32)


def segment_ids(image_lengths, row_len):
    upto = jnp.arange(SEGS)[:, None] <= jnp.arange(SEGS)[None, :]
    bounds = jnp.sum(jnp.where(upto[None], image_lengths[:, :, None], 0), axis=1, dtype=jnp.int32)
    places = jnp.arange(row_len, dtype=jnp.int32)
    return jnp.sum(
        (bounds[:, None, :] <= places[None, :, None]).astype(jnp.int32), axis=-1, dtype=jnp.int32
    )


def visible_block(seg_rows, offset, block_size):
    row_len = seg_rows.shape[0]
    seg_query = seg_rows[offset : offset + block_size]
    matching = seg_query[:, None] == seg_rows[None, :]
    open_key = seg_rows[None, :] != SEGS - 1
    query_place = offset + jnp.arange(block_size, dtype=jnp.int32)
    key_place = jnp.arange(row_len, dtype=jnp.int32)
    return matching & open_key | (query_place[:, None] == key_place[None, :])


def score_block(query_block, key_heads, seg_rows, offset):
    scores = (
        jnp.einsum("qhd,khd->hqk", query_block, key_heads, preferred_element_type=jnp.float32)
        * SCALE_SCORE
    )
    allowed = visible_block(seg_rows, offset, query_block.shape[0])
    return jnp.where(allowed[None], scores, -1e30)


def split_heads(row_values):
    return row_values.reshape(row_values.shape[0], row_values.shape[1] // HEAD_DIM, HEAD_DIM)


def attend_row(row_items):
    query_row, key_row, value_row, seg_rows = row_items
    row_len = query_row.shape[0]
    query_heads = split_heads(query_row)
    key_heads = split_heads(key_row)
    value_heads = split_heads(value_row)
    block_size = min(512, row_len)
    outputs = []
    totals = []
    for offset in range(0, row_len, block_size):
        scores = score_block(query_heads[offset : offset + block_size], key_heads, seg_rows, offset)
        top_score = jnp.max(scores, axis=-1, keepdims=True)
        exponent = jnp.exp(scores - top_score)
        denominator = jnp.sum(exponent, axis=-1, keepdims=True)
        probability = (exponent / denominator).astype(jnp.bfloat16)
        outputs.append(
            jnp.einsum("hqk,khd->qhd", probability, value_heads, preferred_element_type=jnp.float32)
        )
        totals.append(top_score[..., 0] + jnp.log(denominator[..., 0]))
    mixture = jnp.concatenate(outputs, axis=0).reshape(query_row.shape).astype(jnp.bfloat16)
    return (mixture, jnp.concatenate(totals, axis=1))


def attend_back(row_items):
    query_row, key_row, value_row, grad_row, log_total, seg_rows = row_items
    row_len = query_row.shape[0]
    query_heads = split_heads(query_row)
    key_heads = split_heads(key_row)
    value_heads = split_heads(value_row)
    grad_heads = split_heads(grad_row)
    block_size = min(512, row_len)
    key_grad = jnp.zeros(key_heads.shape, jnp.float32)
    value_grad = jnp.zeros(value_heads.shape, jnp.float32)
    query_grads = []
    for offset in range(0, row_len, block_size):
        query_block = query_heads[offset : offset + block_size]
        grad_block = grad_heads[offset : offset + block_size]
        scores = score_block(query_block, key_heads, seg_rows, offset)
        probability = jnp.exp(scores - log_total[:, offset : offset + block_size, None])
        prob_low = probability.astype(jnp.bfloat16)
        prob_grad = jnp.einsum(
            "qhd,khd->hqk", grad_block, value_heads, preferred_element_type=jnp.float32
        )
        inner_sum = jnp.sum(probability * prob_grad, axis=-1, keepdims=True)
        score_grad = (probability * (prob_grad - inner_sum)).astype(jnp.bfloat16)
        query_grads.append(
            jnp.einsum("hqk,khd->qhd", score_grad, key_heads, preferred_element_type=jnp.float32)
            * SCALE_SCORE
        )
        key_grad = (
            key_grad
            + jnp.einsum(
                "hqk,qhd->khd", score_grad, query_block, preferred_element_type=jnp.float32
            )
            * SCALE_SCORE
        )
        value_grad = value_grad + jnp.einsum(
            "hqk,qhd->khd", prob_low, grad_block, preferred_element_type=jnp.float32
        )
    flat_shape = query_row.shape
    query_grad = jnp.concatenate(query_grads, axis=0)
    return (
        query_grad.reshape(flat_shape).astype(jnp.bfloat16),
        key_grad.reshape(flat_shape).astype(jnp.bfloat16),
        value_grad.reshape(flat_shape).astype(jnp.bfloat16),
    )


def layer_forward(hidden_in, params, seg_full):
    attention, upward, downward, vectors, bias_up = params
    vector_values = vectors.astype(jnp.float32)
    normed = layer_norm(hidden_in, vector_values[0], vector_values[1]).astype(jnp.bfloat16)
    queries = (project(normed, attention[0]) + vector_values[2]).astype(jnp.bfloat16)
    key_rows = project(normed, attention[1]).astype(jnp.bfloat16)
    value_rows = (project(normed, attention[2]) + vector_values[3]).astype(jnp.bfloat16)
    query_full, key_full, value_full = (
        lax.all_to_all(queries, "seq", split_axis=2, concat_axis=1, tiled=True),
        lax.all_to_all(key_rows, "seq", split_axis=2, concat_axis=1, tiled=True),
        lax.all_to_all(value_rows, "seq", split_axis=2, concat_axis=1, tiled=True),
    )
    mixture, log_total = lax.map(attend_row, (query_full, key_full, value_full, seg_full))
    mixed_tokens = lax.all_to_all(mixture, "seq", split_axis=1, concat_axis=2, tiled=True)
    residual = hidden_in + (project(mixed_tokens, attention[3]) + vector_values[4])
    normed_two = layer_norm(residual, vector_values[5], vector_values[6]).astype(jnp.bfloat16)
    hidden_pre = project(normed_two, upward) + bias_up.astype(jnp.float32)
    hidden_act = gelu_exact(hidden_pre).astype(jnp.bfloat16)
    result = residual + (project(hidden_act, downward) + vector_values[7])
    saved_values = (
        hidden_in,
        normed,
        query_full,
        key_full,
        value_full,
        log_total,
        mixed_tokens,
        residual,
        normed_two,
        hidden_pre,
        hidden_act,
    )
    return (result, saved_values)


def layer_backward(grad_out, params, saved_values, seg_full):
    attention, upward, downward, vectors, bias_up = params
    vector_values = vectors.astype(jnp.float32)
    (
        hidden_in,
        normed,
        query_full,
        key_full,
        value_full,
        log_total,
        mixed_tokens,
        residual,
        normed_two,
        hidden_pre,
        hidden_act,
    ) = saved_values
    grad_mlp = grad_out.astype(jnp.bfloat16)
    grad_down = outer_sum(hidden_act, grad_mlp)
    grad_act = project_back(grad_mlp, downward)
    grad_pre = jax.vjp(gelu_exact, hidden_pre)[1](grad_act)[0].astype(jnp.bfloat16)
    grad_up = outer_sum(normed_two, grad_pre)
    grad_normed_two = project_back(grad_pre, upward)
    norm_pull_two = jax.vjp(layer_norm, residual, vector_values[5], vector_values[6])[1]
    grad_resid_norm, grad_gain_two, grad_shift_two = norm_pull_two(grad_normed_two)
    grad_residual = grad_out + grad_resid_norm
    grad_proj = grad_residual.astype(jnp.bfloat16)
    grad_outproj = outer_sum(mixed_tokens, grad_proj)
    grad_mixed = project_back(grad_proj, attention[3]).astype(jnp.bfloat16)
    grad_heads = lax.all_to_all(grad_mixed, "seq", split_axis=2, concat_axis=1, tiled=True)
    query_grad, key_grad, value_grad = lax.map(
        attend_back, (query_full, key_full, value_full, grad_heads, log_total, seg_full)
    )
    grad_query, grad_key, grad_value = (
        lax.all_to_all(query_grad, "seq", split_axis=1, concat_axis=2, tiled=True),
        lax.all_to_all(key_grad, "seq", split_axis=1, concat_axis=2, tiled=True),
        lax.all_to_all(value_grad, "seq", split_axis=1, concat_axis=2, tiled=True),
    )
    grad_wq = outer_sum(normed, grad_query)
    grad_wk = outer_sum(normed, grad_key)
    grad_wv = outer_sum(normed, grad_value)
    grad_normed = (
        project_back(grad_query, attention[0])
        + project_back(grad_key, attention[1])
        + project_back(grad_value, attention[2])
    )
    norm_pull_one = jax.vjp(layer_norm, hidden_in, vector_values[0], vector_values[1])[1]
    grad_in_norm, grad_gain_one, grad_shift_one = norm_pull_one(grad_normed)
    grad_in = grad_residual + grad_in_norm
    attention_terms = jnp.stack([grad_wq, grad_wk, grad_wv, grad_outproj])
    vector_terms = jnp.stack(
        [
            grad_gain_one,
            grad_shift_one,
            column_sum(grad_query),
            column_sum(grad_value),
            column_sum(grad_proj),
            grad_gain_two,
            grad_shift_two,
            column_sum(grad_mlp),
        ]
    )
    return (grad_in, (attention_terms, grad_up, grad_down, vector_terms, column_sum(grad_pre)))


def fold_terms(terms, dims, dp_count, seq_count):
    folded = []
    for member in range(len(terms)):
        term = terms[member]
        place = dims[member]
        shape = term.shape
        leading = math.prod(shape[:place])
        owned = shape[place] // (dp_count * seq_count)
        trailing = owned * math.prod(shape[place + 1 :])
        folded.append(term.reshape(leading, dp_count, seq_count, trailing))
    return tuple(folded)


def unfold_terms(received, terms, dims, dp_count, seq_count):
    results = []
    for member in range(len(terms)):
        shape = terms[member].shape
        place = dims[member]
        owned_shape = shape[:place] + (shape[place] // (dp_count * seq_count),) + shape[place + 1 :]
        results.append(jnp.sum(received[member], axis=(1, 2)).reshape(owned_shape))
    return tuple(results)


def optimizer_step(gradient, master, moment, average, step_rate):
    direction = gradient + DECAY_RATE * master
    moment_new = MOMENTUM_RATE * moment + direction
    master_new = master - step_rate * (direction + MOMENTUM_RATE * moment_new)
    average_new = AVERAGE_RATE * average + (1.0 - AVERAGE_RATE) * master_new
    return (gradient, moment_new, average_new, master_new, master_new.astype(jnp.bfloat16))


def plain_step(inputs, cotangent, image_lengths, masters):
    layer_count = masters[0].shape[0]
    dp_count = lax.axis_size("dp")
    seq_count = lax.axis_size("seq")
    seg_full = segment_ids(image_lengths, inputs.shape[1] * seq_count)

    def gather_layer(level_index):
        pieces = tuple((master[level_index].astype(jnp.bfloat16) for master in masters))
        return (
            lax.all_gather(pieces[0], ("dp", "seq"), axis=1, tiled=True),
            lax.all_gather(pieces[1], ("dp", "seq"), axis=0, tiled=True),
            lax.all_gather(pieces[2], ("dp", "seq"), axis=0, tiled=True),
            lax.all_gather(pieces[3], ("dp", "seq"), axis=1, tiled=True),
            lax.all_gather(pieces[4], ("dp", "seq"), axis=0, tiled=True),
        )

    hidden = inputs.astype(jnp.float32)
    kept_params = []
    kept_saved = []
    for level_index in range(layer_count):
        params = gather_layer(level_index)
        hidden, saved_values = layer_forward(hidden, params, seg_full)
        kept_params.append(params)
        kept_saved.append(saved_values)
    output = hidden.astype(jnp.bfloat16)
    stack_dims = (2, 1, 1, 2, 1)
    grad_hidden = cotangent.astype(jnp.float32)
    layer_terms = [None] * layer_count
    for level_index in reversed(range(layer_count)):
        params = kept_params[level_index]
        grad_hidden, terms_here = layer_backward(
            grad_hidden, params, kept_saved[level_index], seg_full
        )
        layer_terms[level_index] = terms_here
    stacked = tuple(
        (jnp.stack([terms_here[member] for terms_here in layer_terms]) for member in range(5))
    )
    folded = fold_terms(stacked, stack_dims, dp_count, seq_count)
    received = jax.tree.map(
        lambda part, own: part.astype(own.dtype),
        lax.all_to_all(
            lax.all_to_all(as_sent(folded), "dp", split_axis=1, concat_axis=1, tiled=True),
            "seq",
            split_axis=2,
            concat_axis=2,
            tiled=True,
        ),
        folded,
    )
    reduced = unfold_terms(received, stacked, stack_dims, dp_count, seq_count)
    return (output, grad_hidden.astype(jnp.bfloat16), *reduced)


MESH = pl.DeviceIdType.MESH
F32 = jnp.float32
BF16 = jnp.bfloat16
KEYS = 896
QBLOCK = 256


def nt(left, right):
    return lax.dot_general(left, right, (((1,), (1,)), ((), ())), preferred_element_type=F32)


def nn(left, right):
    return lax.dot_general(left, right, (((1,), (0,)), ((), ())), preferred_element_type=F32)


def tn(left, right):
    return lax.dot_general(left, right, (((0,), (0,)), ((), ())), preferred_element_type=F32)


def norm_parts(values):
    center = values - jnp.mean(values, axis=-1, keepdims=True)
    scale = lax.rsqrt(jnp.mean(center * center, axis=-1, keepdims=True) + EPSILON)
    return center * scale, scale


def norm_back(values, grad, gain):
    unit, scale = norm_parts(values)
    pulled = grad * gain
    first = jnp.mean(pulled, axis=-1, keepdims=True)
    second = jnp.mean(pulled * unit, axis=-1, keepdims=True)
    result = scale * (pulled - first - unit * second)
    return (
        result,
        jnp.sum(grad * unit, axis=0, keepdims=True),
        jnp.sum(grad, axis=0, keepdims=True),
    )


SEMS = 170


def step_kernel(NZ, x_hbm, cot_hbm, lens, aw_hbm, uw_hbm, dw_hbm, lv, hb, *rest):
    (out, gin, gA_hbm, gU_hbm, gD_hbm, gV, gB) = rest[:7]
    (
        w1, w2, w3, w4, stg, rsl, gm, a, b, qh, kk, vv, kT, vT, oh, ofull, goh, gpo, lse,
        x1, xs, xs_out, hact, gpb, segc, segr, facc, gq, gw1, gw2, gw3, gw4, gw5, xl1, xl2, xl3, xl4, xl5,
        zl1, zl2, zl3, zl4, zl5, cl, ps1, ps2, ps3, ps5, pl1, pl2, pl3, pl5, tt, V, vg, snd, rcv,
        credx, credz, aw, uw, dw, x_in, gA, gU, gD, near,
    ) = rest[7:]
    W = {1: w1, 2: w2, 3: w3, 4: w4}
    GW = {1: gw1, 2: gw2, 3: gw3, 4: gw4, 5: gw5}
    XL = {1: xl1, 2: xl2, 3: xl3, 4: xl4, 5: xl5}
    ZL = {1: zl1, 2: zl2, 3: zl3, 4: zl4, 5: zl5}
    PS = {1: ps1, 2: ps2, 3: ps3, 5: ps5}
    PL = {1: pl1, 2: pl2, 3: pl3, 5: pl5}
    S = 4
    T, D = x_in.shape
    R = aw.shape[2]
    CH = R * S
    DP = NZ * 2
    ORDER = (1, NZ - 1) + tuple(range(2, NZ - 1))
    FJ = hb.shape[1]

    d = lax.axis_index("dp")
    s = lax.axis_index("seq")
    z, x = d // 2, d % 2
    y, c = s // 2, s % 2
    xp = 1 - x

    def xor(k):
        return ((y + k // 2) % 2) * 2 + (c + k % 2) % 2

    member = xor

    def dev(dd, ss):
        return {"dp": dd, "seq": ss}

    core_peer, y_peer, x_peer = dev(d, xor(1)), dev(d, xor(2)), dev(z * 2 + xp, s)

    def zdev(dz):
        return dev(((z + dz) % NZ) * 2 + x, s)

    count = [0]

    def sems(n):
        first = count[0]
        count[0] += n
        assert count[0] <= SEMS
        return first

    def rc(src, dst, device, i):
        return pltpu.make_async_remote_copy(
            src_ref=src, dst_ref=dst, send_sem=snd.at[i], recv_sem=rcv.at[i],
            device_id=device, device_id_type=MESH,
        )

    pending = []
    sent_weights = []

    def flush():
        for copy in pending:
            copy.wait_send()
        pending.clear()

    def rows(i):
        return pl.ds(pl.multiple_of(i * T, T), T)

    H = T // 2

    def half(i, h):
        return pl.ds(pl.multiple_of(i * T + h * H, H), H)

    def chunk(i):
        return pl.ds(pl.multiple_of(i * CH, CH), CH)

    local = []

    def move(src, dst):
        copy = pltpu.make_async_copy(src, dst, near.at[len(local)])
        local.append(None)
        copy.start()
        return copy

    def write_out(ends):
        i = len(local)
        local.append(ends)
        pltpu.make_async_copy(*ends(), near.at[i]).start()

    class Gather:
        def __init__(self, view, i):
            self.c1, self.c2, self.c3 = [], [], []
            for h in range(2):
                own, across = view.at[half(s, h)], view.at[half(xor(2), h)]
                self.c1.append(rc(own, own, core_peer, i + h))
                self.c2.append(rc(own, own, y_peer, i + 2 + h))
                self.c3.append(rc(across, across, core_peer, i + 4 + h))

        def start(self, h):
            self.c2[h].start()
            self.c1[h].start()

        def core(self):
            self.c1[0].wait_recv()
            self.c1[1].wait_recv()

        def forward(self, h):
            self.c2[h].wait_recv()
            self.c3[h].start()

        def last(self, h):
            self.c3[h].wait_recv()

        def done(self):
            pending.extend(self.c1 + self.c2 + self.c3)

    ag_sems = {
        (g, l): sems(2 * NZ - 1 if g != 2 else 2 * NZ + DP - 2) for g in W for l in range(2)
    }

    def part(g, dd):
        if g == 2:
            return pl.ds(pl.multiple_of(dd * CH + c * (CH // 2), 16), CH // 2)
        return chunk(dd)

    def ag_z(g, l, *steps):
        i = ag_sems[g, l]
        own = W[g].at[l, part(g, d)]
        for dz in steps or ORDER:
            rc(own, own, zdev(dz), i + dz - 1).start()
            sent_weights.append((g, i + dz - 1))

    def ag_x(g, l, *steps):
        i = ag_sems[g, l]
        for dz in steps:
            ref = W[g].at[l, part(g, ((z - dz + NZ) % NZ) * 2 + x)]
            if dz:
                rc(ref, ref, zdev(dz), i + dz - 1).wait_recv()
            rc(ref, ref, x_peer, i + NZ - 1 + dz).start()
            sent_weights.append((g, i + NZ - 1 + dz))

    def ag_done(g, l):
        i = ag_sems[g, l] + NZ - 1
        for dz in range(NZ):
            ref = W[g].at[l, part(g, dz)]
            rc(ref, ref, x_peer, i + dz).wait_recv()

    def ag_core(g, l, start):
        i = ag_sems[g, l] + 2 * NZ - 2
        for k in range(1, DP):
            ref = W[g].at[l, part(g, (d + k) % DP)]
            copy = rc(ref, ref, core_peer, i + k)
            if start:
                copy.start()
                sent_weights.append((g, i + k))
            else:
                copy.wait_recv()

    red_sems = {g: sems(2 * NZ + 1 + DP if g == 2 else 2 * NZ + S - 2) for g in range(1, 6)}

    def x_copy(g, l, dz):
        zi = (z + dz) % NZ
        return rc(
            GW[g].at[part(g, zi * 2 + xp)], XL[g].at[dz], x_peer, red_sems[g] + dz
        )

    def z_copy(g, l, dz):
        return rc(
            GW[g].at[part(g, ((z + dz) % NZ) * 2 + x)], ZL[g].at[dz - 1], zdev(dz),
            red_sems[g] + NZ - 1 + dz,
        )

    def s_copies(g, l):
        i = red_sems[g] + 2 * NZ - 2
        return [
            rc(PS[g].at[(s + ds) % S], PL[g].at[s], dev(d, (s + ds) % S), i + ds)
            for ds in range(1, S)
        ]

    def half_copies(l, action):
        i = red_sems[2] + 2 * NZ - 1
        for k in range(2):
            to = 2 * c + k
            copy = pltpu.make_async_remote_copy(
                src_ref=PS[2].at[k], dst_ref=PL[2].at[y], send_sem=snd.at[i + k],
                recv_sem=rcv.at[i + y], device_id=dev(d, to), device_id_type=MESH,
            )
            pl.when(to != s)(functools.partial(action, copy))

    def half_arrivals(l):
        i = red_sems[2] + 2 * NZ - 1
        for k in range(2):
            copy = rc(PL[2].at[k], PL[2].at[k], core_peer, i + k)
            pl.when(2 * k + s // 2 != s)(lambda copy=copy: copy.wait_recv())

    def core_copies(l):
        i = red_sems[2] + 2 * NZ + 1
        other = CH // 2 * (1 - c)
        return [
            rc(
                gw2.at[pl.ds(pl.multiple_of(k * CH + other, 16), CH // 2)], cl.at[k], core_peer, i + k
            )
            for k in range(DP)
        ]

    def red_core(l):
        for copy in core_copies(l):
            copy.start()

    def red_x(g, l):
        if l == 0 and g != 5:
            pl.semaphore_wait(credx.at[g], 1)
        if g == 2:
            for k, copy in enumerate(core_copies(l)):
                copy.wait_recv()
                gw2[part(2, k)] = (gw2[part(2, k)].astype(F32) + cl[k].astype(F32)).astype(BF16)
        for dz in ORDER + (0,):
            x_copy(g, l, dz).start()

    def red_z(g, l, *steps):
        for dz in steps or ORDER + (0,):
            x_copy(g, l, dz).wait_recv()
            mine = part(g, ((z + dz) % NZ) * 2 + x)
            GW[g][mine] = (GW[g][mine].astype(F32) + XL[g][dz].astype(F32)).astype(BF16)
            if dz:
                if l == 0 and g != 5 and dz == ORDER[0]:
                    pl.semaphore_wait(credz.at[g], NZ - 1)
                z_copy(g, l, dz).start()
            elif l == 1 and g != 5:
                pl.semaphore_signal(credx.at[g], 1, device_id=x_peer, device_id_type=MESH)

    def red_sum(g, l):
        total = GW[g][part(g, d)].astype(F32)
        for dz in ORDER:
            z_copy(g, l, dz).wait_recv()
            total = total + ZL[g][dz - 1].astype(F32)
        for dz in ORDER:
            z_copy(g, l, dz).wait_send()
        for dz in range(NZ):
            x_copy(g, l, dz).wait_send()
        if g == 2:
            for copy in core_copies(l):
                copy.wait_send()
        if l == 1 and g != 5:
            for dz in range(1, NZ):
                pl.semaphore_signal(credz.at[g], 1, device_id=zdev(dz), device_id_type=MESH)
        if g == 4:
            gD[l] = total
            write_out(lambda: (gD.at[l], gD_hbm.at[l]))
            return
        if g == 5:
            tt[0:CH, :] = total
        wide = total.shape[1]
        pad = jnp.zeros((PS[g].shape[1] - R, wide), F32)
        for k in range(2 if g == 2 else S):
            piece = jnp.concatenate([total[R * k : R * (k + 1)], pad], axis=0)
            PS[g][k] = piece.astype(BF16)
        if g == 2:
            half_copies(l, lambda copy: copy.start())

            @pl.when(s // 2 == c)
            def _():
                PL[2][y] = PS[2][y]
            return
        PL[g][s] = PS[g][s]
        for copy in s_copies(g, l):
            copy.start()

    def red_write(g, l):
        if g == 2:
            half_arrivals(l)
            gA[l, 3] = PL[2][0].astype(F32)[0:R] + PL[2][1].astype(F32)[0:R]
            write_out(lambda: (gA.at[l, 3], gA_hbm.at[l, 3]))
            half_copies(l, lambda copy: copy.wait_send())
            return
        for copy in s_copies(g, l):
            copy.wait_recv()
        parts = [PL[g][k].astype(F32)[0:R] for k in range(S)]
        if g == 1:
            gA[l, 0] = jnp.concatenate([p[:, 0:192] for p in parts], axis=1)
            gA[l, 1] = jnp.concatenate(
                [q for p in parts for q in (p[:, 256:384], p[:, 192:256])], axis=1
            )
            gA[l, 2] = jnp.concatenate([p[:, 384:576] for p in parts], axis=1)
            write_out(lambda: (gA.at[l, 0:3], gA_hbm.at[l, 0:3]))
        elif g == 3:
            gU[l] = jnp.concatenate(
                [parts[k][:, FJ * i : FJ * (i + 1)] for i in range(DP) for k in range(S)], axis=1
            )
            write_out(lambda: (gU.at[l], gU_hbm.at[l]))
        else:
            biases = jnp.transpose(tt[...])
            tt[0:R, :] = parts[0] + parts[1] + parts[2] + parts[3]
            vectors = jnp.transpose(tt[...])
            for k in range(2):
                gV[k] = vectors[16 * k : 16 * k + 8, 0:R]
                gB[k : k + 1, :] = biases[16 * k + 8 : 16 * k + 9, 0:CH]
        for copy in s_copies(g, l):
            copy.wait_send()

    parity = [0]
    scatter_sems = (sems(5), sems(5))
    gather_sems = (sems(6), sems(6), sems(6))
    forward_sems, backward_sems = sems(3), sems(6)

    class Scatter:
        def __init__(self, shifted=False):
            base = parity[0] * 3
            i = scatter_sems[parity[0]]
            parity[0] = 1 - parity[0]
            self.base = base
            self.shifted = shifted
            self.y_at = 3 * T if shifted else 2 * T
            self.r1 = rc(stg.at[T : 2 * T], rsl.at[base + 1], core_peer, i)
            self.r0, self.r2 = [], []
            for h in range(2):
                part = pl.ds(h * H, H)
                self.r0.append(rc(stg.at[part], rsl.at[base, part], core_peer, i + 1 + h))
                at = pl.ds(self.y_at + h * H, H)
                self.r2.append(rc(stg.at[at], rsl.at[base + 2, part], y_peer, i + 3 + h))

        def slot(self, k, h=None):
            at = 1 + k - 2 * (k // 3) if self.shifted else k
            return rows(at) if h is None else half(at, h)

        def send_core(self, h=None):
            if h is None:
                stg[T : 2 * T] = facc[self.slot(1)].astype(BF16)
                self.r1.start()
            else:
                stg[h * H : (h + 1) * H] = facc[self.slot(3, h)].astype(BF16)
                self.r0[h].start()

        def send_y(self, h):
            self.r0[h].wait_recv()
            stg[self.y_at + h * H : self.y_at + (h + 1) * H] = (
                facc[self.slot(2, h)] + rsl[self.base, h * H : (h + 1) * H].astype(F32)
            ).astype(BF16)
            self.r2[h].start()

        def core_sent(self):
            for copy in (self.r1, *self.r0):
                copy.wait_send()

        def received(self, h):
            if h == 0:
                self.r1.wait_recv()
            self.r2[h].wait_recv()
            self.r2[h].wait_send()
            own = slice(h * H, (h + 1) * H)
            return rsl[self.base + 1, own].astype(F32) + rsl[self.base + 2, own].astype(F32)

        def finish(self, h):
            return facc[self.slot(0, h)] + self.received(h)

    loads = [
        move(src, dst)
        for src, dst in (
            (aw_hbm, aw), (uw_hbm, uw), (x_hbm.at[0], gm.at[0, rows(s)]), (dw_hbm, dw),
            (x_hbm.at[0], x_in), (cot_hbm.at[0], gm.at[1, rows(s)]),
        )
    ]
    barrier = pltpu.get_barrier_semaphore()
    greeted = [core_peer, y_peer, dev(d, xor(3)), x_peer] + [zdev(dz) for dz in range(1, NZ)]
    for device in greeted:
        pl.semaphore_signal(barrier, inc=1, device_id=device, device_id_type=MESH)

    tt[...] = jnp.zeros_like(tt)
    tt[64:72, 0:R] = lv[0]
    tt[72:80, 0:R] = lv[1]
    tt[80:82, 0:CH] = hb[...]
    turned = jnp.transpose(tt[...])
    lane128 = lax.broadcasted_iota(jnp.int32, (1, 128), 1)
    vec_cols = jnp.where(lane128 < 80, turned[0:R, :], 0.0)[:, 64:128]
    bias_cols = jnp.where((lane128 >= 80) & (lane128 < 82), turned[0:CH, :], 0.0)
    loads[0].wait()
    for k in range(S):
        o = 192 * k
        two = []
        for l in range(2):
            wq, wk, wv = aw[l, 0], aw[l, 1], aw[l, 2]
            tail = vec_cols if l == 0 else jnp.zeros((R, 64), F32)
            two.append(
                jnp.concatenate(
                    [wq[:, o : o + 192], wk[:, o + 128 : o + 192], wk[:, o : o + 128],
                     wv[:, o : o + 192], tail],
                    axis=1,
                )
            )
        stg[144 * k : 144 * k + 48, 0:640] = jnp.concatenate(two, axis=0).astype(BF16)
    loads[1].wait()
    for k in range(S):
        two = [
            jnp.concatenate(
                [uw[l][:, (m * S + k) * FJ : (m * S + k + 1) * FJ] for m in range(DP)], axis=1
            )
            for l in range(2)
        ]
        stg[144 * k + 48 : 144 * k + 96, :] = jnp.concatenate([aw[0, 3], aw[1, 3]], axis=0).astype(BF16)
        stg[144 * k + 96 : 144 * k + 144, :] = jnp.concatenate(two, axis=0).astype(BF16)
    for load in loads[2:]:
        load.wait()
    pl.semaphore_wait(barrier, len(greeted))

    def piece_rows(k):
        return pl.multiple_of(k * 144, 16)

    def send_pieces(source, target):
        i = sems(S - 1)
        copies = []
        for ds in (2, 3, 1):
            to = xor(ds)
            copies.append(rc(source(to), target, dev(d, to), i + ds - 1))
        for copy in copies:
            copy.start()
        return copies

    pieces1 = send_pieces(
        lambda to: stg.at[pl.ds(piece_rows(to), 48), 0:640], rsl.at[s, 0:48, 0:640]
    )
    pieces2 = send_pieces(
        lambda to: stg.at[pl.ds(pl.multiple_of(piece_rows(to) + 48, 16), 96), :], rsl.at[s, 48:144, :]
    )
    gather_x = Gather(gm.at[0], gather_sems[0])
    gather_x.start(0)
    gather_x.start(1)
    w4[0, chunk(d)] = dw[0].astype(BF16)
    ag_z(4, 0, *ORDER[:2])
    ag_x(4, 0, 0)
    w4[1, chunk(d)] = dw[1].astype(BF16)
    ag_x(4, 1, 0)
    rsl[s, 0:48, 0:640] = stg[pl.ds(piece_rows(s), 48), 0:640]
    rsl[s, 48:144, :] = stg[pl.ds(pl.multiple_of(piece_rows(s) + 48, 16), 96), :]
    vg[...] = jnp.zeros_like(vg)
    for copy in pieces1:
        copy.wait_recv()
    got = [rsl[k, 0:48, 0:640].astype(F32) for k in range(S)]
    for l in range(2):
        full = jnp.concatenate([g[R * l : R * (l + 1)] for g in got], axis=0)
        if l == 0:
            full = jnp.concatenate([full[:, 0:512], full[:, 512:640] + bias_cols], axis=1)
        w1[l, chunk(d)] = full.astype(BF16)
    ag_z(1, 0)
    ag_x(1, 0, 0)
    ag_x(4, 0, ORDER[0])

    bounds = []
    running = jnp.int32(0)
    for k in range(SEGS):
        running = running + lens[0, k]
        bounds.append(running)
    N = S * T

    def segments(shape, dim):
        place = lax.broadcasted_iota(jnp.int32, shape, dim)
        seg = jnp.zeros(shape, jnp.int32)
        for bound in bounds:
            seg = seg + jnp.where(place >= bound, 1, 0)
        return jnp.where(seg == SEGS - 1, SEGS + place, seg)

    segr[...] = segments((8, N), 1)
    segc[...] = segments((N, 128), 0)

    ag_x(1, 0, ORDER[0])
    for copy in pieces2:
        copy.wait_recv()
    for g, at in ((2, 48), (3, 96)):
        got = [rsl[k, at : at + 48, :].astype(F32) for k in range(S)]
        for l in range(2):
            W[g][l, chunk(d)] = jnp.concatenate(
                [piece[R * l : R * (l + 1)] for piece in got], axis=0
            ).astype(BF16)
    for copy in pieces1 + pieces2:
        copy.wait_send()
    ag_x(1, 0, ORDER[1])
    ag_x(1, 0, *ORDER[2:])
    ag_z(2, 0)
    ag_z(3, 0)
    ag_z(4, 0, *ORDER[2:])
    ag_x(2, 0, 0)
    ag_x(3, 0, 0)
    gather_x.core()
    gather_x.forward(0)
    gather_x.forward(1)
    ag_done(1, 0)
    V[...] = jnp.transpose(w1[0, :, 512:640].astype(F32))[64:96]
    gather_x.last(0)
    gather_x.last(1)
    gather_x.done()

    def vec(l, k):
        return V[8 * l + k : 8 * l + k + 1, :]

    def own_heads(row):
        total = jnp.zeros((1, 192), F32)
        for k in range(S):
            total = total + jnp.where(s == k, row[:, 192 * k : 192 * (k + 1)], 0.0)
        return total

    def at_heads(part):
        total = jnp.zeros((1, D), F32)
        for k in range(S):
            spread = [jnp.zeros((1, 192), F32)] * S
            spread[k] = part
            total = total + jnp.where(s == k, jnp.concatenate(spread, axis=1), 0.0)
        return total

    low = lax.broadcasted_iota(jnp.int32, (T, 128), 1) < 64
    low_rows = lax.broadcasted_iota(jnp.int32, (128, QBLOCK), 0) < 64

    def project_heads(l):
        bias = jnp.concatenate(
            [own_heads(vec(l, 2)), jnp.zeros((1, 192), F32), own_heads(vec(l, 3)), jnp.zeros((1, 64), F32)],
            axis=1,
        )

        @pl.loop(0, S)
        def _(i):
            r = rows(i)
            if l == 0:
                unit, _ = norm_parts(gm[0, r].astype(F32))
                a[0, r] = (unit * vec(0, 0) + vec(0, 1)).astype(BF16)
            full = (nn(a[l, r], w1[l]) + bias).astype(BF16).astype(F32)
            t0, t1, t2, t3, t4 = (full[:, 128 * j : 128 * (j + 1)] for j in range(5))
            t1r = pltpu.roll(t1, 64, 1)
            v4 = jnp.where(low, t4, 0.0)
            qh[l, 0, r] = (jnp.where(low, t0, 0.0) * SCALE_SCORE).astype(BF16)
            qh[l, 1, r] = (jnp.where(low, 0.0, t0) * SCALE_SCORE).astype(BF16)
            qh[l, 2, r] = (jnp.where(low, t1, 0.0) * SCALE_SCORE).astype(BF16)
            kk[l, 0, r] = t2.astype(BF16)
            kk[l, 1, r] = t1r.astype(BF16)
            vv[l, 0, r] = t3.astype(BF16)
            vv[l, 1, r] = v4.astype(BF16)
            kT[l, 0, :, r] = jnp.transpose(t2).astype(BF16)
            kT[l, 1, :, r] = jnp.transpose(t1r).astype(BF16)
            vT[0, :, r] = jnp.transpose(t3).astype(BF16)
            vT[1, :, r] = jnp.transpose(v4).astype(BF16)

    def query_block(qb):
        q = pl.ds(pl.multiple_of(qb * QBLOCK, QBLOCK), QBLOCK)
        k = pl.ds(pl.multiple_of((qb // 2) * (N - KEYS), 128), KEYS)
        return q, k

    def attend(l, points):
        order = (2, 3, 1)
        copies = [
            rc(oh.at[l, rows(xor(k))], goh.at[rows(s)], dev(d, xor(k)), forward_sems + k - 1)
            for k in order
        ]

        @pl.loop(0, N // QBLOCK)
        def _(i):
            for at, action in points.items():
                pl.when(i == at)(action)
            q, k = query_block(member((2 + i) * (1 - i // 2) + (3 - i) * (i // 2)))
            allowed = jnp.concatenate([segc[k, :]] * 2, axis=1) == segr[0:1, q]
            parts = []
            for h in range(3):
                scores = jnp.where(allowed, nt(kk[l, h // 2, k], qh[l, h, q]), -1e30)
                top = jnp.max(scores, axis=0, keepdims=True)
                grown = jnp.exp(scores - top)
                total = jnp.sum(grown, axis=0, keepdims=True)
                lse[l, h : h + 1, q] = top + jnp.log(total)
                parts.append(nn(vT[h // 2, :, k], grown.astype(BF16)) / total)
            oh[l, q, 0:128] = jnp.transpose(jnp.where(low_rows, parts[0], parts[1])).astype(BF16)
            oh[l, q, 128:256] = jnp.transpose(parts[2]).astype(BF16)
            for at in range(3):
                pl.when(i == at)(copies[at].start)

        goh[rows(s)] = oh[l, rows(s)]
        pending.extend(copies)
        return copies

    def attend_grad(l, copies, points):
        facc[:, 0:512] = jnp.zeros((N, 512), F32)

        @pl.loop(0, N // QBLOCK)
        def _(i):
            for at in range(1, S):
                pl.when(i == at)(lambda at=at: (copies[0, at].wait(), copies[1, at].wait())[0])
            for at, action in points.items():
                pl.when(i == at)(action)
            q, k = query_block(member(i))
            allowed = jnp.concatenate([segc[k, :]] * 2, axis=1) == segr[0:1, q]
            tiles = [goh[q, 0:128], goh[q, 128:256]]
            inner = [
                jnp.transpose(tiles[j].astype(F32) * oh[l, q, 128 * j : 128 * (j + 1)].astype(F32))
                for j in range(2)
            ]
            inner = [
                jnp.sum(inner[0][0:64], axis=0, keepdims=True),
                jnp.sum(inner[0][64:128], axis=0, keepdims=True),
                jnp.sum(inner[1], axis=0, keepdims=True),
            ]
            t0 = tiles[0].astype(F32)
            heads = [
                jnp.where(low, t0, 0.0).astype(BF16),
                jnp.where(low, 0.0, t0).astype(BF16),
                tiles[1],
            ]
            parts = []
            for h in range(3):
                p = h // 2
                queries = qh[l, h, q]
                scores = jnp.where(allowed, nt(kk[l, p, k], queries), -1e30)
                prob = jnp.exp(scores - lse[l, h : h + 1, q])
                grad = nt(vv[l, p, k], heads[h])
                grad = (prob * (grad - inner[h])).astype(BF16)
                facc[k, 256 + 128 * p : 384 + 128 * p] += nn(prob.astype(BF16), heads[h])
                facc[k, 128 * p : 128 * (p + 1)] += nn(grad, queries)
                parts.append(nn(kT[l, p, :, k], grad) * SCALE_SCORE)
            gq[q, 0:128] = jnp.transpose(jnp.where(low_rows, parts[0], parts[1])).astype(BF16)
            gq[q, 128:256] = jnp.transpose(jnp.where(low_rows, parts[2], 0.0)).astype(BF16)

        @pl.loop(0, S)
        def _(i):
            r = rows(i)
            other = pltpu.roll(facc[r, 128:256], 64, 1)
            gq[r, 128:256] = (gq[r, 128:256].astype(F32) + other).astype(BF16)
            gq[r, 256:384] = facc[r, 0:128].astype(BF16)
            gq[r, 384:512] = facc[r, 256:384].astype(BF16)
            gq[r, 512:640] = facc[r, 384:512].astype(BF16)

    def exchange(h, copies):
        for ds in (2, 3, 1):
            to = xor(ds)
            copies[h, ds] = rc(
                gq.at[half(to, h), 0:256], goh.at[half(s, h)], dev(d, to),
                backward_sems + 3 * h + ds - 1,
            )
            copies[h, ds].start()

    def up_rows(l, r):
        pre = nn(b[l, r], w3[l]) + V[16 + l : 17 + l, :]
        cdf = 0.5 * (1.0 + lax.erf(pre * 0.7071067811865476))
        density = jnp.exp(-0.5 * pre * pre) * 0.3989422804014327
        hact[l, r] = (pre * cdf).astype(BF16)
        gpb[l, r] = (cdf + pre * density).astype(BF16)

    def up_chip(l, gather, points):
        @pl.loop(0, 2)
        def _(k):
            pl.when(k == 1)(gather.core)
            for at, action in points.items():
                pl.when(k == at)(action)
            up_rows(l, rows(member(k)))

    def up_across(l, gather, h):
        gather.forward(h)

        @pl.loop(0, 2)
        def _(q):
            pl.when(q == 1)(lambda: gather.last(h))
            up_rows(l, half(member(2 + q), h))

    def scatter_rows(term, shifted=False, across=True):
        scatter = Scatter(shifted)

        @pl.loop(0, S)
        def _(i):
            k, h = 3 - i % 2, i // 2
            facc[scatter.slot(k, h)] = term(half(member(k), h))
            pl.when(i == 0)(lambda: scatter.send_core(0))
            pl.when(i == 2)(lambda: scatter.send_core(1))
            if across:
                pl.when(i == 2)(lambda: scatter.send_y(0))

        @pl.loop(0, 2)
        def _(i):
            k = 1 - i
            facc[scatter.slot(k)] = term(rows(member(k)))
            pl.when(i == 0)(scatter.send_core)
            if across:
                pl.when(i == 0)(lambda: scatter.send_y(1))

        return scatter

    def back_rows(l, scatter, r, slot):
        grad_act = nt(gm[l, r], w4[l])
        grad_pre = (grad_act * gpb[l, r].astype(F32)).astype(BF16)
        gpb[l, r] = grad_pre
        facc[slot] = nt(grad_pre, w3[l])
        vg[16 * l + 8 : 16 * l + 9, :] += jnp.sum(grad_pre.astype(F32), axis=0, keepdims=True)

    def back_chip(l, scatter, gather):
        @pl.loop(0, 2)
        def _(i):
            k = i if gather is not None else 1 - i
            if gather is not None:
                pl.when(i == 1)(gather.core)
            back_rows(l, scatter, rows(member(k)), scatter.slot(k))
            pl.when(k == 1)(scatter.send_core)

    def back_across(l, scatter, gather, h):
        if gather is not None:
            gather.forward(h)

        @pl.loop(0, 2)
        def _(i):
            k = 2 + i if gather is not None else 3 - i
            if gather is not None:
                pl.when(i == 1)(lambda: gather.last(h))
            back_rows(l, scatter, half(member(k), h), scatter.slot(k, h))
            pl.when(k == 3)(lambda: scatter.send_core(h))

    def weight_grad(g, left, right):
        @pl.loop(0, 2)
        def _(i):
            m = pl.ds(pl.multiple_of(i * 384, 384), 384)
            GW[g][m, :] = tn(left(m), right()).astype(BF16)

    def column(values):
        return jnp.sum(values.astype(F32), axis=0, keepdims=True)

    gather_cot = Gather(gm.at[1], gather_sems[2])
    last = ORDER[2:]
    for l in range(2):
        project_heads(l)
        if l == 0:
            gather_cot.start(0)
            gather_cot.start(1)
            ag_x(2, 0, *ORDER[:2])

            def core_stage():
                ag_done(2, 0)
                ag_core(2, 0, True)
                ag_x(3, 0, ORDER[1])

            copies = attend(
                0, {1: lambda: ag_x(2, 0, *last), 2: lambda: ag_x(3, 0, ORDER[0]), 3: core_stage}
            )
        else:

            def core_stage():
                ag_done(2, 1)
                ag_core(2, 1, True)

            copies = attend(
                1,
                {
                    1: lambda: ag_x(3, 1, *last),
                    2: lambda: ag_x(4, 1, ORDER[0]),
                    3: core_stage,
                },
            )
            ag_x(4, 1, ORDER[1])
        for copy in copies:
            copy.wait_recv()
        ag_core(2, l, False)
        ofull[l] = jnp.concatenate(
            [goh[T * k : T * (k + 1)].astype(F32)[:, 0:192] for k in range(S)], axis=1
        ).astype(BF16)
        before = x_in[...].astype(F32) if l == 0 else xs[...]
        middle = before + (nn(ofull[l], w2[l]) + vec(l, 4))
        x1[l] = middle
        unit, _ = norm_parts(middle)
        b[l, rows(s)] = (unit * vec(l, 5) + vec(l, 6)).astype(BF16)
        gather_b = Gather(b.at[l], gather_sems[1])
        gather_b.start(0)
        gather_b.start(1)
        if l == 0:
            gather_cot.core()
            gather_cot.forward(0)
            gather_cot.forward(1)
            ag_z(1, 1)
            ag_z(2, 1)
            ag_x(3, 0, *last)
            ag_x(4, 0, ORDER[1])
            ag_x(1, 1, 0)
            gather_cot.last(0)
            gather_cot.last(1)
            gather_cot.done()
        ag_done(3, l)
        up_chip(l, gather_b, {1: lambda: ag_x(4, 0, *last)} if l == 0 else {})
        if l == 1:
            ag_x(4, 1, *last)
            break
        ag_x(2, 1, 0)
        ag_x(3, 1, 0)
        ag_z(3, 1)
        ag_z(4, 1)
        up_across(0, gather_b, 0)
        up_across(0, gather_b, 1)
        gather_b.done()
        ag_done(4, 0)
        scatter = scatter_rows(lambda r: nn(hact[0, r], w4[0]))
        ag_x(1, 1, *ORDER)
        scatter.core_sent()
        flush()
        gather_a = Gather(a.at[1], gather_sems[0])
        for h in range(2):
            own = slice(h * H, (h + 1) * H)
            after = x1[0, own] + (scatter.finish(h) + vec(0, 7))
            xs[own] = after
            unit, _ = norm_parts(after)
            a[1, half(s, h)] = (unit * vec(1, 0) + vec(1, 1)).astype(BF16)
            gather_a.start(h)
        ag_x(2, 1, *ORDER)
        ag_x(3, 1, ORDER[0])
        ag_done(1, 1)
        gather_a.core()
        gather_a.forward(0)
        ag_x(3, 1, ORDER[1])
        gather_a.forward(1)
        gather_a.last(0)
        gather_a.last(1)
        gather_a.done()

    for l in (1, 0):
        first = l == 1
        scatter = Scatter()

        def down_grad():
            weight_grad(4, lambda m: hact[l, :, m], lambda: gm[l])
            red_x(4, l)

        if first:
            up_across(1, gather_b, 0)
            ag_done(4, 1)
            back_across(1, scatter, None, 0)
            scatter.send_y(0)
            up_across(1, gather_b, 1)
            gather_b.done()
            down_grad()
            back_across(1, scatter, None, 1)
            scatter.send_y(1)
            back_chip(1, scatter, None)
        else:
            back_chip(0, scatter, gather)
            red_z(1, 1, ORDER[1])
            back_across(0, scatter, gather, 0)
            scatter.send_y(0)
            red_z(1, 1, *last)
            back_across(0, scatter, gather, 1)
            gather.done()
            scatter.send_y(1)
            down_grad()
            red_z(1, 1, 0)
            red_sum(3, 1)
        vg[16 * l + 7 : 16 * l + 8, :] = column(gm[l, rows(s)])
        weight_grad(3, lambda m: b[l, :, m], lambda: gpb[l])
        red_x(3, l)
        scatter.core_sent()
        if first:
            scatter_out = scatter_rows(lambda r: nn(hact[1, r], w4[1]), True, False)
            red_z(4, 1, ORDER[0])
        else:
            red_z(2, 1)
            red_write(3, 1)
            red_sum(1, 1)
            out_copy.wait()
        flush()
        copies = {}
        sums = [0.0, 0.0, 0.0]
        for h in range(2):
            own = slice(h * H, (h + 1) * H)
            grad_b = scatter.finish(h)
            grad_x1, gain, shift = norm_back(x1[l, own], grad_b, vec(l, 5))
            grad_x1 = grad_x1 + (gm[1, half(s, h)].astype(F32) if first else xs[own])
            if first:
                xs_out[own] = x1[1, own] + facc[scatter_out.slot(0, h)]
            x1[l, own] = grad_x1
            gpo[own] = grad_x1.astype(BF16)
            back = nt(gpo[own], w2[l])
            for k in range(S):
                gq[half(k, h), 0:256] = jnp.concatenate(
                    [back[:, 192 * k : 192 * (k + 1)], jnp.zeros((H, 64), F32)], axis=1
                ).astype(BF16)
            exchange(h, copies)
            goh[half(s, h)] = gq[half(s, h), 0:256]
            sums = [sums[0] + gain, sums[1] + shift, sums[2] + column(gpo[own])]
        vg[16 * l + 5 : 16 * l + 6, :] = sums[0]
        vg[16 * l + 6 : 16 * l + 7, :] = sums[1]
        vg[16 * l + 4 : 16 * l + 5, :] = sums[2]
        if first:
            scatter_out.send_y(0)
            scatter_out.send_y(1)
        if first:
            red_z(4, 1, ORDER[1])
            points = {
                1: lambda: red_z(4, 1, *last),
                2: lambda: red_z(4, 1, 0),
                3: lambda: red_z(3, 1, ORDER[0]),
            }
        else:
            red_z(4, 0, *ORDER[:2])
            points = {
                1: lambda: red_sum(2, 1),
                2: lambda: (red_z(4, 0, *last), red_write(1, 1))[1],
                3: lambda: red_z(4, 0, 0),
            }
        attend_grad(l, copies, points)
        sums = column(gq[...])
        vg[16 * l + 2 : 16 * l + 3, :] = at_heads(sums[:, 0:192])
        vg[16 * l + 3 : 16 * l + 4, :] = at_heads(sums[:, 384:576])
        if first:
            scatter_out.core_sent()
        red_z(3, l, ORDER[1] if first else ORDER[0])
        scatter = scatter_rows(lambda r: nt(gq[r], w1[l]))
        if not first:
            red_z(3, 0, ORDER[1])
        weight_grad(1, lambda m: a[l, :, m], lambda: gq[...])
        red_x(1, l)
        weight_grad(2, lambda m: ofull[l, :, m], lambda: gpo[...])
        red_core(l)
        red_z(3, l, *last)
        red_x(2, l)
        if first:
            for h in range(2):
                own = slice(h * H, (h + 1) * H)
                gpo[own] = (xs_out[own] + (scatter_out.received(h) + vec(1, 7))).astype(BF16)
            out_copy = move(gpo, out.at[0])
            red_z(3, 1, 0)
            red_sum(4, 1)
        else:
            red_write(2, 1)
            red_z(3, 0, 0)
        scatter.core_sent()
        flush()
        sums = [0.0, 0.0]
        if first:
            gather = Gather(gm.at[0], gather_sems[0])
        for h in range(2):
            own = slice(h * H, (h + 1) * H)
            grad_a = scatter.finish(h)
            before = xs[own] if first else x_in[own].astype(F32)
            grad, gain, shift = norm_back(before, grad_a, vec(l, 0))
            grad = grad + x1[l, own]
            sums = [sums[0] + gain, sums[1] + shift]
            if first:
                xs[own] = grad
                gm[0, half(s, h)] = grad.astype(BF16)
                gather.start(h)
            else:
                gpo[own] = grad.astype(BF16)
        vg[16 * l : 16 * l + 1, :] = sums[0]
        vg[16 * l + 1 : 16 * l + 2, :] = sums[1]
        if not first:
            write_out(lambda: (gpo, gin.at[0]))
            gw5[...] = jnp.transpose(vg[...]).astype(BF16)
            red_x(5, 0)
        red_z(1, l, ORDER[0])

    red_sum(4, 0)
    red_z(1, 0, *ORDER[1:], 0)
    red_z(2, 0)
    red_z(5, 0)
    red_sum(3, 0)
    red_sum(1, 0)
    red_write(3, 0)
    red_sum(2, 0)
    red_sum(5, 0)
    red_write(1, 0)
    red_write(2, 0)
    red_write(5, 0)
    for i, ends in enumerate(local):
        if ends is not None:
            pltpu.make_async_copy(*ends(), near.at[i]).wait()
    flush()
    for g, i in sent_weights:
        ref = W[g].at[0, part(g, 0)]
        rc(ref, ref, x_peer, i).wait_send()


def fused_step(inputs, cotangent, image_lengths, attention, upward, downward, vectors, bias_up):
    DP = lax.axis_size("dp")
    S = lax.axis_size("seq")
    NZ = DP // 2
    L = attention.shape[0]
    T, D = inputs.shape[1], inputs.shape[2]
    N = S * T
    R = attention.shape[2]
    CH = R * S
    RP = (R + 15) // 16 * 16
    FJ = bias_up.shape[1]
    vmem, hbm = pl.BlockSpec(memory_space=pltpu.VMEM), pl.BlockSpec(memory_space=pl.ANY)
    V = pltpu.VMEM
    widths = {1: 640, 2: D, 3: D, 4: D, 5: 128}
    scratch = [
        V((L, D, 640), BF16), V((L, D, D), BF16), V((L, D, D), BF16), V((L, D, D), BF16),
        V((4 * T, D), BF16),
        V((6, T, D), BF16),
        V((L, N, D), BF16), V((L, N, D), BF16), V((L, N, D), BF16),
        V((L, 3, N, 128), BF16), V((L, 2, N, 128), BF16), V((L, 2, N, 128), BF16),
        V((L, 2, 128, N), BF16), V((2, 128, N), BF16),
        V((L, N, 256), BF16), V((L, T, D), BF16),
        V((N, 256), BF16), V((T, D), BF16),
        V((L, 8, N), F32),
        V((L, T, D), F32), V((T, D), F32), V((T, D), F32),
        V((L, N, D), BF16), V((L, N, D), BF16),
        V((N, 128), jnp.int32), V((8, N), jnp.int32),
        V((N, D), F32),
        V((N, 640), BF16),
        *[V((D, widths[g]), BF16) for g in range(1, 6)],
        *[V((NZ, CH // 2 if g == 2 else CH, widths[g]), BF16) for g in range(1, 6)],
        *[V((NZ - 1, CH // 2 if g == 2 else CH, widths[g]), BF16) for g in range(1, 6)],
        V((DP, CH // 2, D), BF16),
        *[V((2 if g == 2 else S, RP, widths[g]), BF16) for g in (1, 2, 3, 5)],
        *[V((2 if g == 2 else S, RP, widths[g]), BF16) for g in (1, 2, 3, 5)],
        V((128, 128), F32), V((32, D), F32), V((128, D), F32),
        pltpu.SemaphoreType.DMA((SEMS,)), pltpu.SemaphoreType.DMA((SEMS,)),
        pltpu.SemaphoreType.REGULAR((8,)), pltpu.SemaphoreType.REGULAR((8,)),
        V(attention.shape, F32), V(upward.shape, F32), V(downward.shape, F32),
        V((T, D), BF16),
        V(attention.shape, F32), V(upward.shape, F32), V(downward.shape, F32),
        pltpu.SemaphoreType.DMA((16,)),
    ]
    return pl.pallas_call(
        functools.partial(step_kernel, NZ),
        out_shape=(
            jax.ShapeDtypeStruct(inputs.shape, BF16),
            jax.ShapeDtypeStruct(inputs.shape, BF16),
            jax.ShapeDtypeStruct(attention.shape, F32),
            jax.ShapeDtypeStruct(upward.shape, F32),
            jax.ShapeDtypeStruct(downward.shape, F32),
            jax.ShapeDtypeStruct(vectors.shape, F32),
            jax.ShapeDtypeStruct(bias_up.shape, F32),
        ),
        in_specs=[hbm, hbm, pl.BlockSpec(memory_space=pltpu.SMEM), hbm, hbm, hbm, vmem, vmem],
        out_specs=(hbm,) * 5 + (vmem,) * 2,
        scratch_shapes=scratch,
        compiler_params=pltpu.CompilerParams(
            collective_id=0, has_side_effects=True, vmem_limit_bytes=VMEM_BYTES
        ),
    )(inputs, cotangent, image_lengths, attention, upward, downward, vectors, bias_up)


def fits_fused(inputs, attention, upward, bias_up, dp_count, seq_count):
    own_rows, width = attention.shape[2], attention.shape[3]
    return (
        seq_count == 4
        and dp_count == 8
        and inputs.shape == (1, QBLOCK, 768)
        and width == 768
        and own_rows % 8 == 0
        and upward.shape[2] == seq_count * width
        and bias_up.shape[1] % 16 == 0
    )


def update_kernel(rate, *refs):
    for member in range(5):
        gradient, master, moment, average = (refs[5 * k + member][...] for k in range(4))
        results = optimizer_step(gradient, master, moment, average, rate)
        for k in range(5):
            refs[22 + 5 * member + k][...] = results[k]
    for k in range(2):
        refs[47 + k][...] = refs[20 + k][...]


def fused_update(rate, output, input_grad, reduced, masters, moments, averages):
    attention, upward, downward, vectors, bias_up = masters
    halves = [
        pl.BlockSpec((1, 2) + attention.shape[2:], lambda l, i: (l, i, 0, 0)),
        pl.BlockSpec((1, upward.shape[1], upward.shape[2] // 2), lambda l, i: (l, 0, i)),
        pl.BlockSpec((1, downward.shape[1] // 2, downward.shape[2]), lambda l, i: (l, i, 0)),
        pl.BlockSpec((1,) + vectors.shape[1:], lambda l, i: (l, 0, 0)),
        pl.BlockSpec(bias_up.shape, lambda l, i: (0, 0)),
    ]
    tokens = pl.BlockSpec(
        (1, output.shape[1] // 4, output.shape[2]), lambda l, i: (0, 2 * l + i, 0)
    )
    outs, specs = [], []
    for member in range(5):
        for k in range(5):
            outs.append(jax.ShapeDtypeStruct(masters[member].shape, BF16 if k == 4 else F32))
            specs.append(halves[member])
    outs += [jax.ShapeDtypeStruct(output.shape, BF16)] * 2
    results = pl.pallas_call(
        functools.partial(update_kernel, rate),
        grid=(2, 2),
        out_shape=outs,
        in_specs=halves * 4 + [tokens] * 2,
        out_specs=specs + [tokens] * 2,
        compiler_params=pltpu.CompilerParams(vmem_limit_bytes=VMEM_BYTES),
    )(*reduced, *masters, *moments, *averages, output, input_grad)
    return tuple(results[25:]) + tuple(results[:25])


def per_device(
    inputs,
    cotangent,
    image_lengths,
    attention_weight,
    attention_moment,
    attention_average,
    up_weight,
    up_moment,
    up_average,
    down_weight,
    down_moment,
    down_average,
    layer_vectors,
    vector_moment,
    vector_average,
    hidden_bias,
    bias_moment,
    bias_average,
):
    masters = (attention_weight, up_weight, down_weight, layer_vectors, hidden_bias)
    dp_count = lax.axis_size("dp")
    seq_count = lax.axis_size("seq")
    if fits_fused(inputs, attention_weight, up_weight, hidden_bias, dp_count, seq_count):
        output, input_grad, *reduced = fused_step(inputs, cotangent, image_lengths, *masters)
        moments = (attention_moment, up_moment, down_moment, vector_moment, bias_moment)
        averages = (attention_average, up_average, down_average, vector_average, bias_average)
        rate = LEARN_BASE / math.sqrt(inputs.shape[0] * inputs.shape[1] * dp_count * seq_count)
        return fused_update(rate, output, input_grad, reduced, masters, moments, averages)
    else:
        output, input_grad, *reduced = plain_step(inputs, cotangent, image_lengths, masters)
    total_tokens = inputs.shape[0] * inputs.shape[1] * dp_count * seq_count
    step_rate = LEARN_BASE / math.sqrt(total_tokens)
    states = (
        (attention_weight, attention_moment, attention_average),
        (up_weight, up_moment, up_average),
        (down_weight, down_moment, down_average),
        (layer_vectors, vector_moment, vector_average),
        (hidden_bias, bias_moment, bias_average),
    )
    outcome = [output, input_grad]
    for member in range(5):
        master, moment, average = states[member]
        outcome.extend(optimizer_step(reduced[member], master, moment, average, step_rate))
    return tuple(outcome)


def solution(mesh):
    placed = (
        P("dp", "seq", None),
        P("dp", "seq", None),
        P("dp", None),
        P(None, None, ("dp", "seq"), None),
        P(None, None, ("dp", "seq"), None),
        P(None, None, ("dp", "seq"), None),
        P(None, ("dp", "seq"), None),
        P(None, ("dp", "seq"), None),
        P(None, ("dp", "seq"), None),
        P(None, ("dp", "seq"), None),
        P(None, ("dp", "seq"), None),
        P(None, ("dp", "seq"), None),
        P(None, None, ("dp", "seq")),
        P(None, None, ("dp", "seq")),
        P(None, None, ("dp", "seq")),
        P(None, ("dp", "seq")),
        P(None, ("dp", "seq")),
        P(None, ("dp", "seq")),
    )
    return jax.shard_map(
        per_device,
        mesh=mesh,
        in_specs=placed,
        out_specs=(
            P("dp", "seq", None),
            P("dp", "seq", None),
            P(None, None, ("dp", "seq"), None),
            P(None, None, ("dp", "seq"), None),
            P(None, None, ("dp", "seq"), None),
            P(None, None, ("dp", "seq"), None),
            P(None, None, ("dp", "seq"), None),
            P(None, ("dp", "seq"), None),
            P(None, ("dp", "seq"), None),
            P(None, ("dp", "seq"), None),
            P(None, ("dp", "seq"), None),
            P(None, ("dp", "seq"), None),
            P(None, ("dp", "seq"), None),
            P(None, ("dp", "seq"), None),
            P(None, ("dp", "seq"), None),
            P(None, ("dp", "seq"), None),
            P(None, ("dp", "seq"), None),
            P(None, None, ("dp", "seq")),
            P(None, None, ("dp", "seq")),
            P(None, None, ("dp", "seq")),
            P(None, None, ("dp", "seq")),
            P(None, None, ("dp", "seq")),
            P(None, ("dp", "seq")),
            P(None, ("dp", "seq")),
            P(None, ("dp", "seq")),
            P(None, ("dp", "seq")),
            P(None, ("dp", "seq")),
        ),
        check_vma=False,
    )
```

```python
import functools
import math

import jax
import jax.numpy as jnp
from jax import lax
from jax.experimental import pallas as pl
from jax.experimental.pallas import tpu as pltpu
from jax.sharding import PartitionSpec as P

HEAD_DIM = 64
SEGS = 8


EPSILON = 1e-06
SCALE_SCORE = 0.125
MOMENTUM_RATE = 0.9
DECAY_RATE = 0.0001
AVERAGE_RATE = 0.5
LEARN_BASE = 0.1
VMEM_BYTES = 66900000


def as_sent(shard):
    return jax.tree.map(lambda a: a.astype(jnp.bfloat16) if a.dtype == jnp.float32 else a, shard)


def layer_norm(values, gain_row, shift_row):
    center = values - jnp.mean(values, axis=-1, keepdims=True)
    spread = jnp.mean(center * center, axis=-1, keepdims=True)
    return center * lax.rsqrt(spread + EPSILON) * gain_row + shift_row


def gelu_exact(values):
    return jax.nn.gelu(values, approximate=False)


def project(values, matrix):
    return jnp.einsum("rti,ij->rtj", values, matrix, preferred_element_type=jnp.float32)


def project_back(grad_rows, matrix):
    return jnp.einsum("rtj,ij->rti", grad_rows, matrix, preferred_element_type=jnp.float32)


def outer_sum(values, grad_rows):
    return jnp.einsum("rti,rtj->ij", values, grad_rows, preferred_element_type=jnp.float32)


def column_sum(grad_rows):
    return jnp.sum(grad_rows, axis=(0, 1), dtype=jnp.float32)


def segment_ids(image_lengths, row_len):
    upto = jnp.arange(SEGS)[:, None] <= jnp.arange(SEGS)[None, :]
    bounds = jnp.sum(jnp.where(upto[None], image_lengths[:, :, None], 0), axis=1, dtype=jnp.int32)
    places = jnp.arange(row_len, dtype=jnp.int32)
    return jnp.sum(
        (bounds[:, None, :] <= places[None, :, None]).astype(jnp.int32), axis=-1, dtype=jnp.int32
    )


def visible_block(seg_rows, offset, block_size):
    row_len = seg_rows.shape[0]
    seg_query = seg_rows[offset : offset + block_size]
    matching = seg_query[:, None] == seg_rows[None, :]
    open_key = seg_rows[None, :] != SEGS - 1
    query_place = offset + jnp.arange(block_size, dtype=jnp.int32)
    key_place = jnp.arange(row_len, dtype=jnp.int32)
    return matching & open_key | (query_place[:, None] == key_place[None, :])


def score_block(query_block, key_heads, seg_rows, offset):
    scores = (
        jnp.einsum("qhd,khd->hqk", query_block, key_heads, preferred_element_type=jnp.float32)
        * SCALE_SCORE
    )
    allowed = visible_block(seg_rows, offset, query_block.shape[0])
    return jnp.where(allowed[None], scores, -1e30)


def split_heads(row_values):
    return row_values.reshape(row_values.shape[0], row_values.shape[1] // HEAD_DIM, HEAD_DIM)


def attend_row(row_items):
    query_row, key_row, value_row, seg_rows = row_items
    row_len = query_row.shape[0]
    query_heads = split_heads(query_row)
    key_heads = split_heads(key_row)
    value_heads = split_heads(value_row)
    block_size = min(512, row_len)
    outputs = []
    totals = []
    for offset in range(0, row_len, block_size):
        scores = score_block(query_heads[offset : offset + block_size], key_heads, seg_rows, offset)
        top_score = jnp.max(scores, axis=-1, keepdims=True)
        exponent = jnp.exp(scores - top_score)
        denominator = jnp.sum(exponent, axis=-1, keepdims=True)
        probability = (exponent / denominator).astype(jnp.bfloat16)
        outputs.append(
            jnp.einsum("hqk,khd->qhd", probability, value_heads, preferred_element_type=jnp.float32)
        )
        totals.append(top_score[..., 0] + jnp.log(denominator[..., 0]))
    mixture = jnp.concatenate(outputs, axis=0).reshape(query_row.shape).astype(jnp.bfloat16)
    return (mixture, jnp.concatenate(totals, axis=1))


def attend_back(row_items):
    query_row, key_row, value_row, grad_row, log_total, seg_rows = row_items
    row_len = query_row.shape[0]
    query_heads = split_heads(query_row)
    key_heads = split_heads(key_row)
    value_heads = split_heads(value_row)
    grad_heads = split_heads(grad_row)
    block_size = min(512, row_len)
    key_grad = jnp.zeros(key_heads.shape, jnp.float32)
    value_grad = jnp.zeros(value_heads.shape, jnp.float32)
    query_grads = []
    for offset in range(0, row_len, block_size):
        query_block = query_heads[offset : offset + block_size]
        grad_block = grad_heads[offset : offset + block_size]
        scores = score_block(query_block, key_heads, seg_rows, offset)
        probability = jnp.exp(scores - log_total[:, offset : offset + block_size, None])
        prob_low = probability.astype(jnp.bfloat16)
        prob_grad = jnp.einsum(
            "qhd,khd->hqk", grad_block, value_heads, preferred_element_type=jnp.float32
        )
        inner_sum = jnp.sum(probability * prob_grad, axis=-1, keepdims=True)
        score_grad = (probability * (prob_grad - inner_sum)).astype(jnp.bfloat16)
        query_grads.append(
            jnp.einsum("hqk,khd->qhd", score_grad, key_heads, preferred_element_type=jnp.float32)
            * SCALE_SCORE
        )
        key_grad = (
            key_grad
            + jnp.einsum(
                "hqk,qhd->khd", score_grad, query_block, preferred_element_type=jnp.float32
            )
            * SCALE_SCORE
        )
        value_grad = value_grad + jnp.einsum(
            "hqk,qhd->khd", prob_low, grad_block, preferred_element_type=jnp.float32
        )
    flat_shape = query_row.shape
    query_grad = jnp.concatenate(query_grads, axis=0)
    return (
        query_grad.reshape(flat_shape).astype(jnp.bfloat16),
        key_grad.reshape(flat_shape).astype(jnp.bfloat16),
        value_grad.reshape(flat_shape).astype(jnp.bfloat16),
    )


def layer_forward(hidden_in, params, seg_full):
    attention, upward, downward, vectors, bias_up = params
    vector_values = vectors.astype(jnp.float32)
    normed = layer_norm(hidden_in, vector_values[0], vector_values[1]).astype(jnp.bfloat16)
    queries = (project(normed, attention[0]) + vector_values[2]).astype(jnp.bfloat16)
    key_rows = project(normed, attention[1]).astype(jnp.bfloat16)
    value_rows = (project(normed, attention[2]) + vector_values[3]).astype(jnp.bfloat16)
    query_full, key_full, value_full = (
        lax.all_to_all(queries, "seq", split_axis=2, concat_axis=1, tiled=True),
        lax.all_to_all(key_rows, "seq", split_axis=2, concat_axis=1, tiled=True),
        lax.all_to_all(value_rows, "seq", split_axis=2, concat_axis=1, tiled=True),
    )
    mixture, log_total = lax.map(attend_row, (query_full, key_full, value_full, seg_full))
    mixed_tokens = lax.all_to_all(mixture, "seq", split_axis=1, concat_axis=2, tiled=True)
    residual = hidden_in + (project(mixed_tokens, attention[3]) + vector_values[4])
    normed_two = layer_norm(residual, vector_values[5], vector_values[6]).astype(jnp.bfloat16)
    hidden_pre = project(normed_two, upward) + bias_up.astype(jnp.float32)
    hidden_act = gelu_exact(hidden_pre).astype(jnp.bfloat16)
    result = residual + (project(hidden_act, downward) + vector_values[7])
    saved_values = (
        hidden_in,
        normed,
        query_full,
        key_full,
        value_full,
        log_total,
        mixed_tokens,
        residual,
        normed_two,
        hidden_pre,
        hidden_act,
    )
    return (result, saved_values)


def layer_backward(grad_out, params, saved_values, seg_full):
    attention, upward, downward, vectors, bias_up = params
    vector_values = vectors.astype(jnp.float32)
    (
        hidden_in,
        normed,
        query_full,
        key_full,
        value_full,
        log_total,
        mixed_tokens,
        residual,
        normed_two,
        hidden_pre,
        hidden_act,
    ) = saved_values
    grad_mlp = grad_out.astype(jnp.bfloat16)
    grad_down = outer_sum(hidden_act, grad_mlp)
    grad_act = project_back(grad_mlp, downward)
    grad_pre = jax.vjp(gelu_exact, hidden_pre)[1](grad_act)[0].astype(jnp.bfloat16)
    grad_up = outer_sum(normed_two, grad_pre)
    grad_normed_two = project_back(grad_pre, upward)
    norm_pull_two = jax.vjp(layer_norm, residual, vector_values[5], vector_values[6])[1]
    grad_resid_norm, grad_gain_two, grad_shift_two = norm_pull_two(grad_normed_two)
    grad_residual = grad_out + grad_resid_norm
    grad_proj = grad_residual.astype(jnp.bfloat16)
    grad_outproj = outer_sum(mixed_tokens, grad_proj)
    grad_mixed = project_back(grad_proj, attention[3]).astype(jnp.bfloat16)
    grad_heads = lax.all_to_all(grad_mixed, "seq", split_axis=2, concat_axis=1, tiled=True)
    query_grad, key_grad, value_grad = lax.map(
        attend_back, (query_full, key_full, value_full, grad_heads, log_total, seg_full)
    )
    grad_query, grad_key, grad_value = (
        lax.all_to_all(query_grad, "seq", split_axis=1, concat_axis=2, tiled=True),
        lax.all_to_all(key_grad, "seq", split_axis=1, concat_axis=2, tiled=True),
        lax.all_to_all(value_grad, "seq", split_axis=1, concat_axis=2, tiled=True),
    )
    grad_wq = outer_sum(normed, grad_query)
    grad_wk = outer_sum(normed, grad_key)
    grad_wv = outer_sum(normed, grad_value)
    grad_normed = (
        project_back(grad_query, attention[0])
        + project_back(grad_key, attention[1])
        + project_back(grad_value, attention[2])
    )
    norm_pull_one = jax.vjp(layer_norm, hidden_in, vector_values[0], vector_values[1])[1]
    grad_in_norm, grad_gain_one, grad_shift_one = norm_pull_one(grad_normed)
    grad_in = grad_residual + grad_in_norm
    attention_terms = jnp.stack([grad_wq, grad_wk, grad_wv, grad_outproj])
    vector_terms = jnp.stack(
        [
            grad_gain_one,
            grad_shift_one,
            column_sum(grad_query),
            column_sum(grad_value),
            column_sum(grad_proj),
            grad_gain_two,
            grad_shift_two,
            column_sum(grad_mlp),
        ]
    )
    return (grad_in, (attention_terms, grad_up, grad_down, vector_terms, column_sum(grad_pre)))


def fold_terms(terms, dims, dp_count, seq_count):
    folded = []
    for member in range(len(terms)):
        term = terms[member]
        place = dims[member]
        shape = term.shape
        leading = math.prod(shape[:place])
        owned = shape[place] // (dp_count * seq_count)
        trailing = owned * math.prod(shape[place + 1 :])
        folded.append(term.reshape(leading, dp_count, seq_count, trailing))
    return tuple(folded)


def unfold_terms(received, terms, dims, dp_count, seq_count):
    results = []
    for member in range(len(terms)):
        shape = terms[member].shape
        place = dims[member]
        owned_shape = shape[:place] + (shape[place] // (dp_count * seq_count),) + shape[place + 1 :]
        results.append(jnp.sum(received[member], axis=(1, 2)).reshape(owned_shape))
    return tuple(results)


def optimizer_step(gradient, master, moment, average, step_rate):
    direction = gradient + DECAY_RATE * master
    moment_new = MOMENTUM_RATE * moment + direction
    master_new = master - step_rate * (direction + MOMENTUM_RATE * moment_new)
    average_new = AVERAGE_RATE * average + (1.0 - AVERAGE_RATE) * master_new
    return (gradient, moment_new, average_new, master_new, master_new.astype(jnp.bfloat16))


def plain_step(inputs, cotangent, image_lengths, masters):
    layer_count = masters[0].shape[0]
    dp_count = lax.axis_size("dp")
    seq_count = lax.axis_size("seq")
    seg_full = segment_ids(image_lengths, inputs.shape[1] * seq_count)

    def gather_layer(level_index):
        pieces = tuple((master[level_index].astype(jnp.bfloat16) for master in masters))
        return (
            lax.all_gather(pieces[0], ("dp", "seq"), axis=1, tiled=True),
            lax.all_gather(pieces[1], ("dp", "seq"), axis=0, tiled=True),
            lax.all_gather(pieces[2], ("dp", "seq"), axis=0, tiled=True),
            lax.all_gather(pieces[3], ("dp", "seq"), axis=1, tiled=True),
            lax.all_gather(pieces[4], ("dp", "seq"), axis=0, tiled=True),
        )

    hidden = inputs.astype(jnp.float32)
    kept_params = []
    kept_saved = []
    for level_index in range(layer_count):
        params = gather_layer(level_index)
        hidden, saved_values = layer_forward(hidden, params, seg_full)
        kept_params.append(params)
        kept_saved.append(saved_values)
    output = hidden.astype(jnp.bfloat16)
    stack_dims = (2, 1, 1, 2, 1)
    grad_hidden = cotangent.astype(jnp.float32)
    layer_terms = [None] * layer_count
    for level_index in reversed(range(layer_count)):
        params = kept_params[level_index]
        grad_hidden, terms_here = layer_backward(
            grad_hidden, params, kept_saved[level_index], seg_full
        )
        layer_terms[level_index] = terms_here
    stacked = tuple(
        (jnp.stack([terms_here[member] for terms_here in layer_terms]) for member in range(5))
    )
    folded = fold_terms(stacked, stack_dims, dp_count, seq_count)
    received = jax.tree.map(
        lambda part, own: part.astype(own.dtype),
        lax.all_to_all(
            lax.all_to_all(as_sent(folded), "dp", split_axis=1, concat_axis=1, tiled=True),
            "seq",
            split_axis=2,
            concat_axis=2,
            tiled=True,
        ),
        folded,
    )
    reduced = unfold_terms(received, stacked, stack_dims, dp_count, seq_count)
    return (output, grad_hidden.astype(jnp.bfloat16), *reduced)


MESH = pl.DeviceIdType.MESH
F32 = jnp.float32
BF16 = jnp.bfloat16
KEYS = 896
EDGE_KEYS = 640
QBLOCK = 256


def nt(left, right):
    return lax.dot_general(left, right, (((1,), (1,)), ((), ())), preferred_element_type=F32)


def nn(left, right):
    return lax.dot_general(left, right, (((1,), (0,)), ((), ())), preferred_element_type=F32)


def tn(left, right):
    return lax.dot_general(left, right, (((0,), (0,)), ((), ())), preferred_element_type=F32)


def norm_parts(values):
    center = values - jnp.mean(values, axis=-1, keepdims=True)
    scale = lax.rsqrt(jnp.mean(center * center, axis=-1, keepdims=True) + EPSILON)
    return center * scale, scale


def norm_back(values, grad, gain):
    unit, scale = norm_parts(values)
    pulled = grad * gain
    first = jnp.mean(pulled, axis=-1, keepdims=True)
    second = jnp.mean(pulled * unit, axis=-1, keepdims=True)
    result = scale * (pulled - first - unit * second)
    return (
        result,
        jnp.sum(grad * unit, axis=0, keepdims=True),
        jnp.sum(grad, axis=0, keepdims=True),
    )


SEMS = 178


def step_kernel(NZ, x_hbm, cot_hbm, lens, aw_hbm, uw_hbm, dw_hbm, lv, hb, *rest):
    (out, gin, gA_hbm, gU_hbm, gD_hbm, gV, gB) = rest[:7]
    (
        w1, w2, w3, w4, stg, rsl, gm, a, b, qh, kk, vv, kT, vT, oh, ofull, goh, gpo, lse,
        x1, xs, xs_out, hact, gpb, segc, segr, facc, gq, gw1, gw2, gw3, gw4, gw5, xl1, xl2, xl3, xl4, xl5,
        zl1, zl2, zl3, zl4, zl5, cl, yl, ps1, ps2, ps3, ps5, pl1, pl2, pl3, pl5, tt, V, vg, snd, rcv,
        credx, credz, aw, uw, dw, x_in, gA, gU, gD, near,
    ) = rest[7:]
    W = {1: w1, 2: w2, 3: w3, 4: w4}
    GW = {1: gw1, 2: gw2, 3: gw3, 4: gw4, 5: gw5}
    XL = {1: xl1, 2: xl2, 3: xl3, 4: xl4, 5: xl5}
    ZL = {1: zl1, 2: zl2, 3: zl3, 4: zl4, 5: zl5}
    PS = {1: ps1, 2: ps2, 3: ps3, 5: ps5}
    PL = {1: pl1, 2: pl2, 3: pl3, 5: pl5}
    S = 4
    T, D = x_in.shape
    R = aw.shape[2]
    CH = R * S
    DP = NZ * 2
    ORDER = (1, NZ - 1) + tuple(range(2, NZ - 1))
    FJ = hb.shape[1]

    d = lax.axis_index("dp")
    s = lax.axis_index("seq")
    z, x = d // 2, d % 2
    y, c = s // 2, s % 2
    xp = 1 - x

    def xor(k):
        return ((y + k // 2) % 2) * 2 + (c + k % 2) % 2

    member = xor

    def dev(dd, ss):
        return {"dp": dd, "seq": ss}

    core_peer, y_peer, x_peer = dev(d, xor(1)), dev(d, xor(2)), dev(z * 2 + xp, s)

    def zdev(dz):
        return dev(((z + dz) % NZ) * 2 + x, s)

    count = [0]

    def sems(n):
        first = count[0]
        count[0] += n
        assert count[0] <= SEMS
        return first

    def rc(src, dst, device, i):
        return pltpu.make_async_remote_copy(
            src_ref=src, dst_ref=dst, send_sem=snd.at[i], recv_sem=rcv.at[i],
            device_id=device, device_id_type=MESH,
        )

    pending = []
    sent_weights = []

    def flush():
        for copy in pending:
            copy.wait_send()
        pending.clear()

    def rows(i):
        return pl.ds(pl.multiple_of(i * T, T), T)

    H = T // 2

    def half(i, h):
        return pl.ds(pl.multiple_of(i * T + h * H, H), H)

    def chunk(i):
        return pl.ds(pl.multiple_of(i * CH, CH), CH)

    local = []

    def move(src, dst):
        copy = pltpu.make_async_copy(src, dst, near.at[len(local)])
        local.append(None)
        copy.start()
        return copy

    def write_out(ends):
        i = len(local)
        local.append(ends)
        pltpu.make_async_copy(*ends(), near.at[i]).start()

    class Gather:
        def __init__(self, view, i):
            self.c1, self.c2, self.c3 = [], [], []
            for h in range(2):
                own, across = view.at[half(s, h)], view.at[half(xor(2), h)]
                self.c1.append(rc(own, own, core_peer, i + h))
                self.c2.append(rc(own, own, y_peer, i + 2 + h))
                self.c3.append(rc(across, across, core_peer, i + 4 + h))

        def start(self, h):
            self.c2[h].start()
            self.c1[h].start()

        def core(self):
            self.c1[0].wait_recv()
            self.c1[1].wait_recv()

        def forward(self, h):
            self.c2[h].wait_recv()
            self.c3[h].start()

        def last(self, h):
            self.c3[h].wait_recv()

        def done(self):
            pending.extend(self.c1 + self.c2 + self.c3)

    ag_sems = {
        (g, l): sems(2 * NZ - 1 if g != 2 else 2 * NZ + DP - 2) for g in W for l in range(2)
    }

    def part(g, dd):
        if g == 2:
            return pl.ds(pl.multiple_of(dd * CH + c * (CH // 2), 16), CH // 2)
        return chunk(dd)

    def ag_z(g, l, *steps):
        i = ag_sems[g, l]
        own = W[g].at[l, part(g, d)]
        for dz in steps or ORDER:
            rc(own, own, zdev(dz), i + dz - 1).start()
            sent_weights.append((g, i + dz - 1))

    def ag_x(g, l, *steps):
        i = ag_sems[g, l]
        for dz in steps:
            ref = W[g].at[l, part(g, ((z - dz + NZ) % NZ) * 2 + x)]
            if dz:
                rc(ref, ref, zdev(dz), i + dz - 1).wait_recv()
            rc(ref, ref, x_peer, i + NZ - 1 + dz).start()
            sent_weights.append((g, i + NZ - 1 + dz))

    def ag_done(g, l):
        i = ag_sems[g, l] + NZ - 1
        for dz in range(NZ):
            ref = W[g].at[l, part(g, dz)]
            rc(ref, ref, x_peer, i + dz).wait_recv()

    def ag_core(g, l, start):
        i = ag_sems[g, l] + 2 * NZ - 2
        for k in range(1, DP):
            ref = W[g].at[l, part(g, (d + k) % DP)]
            copy = rc(ref, ref, core_peer, i + k)
            if start:
                copy.start()
                sent_weights.append((g, i + k))
            else:
                copy.wait_recv()

    red_sems = {g: sems(2 * NZ + 1 + DP if g == 2 else 2 * NZ + S - 2) for g in range(1, 6)}

    def columns(g, l):
        return g == 2 and l == 0

    def own_part(g, l, dd):
        rows_of = part(g, dd)
        return (rows_of, pl.ds(pl.multiple_of(y * (D // 2), 128), D // 2)) if columns(g, l) else (rows_of,)

    def landing(g, l, k):
        return (k, slice(None), slice(0, D // 2)) if columns(g, l) else (k,)

    def x_copy(g, l, dz):
        zi = (z + dz) % NZ
        return rc(
            GW[g].at[own_part(g, l, zi * 2 + xp)], XL[g].at[landing(g, l, dz)], x_peer,
            red_sems[g] + dz,
        )

    def z_copy(g, l, dz):
        return rc(
            GW[g].at[own_part(g, l, ((z + dz) % NZ) * 2 + x)], ZL[g].at[landing(g, l, dz - 1)],
            zdev(dz), red_sems[g] + NZ - 1 + dz,
        )

    def s_copies(g, l):
        i = red_sems[g] + 2 * NZ - 2
        return [
            rc(PS[g].at[(s + ds) % S], PL[g].at[s], dev(d, (s + ds) % S), i + ds)
            for ds in range(1, S)
        ]

    def half_copies(l, action):
        i = red_sems[2] + 2 * NZ - 1
        for k in range(2):
            to = 2 * c + k
            copy = pltpu.make_async_remote_copy(
                src_ref=PS[2].at[landing(2, l, k)], dst_ref=PL[2].at[landing(2, l, y)],
                send_sem=snd.at[i + k],
                recv_sem=rcv.at[i + y], device_id=dev(d, to), device_id_type=MESH,
            )
            pl.when(to != s)(functools.partial(action, copy))

    def half_arrivals(l):
        i = red_sems[2] + 2 * NZ - 1
        for k in range(2):
            ref = PL[2].at[landing(2, l, k)]
            copy = rc(ref, ref, core_peer, i + k)
            pl.when(2 * k + s // 2 != s)(lambda copy=copy: copy.wait_recv())

    def core_copies(l):
        i = red_sems[2] + 2 * NZ + 1
        other = CH // 2 * (1 - c)
        return [
            rc(
                gw2.at[pl.ds(pl.multiple_of(k * CH + other, 16), CH // 2)], cl.at[k], core_peer, i + k
            )
            for k in range(DP)
        ]

    def red_core(l):
        for copy in core_copies(l):
            copy.start()

    def core_sum(l):
        for k, copy in enumerate(core_copies(l)):
            copy.wait_recv()
            gw2[part(2, k)] = (gw2[part(2, k)].astype(F32) + cl[k].astype(F32)).astype(BF16)

    def y_copies():
        theirs = pl.ds(pl.multiple_of((1 - y) * (D // 2), 128), D // 2)
        return [rc(gw2.at[part(2, k), theirs], yl.at[k], y_peer, y_sems + k) for k in range(DP)]

    def red_y():
        core_sum(0)
        for copy in y_copies():
            copy.start()

    def y_sum():
        for k, copy in enumerate(y_copies()):
            copy.wait_recv()
            mine = own_part(2, 0, k)
            gw2[mine] = (gw2[mine].astype(F32) + yl[k].astype(F32)).astype(BF16)

    def red_x(g, l):
        if l == 0 and g != 5:
            pl.semaphore_wait(credx.at[g], 1)
        if g == 2:
            y_sum() if l == 0 else core_sum(l)
        for dz in ORDER + (0,):
            x_copy(g, l, dz).start()

    def red_z(g, l, *steps):
        for dz in steps or ORDER + (0,):
            x_copy(g, l, dz).wait_recv()
            mine = own_part(g, l, ((z + dz) % NZ) * 2 + x)
            GW[g][mine] = (
                GW[g][mine].astype(F32) + XL[g][landing(g, l, dz)].astype(F32)
            ).astype(BF16)
            if dz:
                if l == 0 and g != 5 and dz == ORDER[0]:
                    pl.semaphore_wait(credz.at[g], NZ - 1)
                z_copy(g, l, dz).start()
            elif l == 1 and g != 5:
                pl.semaphore_signal(credx.at[g], 1, device_id=x_peer, device_id_type=MESH)

    def red_sum(g, l):
        total = GW[g][own_part(g, l, d)].astype(F32)
        for dz in ORDER:
            z_copy(g, l, dz).wait_recv()
            total = total + ZL[g][landing(g, l, dz - 1)].astype(F32)
        for dz in ORDER:
            z_copy(g, l, dz).wait_send()
        for dz in range(NZ):
            x_copy(g, l, dz).wait_send()
        if g == 2:
            for copy in core_copies(l) + (y_copies() if l == 0 else []):
                copy.wait_send()
        if l == 1 and g != 5:
            for dz in range(1, NZ):
                pl.semaphore_signal(credz.at[g], 1, device_id=zdev(dz), device_id_type=MESH)
        if g == 4:
            gD[l] = total
            write_out(lambda: (gD.at[l], gD_hbm.at[l]))
            return
        if g == 5:
            tt[0:CH, :] = total
        wide = total.shape[1]
        pad = jnp.zeros((PS[g].shape[1] - R, wide), F32)
        for k in range(2 if g == 2 else S):
            piece = jnp.concatenate([total[R * k : R * (k + 1)], pad], axis=0)
            PS[g][landing(g, l, k)] = piece.astype(BF16)
        if g == 2:
            half_copies(l, lambda copy: copy.start())

            @pl.when(s // 2 == c)
            def _():
                PL[2][landing(2, l, y)] = PS[2][landing(2, l, y)]
            return
        PL[g][s] = PS[g][s]
        for copy in s_copies(g, l):
            copy.start()

    def red_write(g, l):
        if g == 2:
            half_arrivals(l)
            two = [PL[2][landing(2, l, k)].astype(F32)[0:R] for k in range(2)]
            gA[l, 3] = jnp.concatenate(two, axis=1) if l == 0 else two[0] + two[1]
            write_out(lambda: (gA.at[l, 3], gA_hbm.at[l, 3]))
            half_copies(l, lambda copy: copy.wait_send())
            return
        for copy in s_copies(g, l):
            copy.wait_recv()
        parts = [PL[g][k].astype(F32)[0:R] for k in range(S)]
        if g == 1:
            gA[l, 0] = jnp.concatenate([p[:, 0:192] for p in parts], axis=1)
            gA[l, 1] = jnp.concatenate(
                [q for p in parts for q in (p[:, 256:384], p[:, 192:256])], axis=1
            )
            gA[l, 2] = jnp.concatenate([p[:, 384:576] for p in parts], axis=1)
            write_out(lambda: (gA.at[l, 0:3], gA_hbm.at[l, 0:3]))
        elif g == 3:
            gU[l] = jnp.concatenate(
                [parts[k][:, FJ * i : FJ * (i + 1)] for i in range(DP) for k in range(S)], axis=1
            )
            write_out(lambda: (gU.at[l], gU_hbm.at[l]))
        else:
            biases = jnp.transpose(tt[...])
            tt[0:R, :] = parts[0] + parts[1] + parts[2] + parts[3]
            vectors = jnp.transpose(tt[...])
            for k in range(2):
                gV[k] = vectors[16 * k : 16 * k + 8, 0:R]
                gB[k : k + 1, :] = biases[16 * k + 8 : 16 * k + 9, 0:CH]
        for copy in s_copies(g, l):
            copy.wait_send()

    parity = [0]
    scatter_sems = (sems(5), sems(5))
    gather_sems = (sems(6), sems(6), sems(6))
    forward_sems, backward_sems, y_sems = sems(3), sems(6), sems(DP)

    class Scatter:
        def __init__(self, shifted=False):
            base = parity[0] * 3
            i = scatter_sems[parity[0]]
            parity[0] = 1 - parity[0]
            self.base = base
            self.shifted = shifted
            self.y_at = 3 * T if shifted else 2 * T
            self.r1 = rc(stg.at[T : 2 * T], rsl.at[base + 1], core_peer, i)
            self.r0, self.r2 = [], []
            for h in range(2):
                part = pl.ds(h * H, H)
                self.r0.append(rc(stg.at[part], rsl.at[base, part], core_peer, i + 1 + h))
                at = pl.ds(self.y_at + h * H, H)
                self.r2.append(rc(stg.at[at], rsl.at[base + 2, part], y_peer, i + 3 + h))

        def slot(self, k, h=None):
            at = 1 + k - 2 * (k // 3) if self.shifted else k
            return rows(at) if h is None else half(at, h)

        def send_core(self, h=None):
            if h is None:
                stg[T : 2 * T] = facc[self.slot(1)].astype(BF16)
                self.r1.start()
            else:
                stg[h * H : (h + 1) * H] = facc[self.slot(3, h)].astype(BF16)
                self.r0[h].start()

        def send_y(self, h):
            self.r0[h].wait_recv()
            stg[self.y_at + h * H : self.y_at + (h + 1) * H] = (
                facc[self.slot(2, h)] + rsl[self.base, h * H : (h + 1) * H].astype(F32)
            ).astype(BF16)
            self.r2[h].start()

        def core_sent(self):
            for copy in (self.r1, *self.r0):
                copy.wait_send()

        def received(self, h):
            if h == 0:
                self.r1.wait_recv()
            self.r2[h].wait_recv()
            self.r2[h].wait_send()
            own = slice(h * H, (h + 1) * H)
            return rsl[self.base + 1, own].astype(F32) + rsl[self.base + 2, own].astype(F32)

        def finish(self, h):
            return facc[self.slot(0, h)] + self.received(h)

    loads = [
        move(src, dst)
        for src, dst in (
            (aw_hbm, aw), (uw_hbm, uw), (x_hbm.at[0], gm.at[0, rows(s)]), (dw_hbm, dw),
            (x_hbm.at[0], x_in), (cot_hbm.at[0], gm.at[1, rows(s)]),
        )
    ]
    barrier = pltpu.get_barrier_semaphore()
    greeted = [core_peer, y_peer, dev(d, xor(3)), x_peer] + [zdev(dz) for dz in range(1, NZ)]
    for device in greeted:
        pl.semaphore_signal(barrier, inc=1, device_id=device, device_id_type=MESH)

    tt[...] = jnp.zeros_like(tt)
    tt[64:72, 0:R] = lv[0]
    tt[72:80, 0:R] = lv[1]
    tt[80:82, 0:CH] = hb[...]
    turned = jnp.transpose(tt[...])
    lane128 = lax.broadcasted_iota(jnp.int32, (1, 128), 1)
    vec_cols = jnp.where(lane128 < 80, turned[0:R, :], 0.0)[:, 64:128]
    bias_cols = jnp.where((lane128 >= 80) & (lane128 < 82), turned[0:CH, :], 0.0)
    loads[0].wait()
    for k in range(S):
        o = 192 * k
        two = []
        for l in range(2):
            wq, wk, wv = aw[l, 0], aw[l, 1], aw[l, 2]
            tail = vec_cols if l == 0 else jnp.zeros((R, 64), F32)
            two.append(
                jnp.concatenate(
                    [wq[:, o : o + 192], wk[:, o + 128 : o + 192], wk[:, o : o + 128],
                     wv[:, o : o + 192], tail],
                    axis=1,
                )
            )
        stg[144 * k : 144 * k + 48, 0:640] = jnp.concatenate(two, axis=0).astype(BF16)
    loads[1].wait()
    for k in range(S):
        two = [
            jnp.concatenate(
                [uw[l][:, (m * S + k) * FJ : (m * S + k + 1) * FJ] for m in range(DP)], axis=1
            )
            for l in range(2)
        ]
        stg[144 * k + 48 : 144 * k + 96, :] = jnp.concatenate([aw[0, 3], aw[1, 3]], axis=0).astype(BF16)
        stg[144 * k + 96 : 144 * k + 144, :] = jnp.concatenate(two, axis=0).astype(BF16)
    for load in loads[2:]:
        load.wait()
    pl.semaphore_wait(barrier, len(greeted))

    def piece_rows(k):
        return pl.multiple_of(k * 144, 16)

    def send_pieces(source, target):
        i = sems(S - 1)
        copies = []
        for ds in (2, 3, 1):
            to = xor(ds)
            copies.append(rc(source(to), target, dev(d, to), i + ds - 1))
        for copy in copies:
            copy.start()
        return copies

    pieces1 = send_pieces(
        lambda to: stg.at[pl.ds(piece_rows(to), 48), 0:640], rsl.at[s, 0:48, 0:640]
    )
    pieces2 = send_pieces(
        lambda to: stg.at[pl.ds(pl.multiple_of(piece_rows(to) + 48, 16), 96), :], rsl.at[s, 48:144, :]
    )
    gather_x = Gather(gm.at[0], gather_sems[0])
    gather_x.start(0)
    gather_x.start(1)
    w4[0, chunk(d)] = dw[0].astype(BF16)
    ag_z(4, 0, *ORDER[:2])
    ag_x(4, 0, 0)
    w4[1, chunk(d)] = dw[1].astype(BF16)
    ag_x(4, 1, 0)
    rsl[s, 0:48, 0:640] = stg[pl.ds(piece_rows(s), 48), 0:640]
    rsl[s, 48:144, :] = stg[pl.ds(pl.multiple_of(piece_rows(s) + 48, 16), 96), :]
    vg[...] = jnp.zeros_like(vg)
    for copy in pieces1:
        copy.wait_recv()
    got = [rsl[k, 0:48, 0:640].astype(F32) for k in range(S)]
    for l in range(2):
        full = jnp.concatenate([g[R * l : R * (l + 1)] for g in got], axis=0)
        if l == 0:
            full = jnp.concatenate([full[:, 0:512], full[:, 512:640] + bias_cols], axis=1)
        w1[l, chunk(d)] = full.astype(BF16)
    ag_z(1, 0)
    ag_x(1, 0, 0)
    ag_x(4, 0, ORDER[0])

    bounds = []
    running = jnp.int32(0)
    for k in range(SEGS):
        running = running + lens[0, k]
        bounds.append(running)
    N = S * T

    def segments(shape, dim):
        place = lax.broadcasted_iota(jnp.int32, shape, dim)
        seg = jnp.zeros(shape, jnp.int32)
        for bound in bounds:
            seg = seg + jnp.where(place >= bound, 1, 0)
        return jnp.where(seg == SEGS - 1, SEGS + place, seg)

    segr[...] = segments((8, N), 1)
    segc[...] = segments((N, 128), 0)

    ag_x(1, 0, ORDER[0])
    for copy in pieces2:
        copy.wait_recv()
    for g, at in ((2, 48), (3, 96)):
        got = [rsl[k, at : at + 48, :].astype(F32) for k in range(S)]
        for l in range(2):
            W[g][l, chunk(d)] = jnp.concatenate(
                [piece[R * l : R * (l + 1)] for piece in got], axis=0
            ).astype(BF16)
    for copy in pieces1 + pieces2:
        copy.wait_send()
    ag_x(1, 0, ORDER[1])
    ag_x(1, 0, *ORDER[2:])
    ag_z(2, 0)
    ag_z(3, 0)
    ag_z(4, 0, *ORDER[2:])
    ag_x(2, 0, 0)
    ag_x(3, 0, 0)
    gather_x.core()
    gather_x.forward(0)
    gather_x.forward(1)
    gather_cot = Gather(gm.at[1], gather_sems[2])
    gather_cot.start(0)
    gather_cot.start(1)
    ag_done(1, 0)
    V[...] = jnp.transpose(w1[0, :, 512:640].astype(F32))[64:96]
    gather_x.last(0)
    gather_x.last(1)
    gather_x.done()

    def vec(l, k):
        return V[8 * l + k : 8 * l + k + 1, :]

    def own_heads(row):
        total = jnp.zeros((1, 192), F32)
        for k in range(S):
            total = total + jnp.where(s == k, row[:, 192 * k : 192 * (k + 1)], 0.0)
        return total

    def at_heads(part):
        total = jnp.zeros((1, D), F32)
        for k in range(S):
            spread = [jnp.zeros((1, 192), F32)] * S
            spread[k] = part
            total = total + jnp.where(s == k, jnp.concatenate(spread, axis=1), 0.0)
        return total

    low = lax.broadcasted_iota(jnp.int32, (T, 128), 1) < 64
    low_rows = lax.broadcasted_iota(jnp.int32, (128, QBLOCK), 0) < 64

    def project_heads(l):
        bias = jnp.concatenate(
            [own_heads(vec(l, 2)), jnp.zeros((1, 192), F32), own_heads(vec(l, 3)), jnp.zeros((1, 64), F32)],
            axis=1,
        )

        @pl.loop(0, S)
        def _(i):
            r = rows(i)
            if l == 0:
                unit, _ = norm_parts(gm[0, r].astype(F32))
                a[0, r] = (unit * vec(0, 0) + vec(0, 1)).astype(BF16)
            full = (nn(a[l, r], w1[l]) + bias).astype(BF16).astype(F32)
            t0, t1, t2, t3, t4 = (full[:, 128 * j : 128 * (j + 1)] for j in range(5))
            t1r = pltpu.roll(t1, 64, 1)
            v4 = jnp.where(low, t4, 0.0)
            qh[l, 0, r] = (jnp.where(low, t0, 0.0) * SCALE_SCORE).astype(BF16)
            qh[l, 1, r] = (jnp.where(low, 0.0, t0) * SCALE_SCORE).astype(BF16)
            qh[l, 2, r] = (jnp.where(low, t1, 0.0) * SCALE_SCORE).astype(BF16)
            kk[l, 0, r] = t2.astype(BF16)
            kk[l, 1, r] = t1r.astype(BF16)
            vv[l, 0, r] = t3.astype(BF16)
            vv[l, 1, r] = v4.astype(BF16)
            kT[l, 0, :, r] = jnp.transpose(t2).astype(BF16)
            kT[l, 1, :, r] = jnp.transpose(t1r).astype(BF16)
            vT[0, :, r] = jnp.transpose(t3).astype(BF16)
            vT[1, :, r] = jnp.transpose(v4).astype(BF16)

    def by_queries(qb, block):
        q = pl.ds(pl.multiple_of(qb * QBLOCK, QBLOCK), QBLOCK)
        edge = (qb == 0) | (qb == N // QBLOCK - 1)
        for size, here in ((EDGE_KEYS, edge), (KEYS, jnp.logical_not(edge))):
            k = pl.ds(pl.multiple_of((qb // 2) * (N - size), 128), size)
            pl.when(here)(functools.partial(block, q, k))

    def attend_block(l, q, k):
        allowed = jnp.concatenate([segc[k, :]] * 2, axis=1) == segr[0:1, q]
        parts = []
        for h in range(3):
            scores = jnp.where(allowed, nt(kk[l, h // 2, k], qh[l, h, q]), -1e30)
            top = jnp.max(scores, axis=0, keepdims=True)
            grown = jnp.exp(scores - top)
            total = jnp.sum(grown, axis=0, keepdims=True)
            lse[l, h : h + 1, q] = top + jnp.log(total)
            parts.append(nn(vT[h // 2, :, k], grown.astype(BF16)) / total)
        oh[l, q, 0:128] = jnp.transpose(jnp.where(low_rows, parts[0], parts[1])).astype(BF16)
        oh[l, q, 128:256] = jnp.transpose(parts[2]).astype(BF16)

    def attend(l, points):
        order = (2, 3, 1)
        copies = [
            rc(oh.at[l, rows(xor(k))], goh.at[rows(s)], dev(d, xor(k)), forward_sems + k - 1)
            for k in order
        ]

        @pl.loop(0, N // QBLOCK)
        def _(i):
            for at, action in points.items():
                pl.when(i == at)(action)
            by_queries(
                member((2 + i) * (1 - i // 2) + (3 - i) * (i // 2)), functools.partial(attend_block, l)
            )
            for at in range(3):
                pl.when(i == at)(copies[at].start)

        goh[rows(s)] = oh[l, rows(s)]
        pending.extend(copies)
        return copies

    def attend_grad_block(l, q, k):
        allowed = jnp.concatenate([segc[k, :]] * 2, axis=1) == segr[0:1, q]
        tiles = [goh[q, 0:128], goh[q, 128:256]]
        inner = [
            jnp.transpose(tiles[j].astype(F32) * oh[l, q, 128 * j : 128 * (j + 1)].astype(F32))
            for j in range(2)
        ]
        inner = [
            jnp.sum(inner[0][0:64], axis=0, keepdims=True),
            jnp.sum(inner[0][64:128], axis=0, keepdims=True),
            jnp.sum(inner[1], axis=0, keepdims=True),
        ]
        t0 = tiles[0].astype(F32)
        heads = [
            jnp.where(low, t0, 0.0).astype(BF16),
            jnp.where(low, 0.0, t0).astype(BF16),
            tiles[1],
        ]
        parts = []
        for h in range(3):
            p = h // 2
            queries = qh[l, h, q]
            scores = jnp.where(allowed, nt(kk[l, p, k], queries), -1e30)
            prob = jnp.exp(scores - lse[l, h : h + 1, q])
            grad = nt(vv[l, p, k], heads[h])
            grad = (prob * (grad - inner[h])).astype(BF16)
            facc[k, 256 + 128 * p : 384 + 128 * p] += nn(prob.astype(BF16), heads[h])
            facc[k, 128 * p : 128 * (p + 1)] += nn(grad, queries)
            parts.append(nn(kT[l, p, :, k], grad) * SCALE_SCORE)
        gq[q, 0:128] = jnp.transpose(jnp.where(low_rows, parts[0], parts[1])).astype(BF16)
        gq[q, 128:256] = jnp.transpose(jnp.where(low_rows, parts[2], 0.0)).astype(BF16)

    def attend_grad(l, copies, points):
        facc[:, 0:512] = jnp.zeros((N, 512), F32)

        @pl.loop(0, N // QBLOCK)
        def _(i):
            for at in range(1, S):
                pl.when(i == at)(lambda at=at: (copies[0, at].wait(), copies[1, at].wait())[0])
            for at, action in points.items():
                pl.when(i == at)(action)
            by_queries(member(i), functools.partial(attend_grad_block, l))

        @pl.loop(0, S)
        def _(i):
            r = rows(i)
            other = pltpu.roll(facc[r, 128:256], 64, 1)
            gq[r, 128:256] = (gq[r, 128:256].astype(F32) + other).astype(BF16)
            gq[r, 256:384] = facc[r, 0:128].astype(BF16)
            gq[r, 384:512] = facc[r, 256:384].astype(BF16)
            gq[r, 512:640] = facc[r, 384:512].astype(BF16)

    def exchange(h, copies):
        for ds in (2, 3, 1):
            to = xor(ds)
            copies[h, ds] = rc(
                gq.at[half(to, h), 0:256], goh.at[half(s, h)], dev(d, to),
                backward_sems + 3 * h + ds - 1,
            )
            copies[h, ds].start()

    def up_rows(l, r):
        pre = nn(b[l, r], w3[l]) + V[16 + l : 17 + l, :]
        cdf = 0.5 * (1.0 + lax.erf(pre * 0.7071067811865476))
        density = jnp.exp(-0.5 * pre * pre) * 0.3989422804014327
        hact[l, r] = (pre * cdf).astype(BF16)
        gpb[l, r] = (cdf + pre * density).astype(BF16)

    def up_chip(l, gather, points):
        @pl.loop(0, 2)
        def _(k):
            pl.when(k == 1)(gather.core)
            for at, action in points.items():
                pl.when(k == at)(action)
            up_rows(l, rows(member(k)))

    def up_across(l, gather, h):
        gather.forward(h)

        @pl.loop(0, 2)
        def _(q):
            pl.when(q == 1)(lambda: gather.last(h))
            up_rows(l, half(member(2 + q), h))

    def scatter_rows(term, shifted=False, across=True):
        scatter = Scatter(shifted)

        @pl.loop(0, S)
        def _(i):
            k, h = 3 - i % 2, i // 2
            facc[scatter.slot(k, h)] = term(half(member(k), h))
            pl.when(i == 0)(lambda: scatter.send_core(0))
            pl.when(i == 2)(lambda: scatter.send_core(1))
            if across:
                pl.when(i == 2)(lambda: scatter.send_y(0))

        @pl.loop(0, 2)
        def _(i):
            k = 1 - i
            facc[scatter.slot(k)] = term(rows(member(k)))
            pl.when(i == 0)(scatter.send_core)
            if across:
                pl.when(i == 0)(lambda: scatter.send_y(1))

        return scatter

    def back_rows(l, scatter, r, slot):
        grad_act = nt(gm[l, r], w4[l])
        grad_pre = (grad_act * gpb[l, r].astype(F32)).astype(BF16)
        gpb[l, r] = grad_pre
        facc[slot] = nt(grad_pre, w3[l])
        vg[16 * l + 8 : 16 * l + 9, :] += jnp.sum(grad_pre.astype(F32), axis=0, keepdims=True)

    def back_chip(l, scatter, gather):
        @pl.loop(0, 2)
        def _(i):
            k = i if gather is not None else 1 - i
            if gather is not None:
                pl.when(i == 1)(gather.core)
            back_rows(l, scatter, rows(member(k)), scatter.slot(k))
            pl.when(k == 1)(scatter.send_core)

    def back_across(l, scatter, gather, h):
        if gather is not None:
            gather.forward(h)

        @pl.loop(0, 2)
        def _(i):
            k = 2 + i if gather is not None else 3 - i
            if gather is not None:
                pl.when(i == 1)(lambda: gather.last(h))
            back_rows(l, scatter, half(member(k), h), scatter.slot(k, h))
            pl.when(k == 3)(lambda: scatter.send_core(h))

    def weight_grad(g, left, right):
        @pl.loop(0, 2)
        def _(i):
            m = pl.ds(pl.multiple_of(i * 384, 384), 384)
            GW[g][m, :] = tn(left(m), right()).astype(BF16)

    def column(values):
        return jnp.sum(values.astype(F32), axis=0, keepdims=True)

    last = ORDER[2:]
    for l in range(2):
        project_heads(l)
        if l == 0:
            ag_x(2, 0, *ORDER[:2])

            def core_stage():
                ag_done(2, 0)
                ag_core(2, 0, True)
                ag_x(3, 0, ORDER[1])
                gather_cot.core()
                gather_cot.forward(0)
                gather_cot.forward(1)

            copies = attend(
                0, {1: lambda: ag_x(2, 0, *last), 2: lambda: ag_x(3, 0, ORDER[0]), 3: core_stage}
            )
        else:

            def core_stage():
                ag_done(2, 1)
                ag_core(2, 1, True)

            copies = attend(
                1,
                {
                    1: lambda: ag_x(3, 1, *last),
                    2: lambda: ag_x(4, 1, ORDER[0]),
                    3: core_stage,
                },
            )
            ag_x(4, 1, ORDER[1])
        for copy in copies:
            copy.wait_recv()
        ag_core(2, l, False)
        ofull[l] = jnp.concatenate(
            [goh[T * k : T * (k + 1)].astype(F32)[:, 0:192] for k in range(S)], axis=1
        ).astype(BF16)
        before = x_in[...].astype(F32) if l == 0 else xs[...]
        middle = before + (nn(ofull[l], w2[l]) + vec(l, 4))
        x1[l] = middle
        unit, _ = norm_parts(middle)
        b[l, rows(s)] = (unit * vec(l, 5) + vec(l, 6)).astype(BF16)
        gather_b = Gather(b.at[l], gather_sems[1])
        gather_b.start(0)
        gather_b.start(1)
        if l == 0:
            ag_x(3, 0, *last)
            ag_z(1, 1)
            ag_z(2, 1)
            ag_x(4, 0, ORDER[1])
            ag_x(1, 1, 0)
            gather_cot.last(0)
            gather_cot.last(1)
            gather_cot.done()
        ag_done(3, l)
        if l == 1:
            up_chip(1, gather_b, {1: lambda: ag_x(4, 1, *last)})
            break
        up_chip(0, gather_b, {1: lambda: ag_x(4, 0, *last)})
        ag_x(2, 1, 0)
        ag_x(3, 1, 0)
        ag_z(3, 1)
        ag_z(4, 1)
        up_across(0, gather_b, 0)
        up_across(0, gather_b, 1)
        gather_b.done()
        ag_done(4, 0)
        scatter = scatter_rows(lambda r: nn(hact[0, r], w4[0]))
        ag_x(1, 1, *ORDER)
        scatter.core_sent()
        flush()
        gather_a = Gather(a.at[1], gather_sems[0])
        for h in range(2):
            own = slice(h * H, (h + 1) * H)
            after = x1[0, own] + (scatter.finish(h) + vec(0, 7))
            xs[own] = after
            unit, _ = norm_parts(after)
            a[1, half(s, h)] = (unit * vec(1, 0) + vec(1, 1)).astype(BF16)
            gather_a.start(h)
        ag_x(2, 1, *ORDER)
        ag_x(3, 1, ORDER[0])
        ag_done(1, 1)
        gather_a.core()
        gather_a.forward(0)
        ag_x(3, 1, ORDER[1])
        gather_a.forward(1)
        gather_a.last(0)
        gather_a.last(1)
        gather_a.done()

    for l in (1, 0):
        first = l == 1
        scatter = Scatter()

        def down_grad():
            weight_grad(4, lambda m: hact[l, :, m], lambda: gm[l])
            red_x(4, l)

        if first:
            ag_done(4, 1)
            back_chip(1, scatter, None)
            up_across(1, gather_b, 0)
            back_across(1, scatter, None, 0)
            scatter.send_y(0)
            up_across(1, gather_b, 1)
            gather_b.done()
            down_grad()
            back_across(1, scatter, None, 1)
            scatter.send_y(1)
        else:
            back_chip(0, scatter, gather)
            red_z(1, 1, ORDER[1])
            back_across(0, scatter, gather, 0)
            scatter.send_y(0)
            red_z(1, 1, *last)
            back_across(0, scatter, gather, 1)
            gather.done()
            red_z(1, 1, 0)
            scatter.send_y(1)
            red_z(2, 1, *ORDER[:2])
            down_grad()
            red_z(2, 1, *last, 0)
            red_sum(3, 1)
        vg[16 * l + 7 : 16 * l + 8, :] = column(gm[l, rows(s)])
        weight_grad(3, lambda m: b[l, :, m], lambda: gpb[l])
        red_x(3, l)
        scatter.core_sent()
        if first:
            scatter_out = scatter_rows(lambda r: nn(hact[1, r], w4[1]), True, False)
        else:
            out_copy.wait()
        flush()
        copies = {}
        sums = [0.0, 0.0, 0.0]
        for h in range(2):
            own = slice(h * H, (h + 1) * H)
            if h and not first:
                red_z(4, 0, ORDER[0])
            grad_b = scatter.finish(h)
            grad_x1, gain, shift = norm_back(x1[l, own], grad_b, vec(l, 5))
            grad_x1 = grad_x1 + (gm[1, half(s, h)].astype(F32) if first else xs[own])
            if first:
                xs_out[own] = x1[1, own] + facc[scatter_out.slot(0, h)]
            x1[l, own] = grad_x1
            gpo[own] = grad_x1.astype(BF16)
            back = nt(gpo[own], w2[l])
            for k in range(S):
                gq[half(k, h), 0:256] = jnp.concatenate(
                    [back[:, 192 * k : 192 * (k + 1)], jnp.zeros((H, 64), F32)], axis=1
                ).astype(BF16)
            exchange(h, copies)
            goh[half(s, h)] = gq[half(s, h), 0:256]
            sums = [sums[0] + gain, sums[1] + shift, sums[2] + column(gpo[own])]
        vg[16 * l + 5 : 16 * l + 6, :] = sums[0]
        vg[16 * l + 6 : 16 * l + 7, :] = sums[1]
        vg[16 * l + 4 : 16 * l + 5, :] = sums[2]
        if first:
            scatter_out.send_y(0)
            scatter_out.send_y(1)
        if first:
            red_z(4, 1, ORDER[0])
            points = {
                1: lambda: red_z(4, 1, ORDER[1]),
                3: lambda: red_z(4, 1, *last),
            }
        else:

            def late():
                red_z(4, 0, *last)
                red_sum(2, 1)
                weight_grad(2, lambda m: ofull[0, :, m], lambda: gpo[...])
                red_core(0)

            points = {
                0: lambda: red_sum(1, 1),
                1: lambda: red_z(4, 0, ORDER[1]),
                2: late,
                3: lambda: (red_y(), red_write(3, 1), red_write(1, 1))[1],
            }
        attend_grad(l, copies, points)
        sums = column(gq[...])
        vg[16 * l + 2 : 16 * l + 3, :] = at_heads(sums[:, 0:192])
        vg[16 * l + 3 : 16 * l + 4, :] = at_heads(sums[:, 384:576])
        if first:
            scatter_out.core_sent()
        red_z(4, l, 0)
        if not first:
            red_z(3, 0, ORDER[0])
        scatter = scatter_rows(lambda r: nt(gq[r], w1[l]))
        red_z(3, l, ORDER[0] if first else ORDER[1])
        weight_grad(1, lambda m: a[l, :, m], lambda: gq[...])
        red_x(1, l)
        if first:
            weight_grad(2, lambda m: ofull[1, :, m], lambda: gpo[...])
            red_core(1)
            red_z(3, 1, ORDER[1])
        if not first:
            red_z(3, 0, *last)
        if first:
            red_x(2, 1)
            for h in range(2):
                own = slice(h * H, (h + 1) * H)
                gpo[own] = (xs_out[own] + (scatter_out.received(h) + vec(1, 7))).astype(BF16)
            out_copy = move(gpo, out.at[0])
            red_z(3, 1, *last)
            red_sum(4, 1)
        else:
            red_x(2, 0)
            red_write(2, 1)
            red_z(3, 0, 0)
        scatter.core_sent()
        flush()
        sums = [0.0, 0.0]
        if first:
            gather = Gather(gm.at[0], gather_sems[0])
        for h in range(2):
            own = slice(h * H, (h + 1) * H)
            grad_a = scatter.finish(h)
            before = xs[own] if first else x_in[own].astype(F32)
            grad, gain, shift = norm_back(before, grad_a, vec(l, 0))
            grad = grad + x1[l, own]
            sums = [sums[0] + gain, sums[1] + shift]
            if first:
                xs[own] = grad
                gm[0, half(s, h)] = grad.astype(BF16)
                gather.start(h)
            else:
                gpo[own] = grad.astype(BF16)
        vg[16 * l : 16 * l + 1, :] = sums[0]
        vg[16 * l + 1 : 16 * l + 2, :] = sums[1]
        if not first:
            write_out(lambda: (gpo, gin.at[0]))
            gw5[...] = jnp.transpose(vg[...]).astype(BF16)
            red_x(5, 0)
        if first:
            red_z(3, 1, 0)
            red_z(1, 1, ORDER[0])

    red_z(1, 0, ORDER[0])
    red_sum(4, 0)
    red_z(1, 0, *ORDER[1:], 0)
    red_z(2, 0)
    red_z(5, 0)
    red_sum(3, 0)
    red_sum(1, 0)
    red_write(3, 0)
    red_sum(2, 0)
    red_sum(5, 0)
    red_write(1, 0)
    red_write(2, 0)
    red_write(5, 0)
    for i, ends in enumerate(local):
        if ends is not None:
            pltpu.make_async_copy(*ends(), near.at[i]).wait()
    flush()
    for g, i in sent_weights:
        ref = W[g].at[0, part(g, 0)]
        rc(ref, ref, x_peer, i).wait_send()


def fused_step(inputs, cotangent, image_lengths, attention, upward, downward, vectors, bias_up):
    DP = lax.axis_size("dp")
    S = lax.axis_size("seq")
    NZ = DP // 2
    L = attention.shape[0]
    T, D = inputs.shape[1], inputs.shape[2]
    N = S * T
    R = attention.shape[2]
    CH = R * S
    RP = (R + 15) // 16 * 16
    FJ = bias_up.shape[1]
    vmem, hbm = pl.BlockSpec(memory_space=pltpu.VMEM), pl.BlockSpec(memory_space=pl.ANY)
    V = pltpu.VMEM
    widths = {1: 640, 2: D, 3: D, 4: D, 5: 128}
    scratch = [
        V((L, D, 640), BF16), V((L, D, D), BF16), V((L, D, D), BF16), V((L, D, D), BF16),
        V((4 * T, D), BF16),
        V((6, T, D), BF16),
        V((L, N, D), BF16), V((L, N, D), BF16), V((L, N, D), BF16),
        V((L, 3, N, 128), BF16), V((L, 2, N, 128), BF16), V((L, 2, N, 128), BF16),
        V((L, 2, 128, N), BF16), V((2, 128, N), BF16),
        V((L, N, 256), BF16), V((L, T, D), BF16),
        V((N, 256), BF16), V((T, D), BF16),
        V((L, 8, N), F32),
        V((L, T, D), F32), V((T, D), F32), V((T, D), F32),
        V((L, N, D), BF16), V((L, N, D), BF16),
        V((N, 128), jnp.int32), V((8, N), jnp.int32),
        V((N, D), F32),
        V((N, 640), BF16),
        *[V((D, widths[g]), BF16) for g in range(1, 6)],
        *[V((NZ, CH // 2 if g == 2 else CH, widths[g]), BF16) for g in range(1, 6)],
        *[V((NZ - 1, CH // 2 if g == 2 else CH, widths[g]), BF16) for g in range(1, 6)],
        V((DP, CH // 2, D), BF16), V((DP, CH // 2, D // 2), BF16),
        *[V((2 if g == 2 else S, RP, widths[g]), BF16) for g in (1, 2, 3, 5)],
        *[V((2 if g == 2 else S, RP, widths[g]), BF16) for g in (1, 2, 3, 5)],
        V((128, 128), F32), V((32, D), F32), V((128, D), F32),
        pltpu.SemaphoreType.DMA((SEMS,)), pltpu.SemaphoreType.DMA((SEMS,)),
        pltpu.SemaphoreType.REGULAR((8,)), pltpu.SemaphoreType.REGULAR((8,)),
        V(attention.shape, F32), V(upward.shape, F32), V(downward.shape, F32),
        V((T, D), BF16),
        V(attention.shape, F32), V(upward.shape, F32), V(downward.shape, F32),
        pltpu.SemaphoreType.DMA((16,)),
    ]
    return pl.pallas_call(
        functools.partial(step_kernel, NZ),
        out_shape=(
            jax.ShapeDtypeStruct(inputs.shape, BF16),
            jax.ShapeDtypeStruct(inputs.shape, BF16),
            jax.ShapeDtypeStruct(attention.shape, F32),
            jax.ShapeDtypeStruct(upward.shape, F32),
            jax.ShapeDtypeStruct(downward.shape, F32),
            jax.ShapeDtypeStruct(vectors.shape, F32),
            jax.ShapeDtypeStruct(bias_up.shape, F32),
        ),
        in_specs=[hbm, hbm, pl.BlockSpec(memory_space=pltpu.SMEM), hbm, hbm, hbm, vmem, vmem],
        out_specs=(hbm,) * 5 + (vmem,) * 2,
        scratch_shapes=scratch,
        compiler_params=pltpu.CompilerParams(
            collective_id=0, has_side_effects=True, vmem_limit_bytes=VMEM_BYTES
        ),
    )(inputs, cotangent, image_lengths, attention, upward, downward, vectors, bias_up)


def fits_fused(inputs, attention, upward, bias_up, dp_count, seq_count):
    own_rows, width = attention.shape[2], attention.shape[3]
    return (
        seq_count == 4
        and dp_count == 8
        and inputs.shape == (1, QBLOCK, 768)
        and width == 768
        and own_rows % 8 == 0
        and upward.shape[2] == seq_count * width
        and bias_up.shape[1] % 16 == 0
    )


def update_kernel(rate, *refs):
    for member in range(5):
        gradient, master, moment, average = (refs[5 * k + member][...] for k in range(4))
        results = optimizer_step(gradient, master, moment, average, rate)
        for k in range(5):
            refs[22 + 5 * member + k][...] = results[k]
    for k in range(2):
        refs[47 + k][...] = refs[20 + k][...]


def fused_update(rate, output, input_grad, reduced, masters, moments, averages):
    attention, upward, downward, vectors, bias_up = masters
    blocks = [
        pl.BlockSpec((1,) + attention.shape[1:], lambda l: (l, 0, 0, 0)),
        pl.BlockSpec((1,) + upward.shape[1:], lambda l: (l, 0, 0)),
        pl.BlockSpec((1,) + downward.shape[1:], lambda l: (l, 0, 0)),
        pl.BlockSpec((1,) + vectors.shape[1:], lambda l: (l, 0, 0)),
        pl.BlockSpec(bias_up.shape, lambda l: (0, 0)),
    ]
    tokens = pl.BlockSpec((1, output.shape[1] // 2, output.shape[2]), lambda l: (0, l, 0))
    outs, specs = [], []
    for member in range(5):
        for k in range(5):
            outs.append(jax.ShapeDtypeStruct(masters[member].shape, BF16 if k == 4 else F32))
            specs.append(blocks[member])
    outs += [jax.ShapeDtypeStruct(output.shape, BF16)] * 2
    results = pl.pallas_call(
        functools.partial(update_kernel, rate),
        grid=(2,),
        out_shape=outs,
        in_specs=blocks * 4 + [tokens] * 2,
        out_specs=specs + [tokens] * 2,
        compiler_params=pltpu.CompilerParams(vmem_limit_bytes=VMEM_BYTES),
    )(*reduced, *masters, *moments, *averages, output, input_grad)
    return tuple(results[25:]) + tuple(results[:25])


def per_device(
    inputs,
    cotangent,
    image_lengths,
    attention_weight,
    attention_moment,
    attention_average,
    up_weight,
    up_moment,
    up_average,
    down_weight,
    down_moment,
    down_average,
    layer_vectors,
    vector_moment,
    vector_average,
    hidden_bias,
    bias_moment,
    bias_average,
):
    masters = (attention_weight, up_weight, down_weight, layer_vectors, hidden_bias)
    dp_count = lax.axis_size("dp")
    seq_count = lax.axis_size("seq")
    if fits_fused(inputs, attention_weight, up_weight, hidden_bias, dp_count, seq_count):
        output, input_grad, *reduced = fused_step(inputs, cotangent, image_lengths, *masters)
        moments = (attention_moment, up_moment, down_moment, vector_moment, bias_moment)
        averages = (attention_average, up_average, down_average, vector_average, bias_average)
        rate = LEARN_BASE / math.sqrt(inputs.shape[0] * inputs.shape[1] * dp_count * seq_count)
        return fused_update(rate, output, input_grad, reduced, masters, moments, averages)
    else:
        output, input_grad, *reduced = plain_step(inputs, cotangent, image_lengths, masters)
    total_tokens = inputs.shape[0] * inputs.shape[1] * dp_count * seq_count
    step_rate = LEARN_BASE / math.sqrt(total_tokens)
    states = (
        (attention_weight, attention_moment, attention_average),
        (up_weight, up_moment, up_average),
        (down_weight, down_moment, down_average),
        (layer_vectors, vector_moment, vector_average),
        (hidden_bias, bias_moment, bias_average),
    )
    outcome = [output, input_grad]
    for member in range(5):
        master, moment, average = states[member]
        outcome.extend(optimizer_step(reduced[member], master, moment, average, step_rate))
    return tuple(outcome)


def solution(mesh):
    placed = (
        P("dp", "seq", None),
        P("dp", "seq", None),
        P("dp", None),
        P(None, None, ("dp", "seq"), None),
        P(None, None, ("dp", "seq"), None),
        P(None, None, ("dp", "seq"), None),
        P(None, ("dp", "seq"), None),
        P(None, ("dp", "seq"), None),
        P(None, ("dp", "seq"), None),
        P(None, ("dp", "seq"), None),
        P(None, ("dp", "seq"), None),
        P(None, ("dp", "seq"), None),
        P(None, None, ("dp", "seq")),
        P(None, None, ("dp", "seq")),
        P(None, None, ("dp", "seq")),
        P(None, ("dp", "seq")),
        P(None, ("dp", "seq")),
        P(None, ("dp", "seq")),
    )
    return jax.shard_map(
        per_device,
        mesh=mesh,
        in_specs=placed,
        out_specs=(
            P("dp", "seq", None),
            P("dp", "seq", None),
            P(None, None, ("dp", "seq"), None),
            P(None, None, ("dp", "seq"), None),
            P(None, None, ("dp", "seq"), None),
            P(None, None, ("dp", "seq"), None),
            P(None, None, ("dp", "seq"), None),
            P(None, ("dp", "seq"), None),
            P(None, ("dp", "seq"), None),
            P(None, ("dp", "seq"), None),
            P(None, ("dp", "seq"), None),
            P(None, ("dp", "seq"), None),
            P(None, ("dp", "seq"), None),
            P(None, ("dp", "seq"), None),
            P(None, ("dp", "seq"), None),
            P(None, ("dp", "seq"), None),
            P(None, ("dp", "seq"), None),
            P(None, None, ("dp", "seq")),
            P(None, None, ("dp", "seq")),
            P(None, None, ("dp", "seq")),
            P(None, None, ("dp", "seq")),
            P(None, None, ("dp", "seq")),
            P(None, ("dp", "seq")),
            P(None, ("dp", "seq")),
            P(None, ("dp", "seq")),
            P(None, ("dp", "seq")),
            P(None, ("dp", "seq")),
        ),
        check_vma=False,
    )
```

```python
import functools
import math

import jax
import jax.numpy as jnp
from jax import lax
from jax.experimental import pallas as pl
from jax.experimental.pallas import tpu as pltpu
from jax.sharding import PartitionSpec as P

HEAD_DIM = 64
SEGS = 8


EPSILON = 1e-06
SCALE_SCORE = 0.125
MOMENTUM_RATE = 0.9
DECAY_RATE = 0.0001
AVERAGE_RATE = 0.5
LEARN_BASE = 0.1
VMEM_BYTES = 66900000


def as_sent(shard):
    return jax.tree.map(lambda a: a.astype(jnp.bfloat16) if a.dtype == jnp.float32 else a, shard)


def layer_norm(values, gain_row, shift_row):
    center = values - jnp.mean(values, axis=-1, keepdims=True)
    spread = jnp.mean(center * center, axis=-1, keepdims=True)
    return center * lax.rsqrt(spread + EPSILON) * gain_row + shift_row


def gelu_exact(values):
    return jax.nn.gelu(values, approximate=False)


def project(values, matrix):
    return jnp.einsum("rti,ij->rtj", values, matrix, preferred_element_type=jnp.float32)


def project_back(grad_rows, matrix):
    return jnp.einsum("rtj,ij->rti", grad_rows, matrix, preferred_element_type=jnp.float32)


def outer_sum(values, grad_rows):
    return jnp.einsum("rti,rtj->ij", values, grad_rows, preferred_element_type=jnp.float32)


def column_sum(grad_rows):
    return jnp.sum(grad_rows, axis=(0, 1), dtype=jnp.float32)


def segment_ids(image_lengths, row_len):
    upto = jnp.arange(SEGS)[:, None] <= jnp.arange(SEGS)[None, :]
    bounds = jnp.sum(jnp.where(upto[None], image_lengths[:, :, None], 0), axis=1, dtype=jnp.int32)
    places = jnp.arange(row_len, dtype=jnp.int32)
    return jnp.sum(
        (bounds[:, None, :] <= places[None, :, None]).astype(jnp.int32), axis=-1, dtype=jnp.int32
    )


def visible_block(seg_rows, offset, block_size):
    row_len = seg_rows.shape[0]
    seg_query = seg_rows[offset : offset + block_size]
    matching = seg_query[:, None] == seg_rows[None, :]
    open_key = seg_rows[None, :] != SEGS - 1
    query_place = offset + jnp.arange(block_size, dtype=jnp.int32)
    key_place = jnp.arange(row_len, dtype=jnp.int32)
    return matching & open_key | (query_place[:, None] == key_place[None, :])


def score_block(query_block, key_heads, seg_rows, offset):
    scores = (
        jnp.einsum("qhd,khd->hqk", query_block, key_heads, preferred_element_type=jnp.float32)
        * SCALE_SCORE
    )
    allowed = visible_block(seg_rows, offset, query_block.shape[0])
    return jnp.where(allowed[None], scores, -1e30)


def split_heads(row_values):
    return row_values.reshape(row_values.shape[0], row_values.shape[1] // HEAD_DIM, HEAD_DIM)


def attend_row(row_items):
    query_row, key_row, value_row, seg_rows = row_items
    row_len = query_row.shape[0]
    query_heads = split_heads(query_row)
    key_heads = split_heads(key_row)
    value_heads = split_heads(value_row)
    block_size = min(512, row_len)
    outputs = []
    totals = []
    for offset in range(0, row_len, block_size):
        scores = score_block(query_heads[offset : offset + block_size], key_heads, seg_rows, offset)
        top_score = jnp.max(scores, axis=-1, keepdims=True)
        exponent = jnp.exp(scores - top_score)
        denominator = jnp.sum(exponent, axis=-1, keepdims=True)
        probability = (exponent / denominator).astype(jnp.bfloat16)
        outputs.append(
            jnp.einsum("hqk,khd->qhd", probability, value_heads, preferred_element_type=jnp.float32)
        )
        totals.append(top_score[..., 0] + jnp.log(denominator[..., 0]))
    mixture = jnp.concatenate(outputs, axis=0).reshape(query_row.shape).astype(jnp.bfloat16)
    return (mixture, jnp.concatenate(totals, axis=1))


def attend_back(row_items):
    query_row, key_row, value_row, grad_row, log_total, seg_rows = row_items
    row_len = query_row.shape[0]
    query_heads = split_heads(query_row)
    key_heads = split_heads(key_row)
    value_heads = split_heads(value_row)
    grad_heads = split_heads(grad_row)
    block_size = min(512, row_len)
    key_grad = jnp.zeros(key_heads.shape, jnp.float32)
    value_grad = jnp.zeros(value_heads.shape, jnp.float32)
    query_grads = []
    for offset in range(0, row_len, block_size):
        query_block = query_heads[offset : offset + block_size]
        grad_block = grad_heads[offset : offset + block_size]
        scores = score_block(query_block, key_heads, seg_rows, offset)
        probability = jnp.exp(scores - log_total[:, offset : offset + block_size, None])
        prob_low = probability.astype(jnp.bfloat16)
        prob_grad = jnp.einsum(
            "qhd,khd->hqk", grad_block, value_heads, preferred_element_type=jnp.float32
        )
        inner_sum = jnp.sum(probability * prob_grad, axis=-1, keepdims=True)
        score_grad = (probability * (prob_grad - inner_sum)).astype(jnp.bfloat16)
        query_grads.append(
            jnp.einsum("hqk,khd->qhd", score_grad, key_heads, preferred_element_type=jnp.float32)
            * SCALE_SCORE
        )
        key_grad = (
            key_grad
            + jnp.einsum(
                "hqk,qhd->khd", score_grad, query_block, preferred_element_type=jnp.float32
            )
            * SCALE_SCORE
        )
        value_grad = value_grad + jnp.einsum(
            "hqk,qhd->khd", prob_low, grad_block, preferred_element_type=jnp.float32
        )
    flat_shape = query_row.shape
    query_grad = jnp.concatenate(query_grads, axis=0)
    return (
        query_grad.reshape(flat_shape).astype(jnp.bfloat16),
        key_grad.reshape(flat_shape).astype(jnp.bfloat16),
        value_grad.reshape(flat_shape).astype(jnp.bfloat16),
    )


def layer_forward(hidden_in, params, seg_full):
    attention, upward, downward, vectors, bias_up = params
    vector_values = vectors.astype(jnp.float32)
    normed = layer_norm(hidden_in, vector_values[0], vector_values[1]).astype(jnp.bfloat16)
    queries = (project(normed, attention[0]) + vector_values[2]).astype(jnp.bfloat16)
    key_rows = project(normed, attention[1]).astype(jnp.bfloat16)
    value_rows = (project(normed, attention[2]) + vector_values[3]).astype(jnp.bfloat16)
    query_full, key_full, value_full = (
        lax.all_to_all(queries, "seq", split_axis=2, concat_axis=1, tiled=True),
        lax.all_to_all(key_rows, "seq", split_axis=2, concat_axis=1, tiled=True),
        lax.all_to_all(value_rows, "seq", split_axis=2, concat_axis=1, tiled=True),
    )
    mixture, log_total = lax.map(attend_row, (query_full, key_full, value_full, seg_full))
    mixed_tokens = lax.all_to_all(mixture, "seq", split_axis=1, concat_axis=2, tiled=True)
    residual = hidden_in + (project(mixed_tokens, attention[3]) + vector_values[4])
    normed_two = layer_norm(residual, vector_values[5], vector_values[6]).astype(jnp.bfloat16)
    hidden_pre = project(normed_two, upward) + bias_up.astype(jnp.float32)
    hidden_act = gelu_exact(hidden_pre).astype(jnp.bfloat16)
    result = residual + (project(hidden_act, downward) + vector_values[7])
    saved_values = (
        hidden_in,
        normed,
        query_full,
        key_full,
        value_full,
        log_total,
        mixed_tokens,
        residual,
        normed_two,
        hidden_pre,
        hidden_act,
    )
    return (result, saved_values)


def layer_backward(grad_out, params, saved_values, seg_full):
    attention, upward, downward, vectors, bias_up = params
    vector_values = vectors.astype(jnp.float32)
    (
        hidden_in,
        normed,
        query_full,
        key_full,
        value_full,
        log_total,
        mixed_tokens,
        residual,
        normed_two,
        hidden_pre,
        hidden_act,
    ) = saved_values
    grad_mlp = grad_out.astype(jnp.bfloat16)
    grad_down = outer_sum(hidden_act, grad_mlp)
    grad_act = project_back(grad_mlp, downward)
    grad_pre = jax.vjp(gelu_exact, hidden_pre)[1](grad_act)[0].astype(jnp.bfloat16)
    grad_up = outer_sum(normed_two, grad_pre)
    grad_normed_two = project_back(grad_pre, upward)
    norm_pull_two = jax.vjp(layer_norm, residual, vector_values[5], vector_values[6])[1]
    grad_resid_norm, grad_gain_two, grad_shift_two = norm_pull_two(grad_normed_two)
    grad_residual = grad_out + grad_resid_norm
    grad_proj = grad_residual.astype(jnp.bfloat16)
    grad_outproj = outer_sum(mixed_tokens, grad_proj)
    grad_mixed = project_back(grad_proj, attention[3]).astype(jnp.bfloat16)
    grad_heads = lax.all_to_all(grad_mixed, "seq", split_axis=2, concat_axis=1, tiled=True)
    query_grad, key_grad, value_grad = lax.map(
        attend_back, (query_full, key_full, value_full, grad_heads, log_total, seg_full)
    )
    grad_query, grad_key, grad_value = (
        lax.all_to_all(query_grad, "seq", split_axis=1, concat_axis=2, tiled=True),
        lax.all_to_all(key_grad, "seq", split_axis=1, concat_axis=2, tiled=True),
        lax.all_to_all(value_grad, "seq", split_axis=1, concat_axis=2, tiled=True),
    )
    grad_wq = outer_sum(normed, grad_query)
    grad_wk = outer_sum(normed, grad_key)
    grad_wv = outer_sum(normed, grad_value)
    grad_normed = (
        project_back(grad_query, attention[0])
        + project_back(grad_key, attention[1])
        + project_back(grad_value, attention[2])
    )
    norm_pull_one = jax.vjp(layer_norm, hidden_in, vector_values[0], vector_values[1])[1]
    grad_in_norm, grad_gain_one, grad_shift_one = norm_pull_one(grad_normed)
    grad_in = grad_residual + grad_in_norm
    attention_terms = jnp.stack([grad_wq, grad_wk, grad_wv, grad_outproj])
    vector_terms = jnp.stack(
        [
            grad_gain_one,
            grad_shift_one,
            column_sum(grad_query),
            column_sum(grad_value),
            column_sum(grad_proj),
            grad_gain_two,
            grad_shift_two,
            column_sum(grad_mlp),
        ]
    )
    return (grad_in, (attention_terms, grad_up, grad_down, vector_terms, column_sum(grad_pre)))


def fold_terms(terms, dims, dp_count, seq_count):
    folded = []
    for member in range(len(terms)):
        term = terms[member]
        place = dims[member]
        shape = term.shape
        leading = math.prod(shape[:place])
        owned = shape[place] // (dp_count * seq_count)
        trailing = owned * math.prod(shape[place + 1 :])
        folded.append(term.reshape(leading, dp_count, seq_count, trailing))
    return tuple(folded)


def unfold_terms(received, terms, dims, dp_count, seq_count):
    results = []
    for member in range(len(terms)):
        shape = terms[member].shape
        place = dims[member]
        owned_shape = shape[:place] + (shape[place] // (dp_count * seq_count),) + shape[place + 1 :]
        results.append(jnp.sum(received[member], axis=(1, 2)).reshape(owned_shape))
    return tuple(results)


def optimizer_step(gradient, master, moment, average, step_rate):
    direction = gradient + DECAY_RATE * master
    moment_new = MOMENTUM_RATE * moment + direction
    master_new = master - step_rate * (direction + MOMENTUM_RATE * moment_new)
    average_new = AVERAGE_RATE * average + (1.0 - AVERAGE_RATE) * master_new
    return (gradient, moment_new, average_new, master_new, master_new.astype(jnp.bfloat16))


def plain_step(inputs, cotangent, image_lengths, masters):
    layer_count = masters[0].shape[0]
    dp_count = lax.axis_size("dp")
    seq_count = lax.axis_size("seq")
    seg_full = segment_ids(image_lengths, inputs.shape[1] * seq_count)

    def gather_layer(level_index):
        pieces = tuple((master[level_index].astype(jnp.bfloat16) for master in masters))
        return (
            lax.all_gather(pieces[0], ("dp", "seq"), axis=1, tiled=True),
            lax.all_gather(pieces[1], ("dp", "seq"), axis=0, tiled=True),
            lax.all_gather(pieces[2], ("dp", "seq"), axis=0, tiled=True),
            lax.all_gather(pieces[3], ("dp", "seq"), axis=1, tiled=True),
            lax.all_gather(pieces[4], ("dp", "seq"), axis=0, tiled=True),
        )

    hidden = inputs.astype(jnp.float32)
    kept_params = []
    kept_saved = []
    for level_index in range(layer_count):
        params = gather_layer(level_index)
        hidden, saved_values = layer_forward(hidden, params, seg_full)
        kept_params.append(params)
        kept_saved.append(saved_values)
    output = hidden.astype(jnp.bfloat16)
    stack_dims = (2, 1, 1, 2, 1)
    grad_hidden = cotangent.astype(jnp.float32)
    layer_terms = [None] * layer_count
    for level_index in reversed(range(layer_count)):
        params = kept_params[level_index]
        grad_hidden, terms_here = layer_backward(
            grad_hidden, params, kept_saved[level_index], seg_full
        )
        layer_terms[level_index] = terms_here
    stacked = tuple(
        (jnp.stack([terms_here[member] for terms_here in layer_terms]) for member in range(5))
    )
    folded = fold_terms(stacked, stack_dims, dp_count, seq_count)
    received = jax.tree.map(
        lambda part, own: part.astype(own.dtype),
        lax.all_to_all(
            lax.all_to_all(as_sent(folded), "dp", split_axis=1, concat_axis=1, tiled=True),
            "seq",
            split_axis=2,
            concat_axis=2,
            tiled=True,
        ),
        folded,
    )
    reduced = unfold_terms(received, stacked, stack_dims, dp_count, seq_count)
    return (output, grad_hidden.astype(jnp.bfloat16), *reduced)


MESH = pl.DeviceIdType.MESH
F32 = jnp.float32
BF16 = jnp.bfloat16
KEYS = 896
EDGE_KEYS = 640
QBLOCK = 256


def nt(left, right):
    return lax.dot_general(left, right, (((1,), (1,)), ((), ())), preferred_element_type=F32)


def nn(left, right):
    return lax.dot_general(left, right, (((1,), (0,)), ((), ())), preferred_element_type=F32)


def tn(left, right):
    return lax.dot_general(left, right, (((0,), (0,)), ((), ())), preferred_element_type=F32)


def norm_parts(values):
    center = values - jnp.mean(values, axis=-1, keepdims=True)
    scale = lax.rsqrt(jnp.mean(center * center, axis=-1, keepdims=True) + EPSILON)
    return center * scale, scale


def norm_back(values, grad, gain):
    unit, scale = norm_parts(values)
    pulled = grad * gain
    first = jnp.mean(pulled, axis=-1, keepdims=True)
    second = jnp.mean(pulled * unit, axis=-1, keepdims=True)
    result = scale * (pulled - first - unit * second)
    return (
        result,
        jnp.sum(grad * unit, axis=0, keepdims=True),
        jnp.sum(grad, axis=0, keepdims=True),
    )


SEMS = 178


def step_kernel(NZ, x_hbm, cot_hbm, lens, aw_hbm, uw_hbm, dw_hbm, lv, hb, *rest):
    (out, gin, gA_hbm, gU_hbm, gD_hbm, gV, gB) = rest[:7]
    (
        w1, w2, w3, w4, stg, rsl, gm, a, b, qh, kk, vv, kT, vT, oh, ofull, goh, gpo, lse, heads_t,
        x1, xs, xs_out, hact, gpb, segc, segr, facc, gq, gw1, gw2, gw3, gw4, gw5, xl1, xl2, xl3, xl4, xl5,
        zl1, zl2, zl3, zl4, zl5, cl, yl, ps1, ps2, ps3, ps5, pl1, pl2, pl3, pl5, tt, V, vg, snd, rcv,
        credx, credz, aw, uw, dw, x_in, gA, gU, gD, near,
    ) = rest[7:]
    W = {1: w1, 2: w2, 3: w3, 4: w4}
    GW = {1: gw1, 2: gw2, 3: gw3, 4: gw4, 5: gw5}
    XL = {1: xl1, 2: xl2, 3: xl3, 4: xl4, 5: xl5}
    ZL = {1: zl1, 2: zl2, 3: zl3, 4: zl4, 5: zl5}
    PS = {1: ps1, 2: ps2, 3: ps3, 5: ps5}
    PL = {1: pl1, 2: pl2, 3: pl3, 5: pl5}
    S = 4
    T, D = x_in.shape
    R = aw.shape[2]
    CH = R * S
    DP = NZ * 2
    ORDER = (1, NZ - 1) + tuple(range(2, NZ - 1))
    FJ = hb.shape[1]

    d = lax.axis_index("dp")
    s = lax.axis_index("seq")
    z, x = d // 2, d % 2
    y, c = s // 2, s % 2
    xp = 1 - x

    def xor(k):
        return ((y + k // 2) % 2) * 2 + (c + k % 2) % 2

    member = xor

    def dev(dd, ss):
        return {"dp": dd, "seq": ss}

    core_peer, y_peer, x_peer = dev(d, xor(1)), dev(d, xor(2)), dev(z * 2 + xp, s)

    def zdev(dz):
        return dev(((z + dz) % NZ) * 2 + x, s)

    count = [0]

    def sems(n):
        first = count[0]
        count[0] += n
        assert count[0] <= SEMS
        return first

    def rc(src, dst, device, i):
        return pltpu.make_async_remote_copy(
            src_ref=src, dst_ref=dst, send_sem=snd.at[i], recv_sem=rcv.at[i],
            device_id=device, device_id_type=MESH,
        )

    pending = []
    sent_weights = []

    def flush():
        for copy in pending:
            copy.wait_send()
        pending.clear()

    def rows(i):
        return pl.ds(pl.multiple_of(i * T, T), T)

    H = T // 2

    def half(i, h):
        return pl.ds(pl.multiple_of(i * T + h * H, H), H)

    def chunk(i):
        return pl.ds(pl.multiple_of(i * CH, CH), CH)

    local = []

    def move(src, dst):
        copy = pltpu.make_async_copy(src, dst, near.at[len(local)])
        local.append(None)
        copy.start()
        return copy

    def write_out(ends):
        i = len(local)
        local.append(ends)
        pltpu.make_async_copy(*ends(), near.at[i]).start()

    class Gather:
        def __init__(self, view, i):
            self.c1, self.c2, self.c3 = [], [], []
            for h in range(2):
                own, across = view.at[half(s, h)], view.at[half(xor(2), h)]
                self.c1.append(rc(own, own, core_peer, i + h))
                self.c2.append(rc(own, own, y_peer, i + 2 + h))
                self.c3.append(rc(across, across, core_peer, i + 4 + h))

        def start(self, h):
            self.c2[h].start()
            self.c1[h].start()

        def core(self):
            self.c1[0].wait_recv()
            self.c1[1].wait_recv()

        def forward(self, h):
            self.c2[h].wait_recv()
            self.c3[h].start()

        def last(self, h):
            self.c3[h].wait_recv()

        def done(self):
            pending.extend(self.c1 + self.c2 + self.c3)

    ag_sems = {
        (g, l): sems(2 * NZ - 1 if g != 2 else 2 * NZ + DP - 2) for g in W for l in range(2)
    }

    def part(g, dd):
        if g == 2:
            return pl.ds(pl.multiple_of(dd * CH + c * (CH // 2), 16), CH // 2)
        return chunk(dd)

    def ag_z(g, l, *steps):
        i = ag_sems[g, l]
        own = W[g].at[l, part(g, d)]
        for dz in steps or ORDER:
            rc(own, own, zdev(dz), i + dz - 1).start()
            sent_weights.append((g, i + dz - 1))

    def ag_x(g, l, *steps):
        i = ag_sems[g, l]
        for dz in steps:
            ref = W[g].at[l, part(g, ((z - dz + NZ) % NZ) * 2 + x)]
            if dz:
                rc(ref, ref, zdev(dz), i + dz - 1).wait_recv()
            rc(ref, ref, x_peer, i + NZ - 1 + dz).start()
            sent_weights.append((g, i + NZ - 1 + dz))

    def ag_done(g, l):
        i = ag_sems[g, l] + NZ - 1
        for dz in range(NZ):
            ref = W[g].at[l, part(g, dz)]
            rc(ref, ref, x_peer, i + dz).wait_recv()

    def ag_core(g, l, start):
        i = ag_sems[g, l] + 2 * NZ - 2
        for k in range(1, DP):
            ref = W[g].at[l, part(g, (d + k) % DP)]
            copy = rc(ref, ref, core_peer, i + k)
            if start:
                copy.start()
                sent_weights.append((g, i + k))
            else:
                copy.wait_recv()

    red_sems = {g: sems(2 * NZ + 1 + DP if g == 2 else 2 * NZ + S - 2) for g in range(1, 6)}

    def columns(g, l):
        return g == 2 and l == 0

    def own_part(g, l, dd):
        rows_of = part(g, dd)
        return (rows_of, pl.ds(pl.multiple_of(y * (D // 2), 128), D // 2)) if columns(g, l) else (rows_of,)

    def landing(g, l, k):
        return (k, slice(None), slice(0, D // 2)) if columns(g, l) else (k,)

    def x_copy(g, l, dz):
        zi = (z + dz) % NZ
        return rc(
            GW[g].at[own_part(g, l, zi * 2 + xp)], XL[g].at[landing(g, l, dz)], x_peer,
            red_sems[g] + dz,
        )

    def z_copy(g, l, dz):
        return rc(
            GW[g].at[own_part(g, l, ((z + dz) % NZ) * 2 + x)], ZL[g].at[landing(g, l, dz - 1)],
            zdev(dz), red_sems[g] + NZ - 1 + dz,
        )

    def s_copies(g, l):
        i = red_sems[g] + 2 * NZ - 2
        return [
            rc(PS[g].at[(s + ds) % S], PL[g].at[s], dev(d, (s + ds) % S), i + ds)
            for ds in range(1, S)
        ]

    def half_copies(l, action):
        i = red_sems[2] + 2 * NZ - 1
        for k in range(2):
            to = 2 * c + k
            copy = pltpu.make_async_remote_copy(
                src_ref=PS[2].at[landing(2, l, k)], dst_ref=PL[2].at[landing(2, l, y)],
                send_sem=snd.at[i + k],
                recv_sem=rcv.at[i + y], device_id=dev(d, to), device_id_type=MESH,
            )
            pl.when(to != s)(functools.partial(action, copy))

    def half_arrivals(l):
        i = red_sems[2] + 2 * NZ - 1
        for k in range(2):
            ref = PL[2].at[landing(2, l, k)]
            copy = rc(ref, ref, core_peer, i + k)
            pl.when(2 * k + s // 2 != s)(lambda copy=copy: copy.wait_recv())

    def core_copies(l):
        i = red_sems[2] + 2 * NZ + 1
        other = CH // 2 * (1 - c)
        return [
            rc(
                gw2.at[pl.ds(pl.multiple_of(k * CH + other, 16), CH // 2)], cl.at[k], core_peer, i + k
            )
            for k in range(DP)
        ]

    def red_core(l):
        for copy in core_copies(l):
            copy.start()

    def core_sum(l):
        for k, copy in enumerate(core_copies(l)):
            copy.wait_recv()
            gw2[part(2, k)] = (gw2[part(2, k)].astype(F32) + cl[k].astype(F32)).astype(BF16)

    def y_copies():
        theirs = pl.ds(pl.multiple_of((1 - y) * (D // 2), 128), D // 2)
        return [rc(gw2.at[part(2, k), theirs], yl.at[k], y_peer, y_sems + k) for k in range(DP)]

    def red_y():
        core_sum(0)
        for copy in y_copies():
            copy.start()

    def y_sum():
        for k, copy in enumerate(y_copies()):
            copy.wait_recv()
            mine = own_part(2, 0, k)
            gw2[mine] = (gw2[mine].astype(F32) + yl[k].astype(F32)).astype(BF16)

    def red_x(g, l):
        if l == 0 and g != 5:
            pl.semaphore_wait(credx.at[g], 1)
        if g == 2:
            y_sum() if l == 0 else core_sum(l)
        for dz in ORDER + (0,):
            x_copy(g, l, dz).start()

    def red_z(g, l, *steps):
        for dz in steps or ORDER + (0,):
            x_copy(g, l, dz).wait_recv()
            mine = own_part(g, l, ((z + dz) % NZ) * 2 + x)
            GW[g][mine] = (
                GW[g][mine].astype(F32) + XL[g][landing(g, l, dz)].astype(F32)
            ).astype(BF16)
            if dz:
                if l == 0 and g != 5 and dz == ORDER[0]:
                    pl.semaphore_wait(credz.at[g], NZ - 1)
                z_copy(g, l, dz).start()
            elif l == 1 and g != 5:
                pl.semaphore_signal(credx.at[g], 1, device_id=x_peer, device_id_type=MESH)

    def red_sum(g, l):
        total = GW[g][own_part(g, l, d)].astype(F32)
        for dz in ORDER:
            z_copy(g, l, dz).wait_recv()
            total = total + ZL[g][landing(g, l, dz - 1)].astype(F32)
        for dz in ORDER:
            z_copy(g, l, dz).wait_send()
        for dz in range(NZ):
            x_copy(g, l, dz).wait_send()
        if g == 2:
            for copy in core_copies(l) + (y_copies() if l == 0 else []):
                copy.wait_send()
        if l == 1 and g != 5:
            for dz in range(1, NZ):
                pl.semaphore_signal(credz.at[g], 1, device_id=zdev(dz), device_id_type=MESH)
        if g == 4:
            gD[l] = total
            write_out(lambda: (gD.at[l], gD_hbm.at[l]))
            return
        if g == 5:
            tt[0:CH, :] = total
        wide = total.shape[1]
        pad = jnp.zeros((PS[g].shape[1] - R, wide), F32)
        for k in range(2 if g == 2 else S):
            piece = jnp.concatenate([total[R * k : R * (k + 1)], pad], axis=0)
            PS[g][landing(g, l, k)] = piece.astype(BF16)
        if g == 2:
            half_copies(l, lambda copy: copy.start())

            @pl.when(s // 2 == c)
            def _():
                PL[2][landing(2, l, y)] = PS[2][landing(2, l, y)]
            return
        PL[g][s] = PS[g][s]
        for copy in s_copies(g, l):
            copy.start()

    def red_write(g, l):
        if g == 2:
            half_arrivals(l)
            two = [PL[2][landing(2, l, k)].astype(F32)[0:R] for k in range(2)]
            gA[l, 3] = jnp.concatenate(two, axis=1) if l == 0 else two[0] + two[1]
            write_out(lambda: (gA.at[l, 3], gA_hbm.at[l, 3]))
            half_copies(l, lambda copy: copy.wait_send())
            return
        for copy in s_copies(g, l):
            copy.wait_recv()
        parts = [PL[g][k].astype(F32)[0:R] for k in range(S)]
        if g == 1:
            gA[l, 0] = jnp.concatenate([p[:, 0:192] for p in parts], axis=1)
            gA[l, 1] = jnp.concatenate(
                [q for p in parts for q in (p[:, 256:384], p[:, 192:256])], axis=1
            )
            gA[l, 2] = jnp.concatenate([p[:, 384:576] for p in parts], axis=1)
            write_out(lambda: (gA.at[l, 0:3], gA_hbm.at[l, 0:3]))
        elif g == 3:
            gU[l] = jnp.concatenate(
                [parts[k][:, FJ * i : FJ * (i + 1)] for i in range(DP) for k in range(S)], axis=1
            )
            write_out(lambda: (gU.at[l], gU_hbm.at[l]))
        else:
            biases = jnp.transpose(tt[...])
            tt[0:R, :] = parts[0] + parts[1] + parts[2] + parts[3]
            vectors = jnp.transpose(tt[...])
            for k in range(2):
                gV[k] = vectors[16 * k : 16 * k + 8, 0:R]
                gB[k : k + 1, :] = biases[16 * k + 8 : 16 * k + 9, 0:CH]
        for copy in s_copies(g, l):
            copy.wait_send()

    parity = [0]
    scatter_sems = (sems(5), sems(5))
    gather_sems = (sems(6), sems(6), sems(6))
    forward_sems, backward_sems, y_sems = sems(3), sems(6), sems(DP)

    class Scatter:
        def __init__(self, shifted=False):
            base = parity[0] * 3
            i = scatter_sems[parity[0]]
            parity[0] = 1 - parity[0]
            self.base = base
            self.shifted = shifted
            self.y_at = 3 * T if shifted else 2 * T
            self.r1 = rc(stg.at[T : 2 * T], rsl.at[base + 1], core_peer, i)
            self.r0, self.r2 = [], []
            for h in range(2):
                part = pl.ds(h * H, H)
                self.r0.append(rc(stg.at[part], rsl.at[base, part], core_peer, i + 1 + h))
                at = pl.ds(self.y_at + h * H, H)
                self.r2.append(rc(stg.at[at], rsl.at[base + 2, part], y_peer, i + 3 + h))

        def slot(self, k, h=None):
            at = 1 + k - 2 * (k // 3) if self.shifted else k
            return rows(at) if h is None else half(at, h)

        def send_core(self, h=None):
            if h is None:
                stg[T : 2 * T] = facc[self.slot(1)].astype(BF16)
                self.r1.start()
            else:
                stg[h * H : (h + 1) * H] = facc[self.slot(3, h)].astype(BF16)
                self.r0[h].start()

        def send_y(self, h):
            self.r0[h].wait_recv()
            stg[self.y_at + h * H : self.y_at + (h + 1) * H] = (
                facc[self.slot(2, h)] + rsl[self.base, h * H : (h + 1) * H].astype(F32)
            ).astype(BF16)
            self.r2[h].start()

        def core_sent(self):
            for copy in (self.r1, *self.r0):
                copy.wait_send()

        def received(self, h):
            if h == 0:
                self.r1.wait_recv()
            self.r2[h].wait_recv()
            self.r2[h].wait_send()
            own = slice(h * H, (h + 1) * H)
            return rsl[self.base + 1, own].astype(F32) + rsl[self.base + 2, own].astype(F32)

        def finish(self, h):
            return facc[self.slot(0, h)] + self.received(h)

    loads = [
        move(src, dst)
        for src, dst in (
            (aw_hbm, aw), (uw_hbm, uw), (x_hbm.at[0], gm.at[0, rows(s)]), (dw_hbm, dw),
            (x_hbm.at[0], x_in), (cot_hbm.at[0], gm.at[1, rows(s)]),
        )
    ]
    barrier = pltpu.get_barrier_semaphore()
    greeted = [core_peer, y_peer, dev(d, xor(3)), x_peer] + [zdev(dz) for dz in range(1, NZ)]
    for device in greeted:
        pl.semaphore_signal(barrier, inc=1, device_id=device, device_id_type=MESH)

    tt[...] = jnp.zeros_like(tt)
    tt[64:72, 0:R] = lv[0]
    tt[72:80, 0:R] = lv[1]
    tt[80:82, 0:CH] = hb[...]
    turned = jnp.transpose(tt[...])
    lane128 = lax.broadcasted_iota(jnp.int32, (1, 128), 1)
    vec_cols = jnp.where(lane128 < 80, turned[0:R, :], 0.0)[:, 64:128]
    bias_cols = jnp.where((lane128 >= 80) & (lane128 < 82), turned[0:CH, :], 0.0)
    loads[0].wait()
    for k in range(S):
        o = 192 * k
        two = []
        for l in range(2):
            wq, wk, wv = aw[l, 0], aw[l, 1], aw[l, 2]
            tail = vec_cols if l == 0 else jnp.zeros((R, 64), F32)
            two.append(
                jnp.concatenate(
                    [wq[:, o : o + 192], wk[:, o + 128 : o + 192], wk[:, o : o + 128],
                     wv[:, o : o + 192], tail],
                    axis=1,
                )
            )
        stg[144 * k : 144 * k + 48, 0:640] = jnp.concatenate(two, axis=0).astype(BF16)
    loads[1].wait()
    for k in range(S):
        two = [
            jnp.concatenate(
                [uw[l][:, (m * S + k) * FJ : (m * S + k + 1) * FJ] for m in range(DP)], axis=1
            )
            for l in range(2)
        ]
        stg[144 * k + 48 : 144 * k + 96, :] = jnp.concatenate([aw[0, 3], aw[1, 3]], axis=0).astype(BF16)
        stg[144 * k + 96 : 144 * k + 144, :] = jnp.concatenate(two, axis=0).astype(BF16)
    for load in loads[2:]:
        load.wait()
    pl.semaphore_wait(barrier, len(greeted))

    def piece_rows(k):
        return pl.multiple_of(k * 144, 16)

    def send_pieces(source, target):
        i = sems(S - 1)
        copies = []
        for ds in (2, 3, 1):
            to = xor(ds)
            copies.append(rc(source(to), target, dev(d, to), i + ds - 1))
        for copy in copies:
            copy.start()
        return copies

    pieces1 = send_pieces(
        lambda to: stg.at[pl.ds(piece_rows(to), 48), 0:640], rsl.at[s, 0:48, 0:640]
    )
    pieces2 = send_pieces(
        lambda to: stg.at[pl.ds(pl.multiple_of(piece_rows(to) + 48, 16), 96), :], rsl.at[s, 48:144, :]
    )
    gather_x = Gather(gm.at[0], gather_sems[0])
    gather_x.start(0)
    gather_x.start(1)
    w4[0, chunk(d)] = dw[0].astype(BF16)
    ag_z(4, 0, *ORDER[:2])
    ag_x(4, 0, 0)
    w4[1, chunk(d)] = dw[1].astype(BF16)
    ag_x(4, 1, 0)
    rsl[s, 0:48, 0:640] = stg[pl.ds(piece_rows(s), 48), 0:640]
    rsl[s, 48:144, :] = stg[pl.ds(pl.multiple_of(piece_rows(s) + 48, 16), 96), :]
    vg[...] = jnp.zeros_like(vg)
    for copy in pieces1:
        copy.wait_recv()
    got = [rsl[k, 0:48, 0:640].astype(F32) for k in range(S)]
    for l in range(2):
        full = jnp.concatenate([g[R * l : R * (l + 1)] for g in got], axis=0)
        if l == 0:
            full = jnp.concatenate([full[:, 0:512], full[:, 512:640] + bias_cols], axis=1)
        w1[l, chunk(d)] = full.astype(BF16)
    ag_z(1, 0)
    ag_x(1, 0, 0)
    ag_x(4, 0, ORDER[0])

    bounds = []
    running = jnp.int32(0)
    for k in range(SEGS):
        running = running + lens[0, k]
        bounds.append(running)
    N = S * T

    def segments(shape, dim):
        place = lax.broadcasted_iota(jnp.int32, shape, dim)
        seg = jnp.zeros(shape, jnp.int32)
        for bound in bounds:
            seg = seg + jnp.where(place >= bound, 1, 0)
        return jnp.where(seg == SEGS - 1, SEGS + place, seg)

    segr[...] = segments((8, N), 1)
    segc[...] = segments((N, 128), 0)

    ag_x(1, 0, ORDER[0])
    for copy in pieces2:
        copy.wait_recv()
    for g, at in ((2, 48), (3, 96)):
        got = [rsl[k, at : at + 48, :].astype(F32) for k in range(S)]
        for l in range(2):
            W[g][l, chunk(d)] = jnp.concatenate(
                [piece[R * l : R * (l + 1)] for piece in got], axis=0
            ).astype(BF16)
    for copy in pieces1 + pieces2:
        copy.wait_send()
    ag_x(1, 0, ORDER[1])
    ag_x(1, 0, *ORDER[2:])
    ag_z(2, 0)
    ag_z(3, 0)
    ag_z(4, 0, *ORDER[2:])
    ag_x(2, 0, 0)
    ag_x(3, 0, 0)
    gather_x.core()
    gather_x.forward(0)
    gather_x.forward(1)
    gather_cot = Gather(gm.at[1], gather_sems[2])
    gather_cot.start(0)
    gather_cot.start(1)
    ag_done(1, 0)
    V[...] = jnp.transpose(w1[0, :, 512:640].astype(F32))[64:96]
    gather_x.last(0)
    gather_x.last(1)
    gather_x.done()

    def vec(l, k):
        return V[8 * l + k : 8 * l + k + 1, :]

    def own_heads(row):
        total = jnp.zeros((1, 192), F32)
        for k in range(S):
            total = total + jnp.where(s == k, row[:, 192 * k : 192 * (k + 1)], 0.0)
        return total

    def at_heads(part):
        total = jnp.zeros((1, D), F32)
        for k in range(S):
            spread = [jnp.zeros((1, 192), F32)] * S
            spread[k] = part
            total = total + jnp.where(s == k, jnp.concatenate(spread, axis=1), 0.0)
        return total

    low = lax.broadcasted_iota(jnp.int32, (T, 128), 1) < 64
    low_rows = lax.broadcasted_iota(jnp.int32, (128, QBLOCK), 0) < 64

    def project_heads(l):
        bias = jnp.concatenate(
            [own_heads(vec(l, 2)), jnp.zeros((1, 192), F32), own_heads(vec(l, 3)), jnp.zeros((1, 64), F32)],
            axis=1,
        )

        @pl.loop(0, S)
        def _(i):
            r = rows(i)
            if l == 0:
                unit, _ = norm_parts(gm[0, r].astype(F32))
                a[0, r] = (unit * vec(0, 0) + vec(0, 1)).astype(BF16)
            full = (nn(a[l, r], w1[l]) + bias).astype(BF16).astype(F32)
            t0, t1, t2, t3, t4 = (full[:, 128 * j : 128 * (j + 1)] for j in range(5))
            t1r = pltpu.roll(t1, 64, 1)
            v4 = jnp.where(low, t4, 0.0)
            qh[l, 0, r] = (jnp.where(low, t0, 0.0) * SCALE_SCORE).astype(BF16)
            qh[l, 1, r] = (jnp.where(low, 0.0, t0) * SCALE_SCORE).astype(BF16)
            qh[l, 2, r] = (jnp.where(low, t1, 0.0) * SCALE_SCORE).astype(BF16)
            kk[l, 0, r] = t2.astype(BF16)
            kk[l, 1, r] = t1r.astype(BF16)
            vv[l, 0, r] = t3.astype(BF16)
            vv[l, 1, r] = v4.astype(BF16)
            kT[l, 0, :, r] = jnp.transpose(t2).astype(BF16)
            kT[l, 1, :, r] = jnp.transpose(t1r).astype(BF16)
            vT[0, :, r] = jnp.transpose(t3).astype(BF16)
            vT[1, :, r] = jnp.transpose(v4).astype(BF16)

    def by_queries(qb, block):
        q = pl.ds(pl.multiple_of(qb * QBLOCK, QBLOCK), QBLOCK)
        edge = (qb == 0) | (qb == N // QBLOCK - 1)
        for size, here in ((EDGE_KEYS, edge), (KEYS, jnp.logical_not(edge))):
            k = pl.ds(pl.multiple_of((qb // 2) * (N - size), 128), size)
            pl.when(here)(functools.partial(block, q, k))

    def keep_head(h, part):
        p = h // 2
        heads_t[p] = jnp.where(low_rows & (h == 1), heads_t[p], part)

    def attend_block(l, q, k):
        @pl.loop(0, 3)
        def _(h):
            p = h // 2
            allowed = jnp.concatenate([segc[k, :]] * 2, axis=1) == segr[0:1, q]
            scores = jnp.where(allowed, nt(kk[l, p, k], qh[l, h, q]), -1e30)
            top = jnp.max(scores, axis=0, keepdims=True)
            grown = jnp.exp(scores - top)
            total = jnp.sum(grown, axis=0, keepdims=True)
            lse[l, h, :, q] = jnp.broadcast_to(top + jnp.log(total), (8, QBLOCK))
            keep_head(h, nn(vT[p, :, k], grown.astype(BF16)) / total)

        for p in range(2):
            oh[l, q, 128 * p : 128 * (p + 1)] = jnp.transpose(heads_t[p]).astype(BF16)

    def attend(l, points):
        order = (2, 3, 1)
        copies = [
            rc(oh.at[l, rows(xor(k))], goh.at[rows(s)], dev(d, xor(k)), forward_sems + k - 1)
            for k in order
        ]

        @pl.loop(0, N // QBLOCK)
        def _(i):
            for at, action in points.items():
                pl.when(i == at)(action)
            by_queries(
                member((2 + i) * (1 - i // 2) + (3 - i) * (i // 2)), functools.partial(attend_block, l)
            )
            for at in range(3):
                pl.when(i == at)(copies[at].start)

        goh[rows(s)] = oh[l, rows(s)]
        pending.extend(copies)
        return copies

    def attend_grad_block(l, q, k):
        @pl.loop(0, 3)
        def _(h):
            p = h // 2

            def tile(i):
                return pl.ds(pl.multiple_of(128 * i, 128), 128)

            head = jnp.where(low == (h != 1), goh[q, tile(p)].astype(F32), 0.0)
            inner = jnp.sum(
                jnp.transpose(head * oh[l, q, tile(p)].astype(F32)), axis=0, keepdims=True
            )
            head = head.astype(BF16)
            queries = qh[l, h, q]
            allowed = jnp.concatenate([segc[k, :]] * 2, axis=1) == segr[0:1, q]
            scores = jnp.where(allowed, nt(kk[l, p, k], queries), -1e30)
            prob = jnp.exp(scores - lse[l, h, 0:1, q])
            grad = nt(vv[l, p, k], head)
            grad = (prob * (grad - inner)).astype(BF16)
            facc[k, tile(2 + p)] += nn(prob.astype(BF16), head)
            facc[k, tile(p)] += nn(grad, queries)
            keep_head(h, nn(kT[l, p, :, k], grad) * SCALE_SCORE)

        gq[q, 0:128] = jnp.transpose(heads_t[0]).astype(BF16)
        gq[q, 128:256] = jnp.transpose(jnp.where(low_rows, heads_t[1], 0.0)).astype(BF16)

    def attend_grad(l, copies, points):
        facc[:, 0:512] = jnp.zeros((N, 512), F32)

        @pl.loop(0, N // QBLOCK)
        def _(i):
            for at in range(1, S):
                pl.when(i == at)(lambda at=at: (copies[0, at].wait(), copies[1, at].wait())[0])
            for at, action in points.items():
                pl.when(i == at)(action)
            by_queries(member(i), functools.partial(attend_grad_block, l))

        @pl.loop(0, S)
        def _(i):
            r = rows(i)
            other = pltpu.roll(facc[r, 128:256], 64, 1)
            gq[r, 128:256] = (gq[r, 128:256].astype(F32) + other).astype(BF16)
            gq[r, 256:384] = facc[r, 0:128].astype(BF16)
            gq[r, 384:512] = facc[r, 256:384].astype(BF16)
            gq[r, 512:640] = facc[r, 384:512].astype(BF16)

    def exchange(h, copies):
        for ds in (2, 3, 1):
            to = xor(ds)
            copies[h, ds] = rc(
                gq.at[half(to, h), 0:256], goh.at[half(s, h)], dev(d, to),
                backward_sems + 3 * h + ds - 1,
            )
            copies[h, ds].start()

    def up_rows(l, r):
        pre = nn(b[l, r], w3[l]) + V[16 + l : 17 + l, :]
        cdf = 0.5 * (1.0 + lax.erf(pre * 0.7071067811865476))
        density = jnp.exp(-0.5 * pre * pre) * 0.3989422804014327
        hact[l, r] = (pre * cdf).astype(BF16)
        gpb[l, r] = (cdf + pre * density).astype(BF16)

    def up_chip(l, gather, points):
        @pl.loop(0, 2)
        def _(k):
            pl.when(k == 1)(gather.core)
            for at, action in points.items():
                pl.when(k == at)(action)
            up_rows(l, rows(member(k)))

    def up_across(l, gather, h):
        gather.forward(h)

        @pl.loop(0, 2)
        def _(q):
            pl.when(q == 1)(lambda: gather.last(h))
            up_rows(l, half(member(2 + q), h))

    def scatter_rows(term, shifted=False, across=True):
        scatter = Scatter(shifted)

        @pl.loop(0, S)
        def _(i):
            k, h = 3 - i % 2, i // 2
            facc[scatter.slot(k, h)] = term(half(member(k), h))
            pl.when(i == 0)(lambda: scatter.send_core(0))
            pl.when(i == 2)(lambda: scatter.send_core(1))
            if across:
                pl.when(i == 2)(lambda: scatter.send_y(0))

        @pl.loop(0, 2)
        def _(i):
            k = 1 - i
            facc[scatter.slot(k)] = term(rows(member(k)))
            pl.when(i == 0)(scatter.send_core)
            if across:
                pl.when(i == 0)(lambda: scatter.send_y(1))

        return scatter

    def back_rows(l, scatter, r, slot):
        grad_act = nt(gm[l, r], w4[l])
        grad_pre = (grad_act * gpb[l, r].astype(F32)).astype(BF16)
        gpb[l, r] = grad_pre
        facc[slot] = nt(grad_pre, w3[l])
        vg[16 * l + 8 : 16 * l + 9, :] += jnp.sum(grad_pre.astype(F32), axis=0, keepdims=True)

    def back_chip(l, scatter, gather):
        @pl.loop(0, 2)
        def _(i):
            k = i if gather is not None else 1 - i
            if gather is not None:
                pl.when(i == 1)(gather.core)
            back_rows(l, scatter, rows(member(k)), scatter.slot(k))
            pl.when(k == 1)(scatter.send_core)

    def back_across(l, scatter, gather, h):
        if gather is not None:
            gather.forward(h)

        @pl.loop(0, 2)
        def _(i):
            k = 2 + i if gather is not None else 3 - i
            if gather is not None:
                pl.when(i == 1)(lambda: gather.last(h))
            back_rows(l, scatter, half(member(k), h), scatter.slot(k, h))
            pl.when(k == 3)(lambda: scatter.send_core(h))

    def weight_grad(g, left, right):
        @pl.loop(0, 2)
        def _(i):
            m = pl.ds(pl.multiple_of(i * 384, 384), 384)
            GW[g][m, :] = tn(left(m), right()).astype(BF16)

    def column(values):
        return jnp.sum(values.astype(F32), axis=0, keepdims=True)

    last = ORDER[2:]
    for l in range(2):
        project_heads(l)
        if l == 0:
            ag_x(2, 0, *ORDER[:2])

            def core_stage():
                ag_done(2, 0)
                ag_core(2, 0, True)
                ag_x(3, 0, ORDER[1])
                gather_cot.core()
                gather_cot.forward(0)
                gather_cot.forward(1)

            copies = attend(
                0, {1: lambda: ag_x(2, 0, *last), 2: lambda: ag_x(3, 0, ORDER[0]), 3: core_stage}
            )
        else:

            def core_stage():
                ag_done(2, 1)
                ag_core(2, 1, True)

            copies = attend(
                1,
                {
                    1: lambda: ag_x(3, 1, *last),
                    2: lambda: ag_x(4, 1, ORDER[0]),
                    3: core_stage,
                },
            )
            ag_x(4, 1, ORDER[1])
        for copy in copies:
            copy.wait_recv()
        ag_core(2, l, False)
        ofull[l] = jnp.concatenate(
            [goh[T * k : T * (k + 1)].astype(F32)[:, 0:192] for k in range(S)], axis=1
        ).astype(BF16)
        before = x_in[...].astype(F32) if l == 0 else xs[...]
        middle = before + (nn(ofull[l], w2[l]) + vec(l, 4))
        x1[l] = middle
        unit, _ = norm_parts(middle)
        b[l, rows(s)] = (unit * vec(l, 5) + vec(l, 6)).astype(BF16)
        gather_b = Gather(b.at[l], gather_sems[1])
        gather_b.start(0)
        gather_b.start(1)
        if l == 0:
            ag_x(3, 0, *last)
            ag_z(1, 1)
            ag_z(2, 1)
            ag_x(4, 0, ORDER[1])
            ag_x(1, 1, 0)
            gather_cot.last(0)
            gather_cot.last(1)
            gather_cot.done()
        ag_done(3, l)
        if l == 1:
            up_chip(1, gather_b, {1: lambda: ag_x(4, 1, *last)})
            break
        up_chip(0, gather_b, {1: lambda: ag_x(4, 0, *last)})
        ag_x(2, 1, 0)
        ag_x(3, 1, 0)
        ag_z(3, 1)
        ag_z(4, 1)
        up_across(0, gather_b, 0)
        up_across(0, gather_b, 1)
        gather_b.done()
        ag_done(4, 0)
        scatter = scatter_rows(lambda r: nn(hact[0, r], w4[0]))
        ag_x(1, 1, *ORDER)
        scatter.core_sent()
        flush()
        gather_a = Gather(a.at[1], gather_sems[0])
        for h in range(2):
            own = slice(h * H, (h + 1) * H)
            after = x1[0, own] + (scatter.finish(h) + vec(0, 7))
            xs[own] = after
            unit, _ = norm_parts(after)
            a[1, half(s, h)] = (unit * vec(1, 0) + vec(1, 1)).astype(BF16)
            gather_a.start(h)
        ag_x(2, 1, *ORDER)
        ag_x(3, 1, ORDER[0])
        ag_done(1, 1)
        gather_a.core()
        gather_a.forward(0)
        ag_x(3, 1, ORDER[1])
        gather_a.forward(1)
        gather_a.last(0)
        gather_a.last(1)
        gather_a.done()

    for l in (1, 0):
        first = l == 1
        scatter = Scatter()

        def down_grad():
            weight_grad(4, lambda m: hact[l, :, m], lambda: gm[l])
            red_x(4, l)

        if first:
            ag_done(4, 1)
            back_chip(1, scatter, None)
            up_across(1, gather_b, 0)
            back_across(1, scatter, None, 0)
            scatter.send_y(0)
            up_across(1, gather_b, 1)
            gather_b.done()
            down_grad()
            back_across(1, scatter, None, 1)
            scatter.send_y(1)
        else:
            back_chip(0, scatter, gather)
            red_z(1, 1, ORDER[1])
            back_across(0, scatter, gather, 0)
            scatter.send_y(0)
            red_z(1, 1, *last)
            back_across(0, scatter, gather, 1)
            gather.done()
            red_z(1, 1, 0)
            scatter.send_y(1)
            red_z(2, 1, *ORDER[:2])
            down_grad()
            red_z(2, 1, *last, 0)
            red_sum(3, 1)
        vg[16 * l + 7 : 16 * l + 8, :] = column(gm[l, rows(s)])
        weight_grad(3, lambda m: b[l, :, m], lambda: gpb[l])
        red_x(3, l)
        scatter.core_sent()
        if first:
            scatter_out = scatter_rows(lambda r: nn(hact[1, r], w4[1]), True, False)
        else:
            out_copy.wait()
        flush()
        copies = {}
        sums = [0.0, 0.0, 0.0]
        for h in range(2):
            own = slice(h * H, (h + 1) * H)
            if h and not first:
                red_z(4, 0, ORDER[0])
            grad_b = scatter.finish(h)
            grad_x1, gain, shift = norm_back(x1[l, own], grad_b, vec(l, 5))
            grad_x1 = grad_x1 + (gm[1, half(s, h)].astype(F32) if first else xs[own])
            if first:
                xs_out[own] = x1[1, own] + facc[scatter_out.slot(0, h)]
            x1[l, own] = grad_x1
            gpo[own] = grad_x1.astype(BF16)
            back = nt(gpo[own], w2[l])
            for k in range(S):
                gq[half(k, h), 0:256] = jnp.concatenate(
                    [back[:, 192 * k : 192 * (k + 1)], jnp.zeros((H, 64), F32)], axis=1
                ).astype(BF16)
            exchange(h, copies)
            goh[half(s, h)] = gq[half(s, h), 0:256]
            sums = [sums[0] + gain, sums[1] + shift, sums[2] + column(gpo[own])]
        vg[16 * l + 5 : 16 * l + 6, :] = sums[0]
        vg[16 * l + 6 : 16 * l + 7, :] = sums[1]
        vg[16 * l + 4 : 16 * l + 5, :] = sums[2]
        if first:
            scatter_out.send_y(0)
            scatter_out.send_y(1)
        if first:
            red_z(4, 1, ORDER[0])
            points = {
                1: lambda: red_z(4, 1, ORDER[1]),
                3: lambda: red_z(4, 1, *last),
            }
        else:

            def late():
                red_z(4, 0, *last)
                red_sum(2, 1)
                weight_grad(2, lambda m: ofull[0, :, m], lambda: gpo[...])
                red_core(0)

            points = {
                0: lambda: red_sum(1, 1),
                1: lambda: red_z(4, 0, ORDER[1]),
                2: late,
                3: lambda: (red_y(), red_write(3, 1), red_write(1, 1))[1],
            }
        attend_grad(l, copies, points)
        sums = column(gq[...])
        vg[16 * l + 2 : 16 * l + 3, :] = at_heads(sums[:, 0:192])
        vg[16 * l + 3 : 16 * l + 4, :] = at_heads(sums[:, 384:576])
        if first:
            scatter_out.core_sent()
        red_z(4, l, 0)
        if not first:
            red_z(3, 0, ORDER[0])
        scatter = scatter_rows(lambda r: nt(gq[r], w1[l]))
        red_z(3, l, ORDER[0] if first else ORDER[1])
        weight_grad(1, lambda m: a[l, :, m], lambda: gq[...])
        red_x(1, l)
        if first:
            weight_grad(2, lambda m: ofull[1, :, m], lambda: gpo[...])
            red_core(1)
            red_z(3, 1, ORDER[1])
        if not first:
            red_z(3, 0, *last)
        if first:
            red_x(2, 1)
            for h in range(2):
                own = slice(h * H, (h + 1) * H)
                gpo[own] = (xs_out[own] + (scatter_out.received(h) + vec(1, 7))).astype(BF16)
            out_copy = move(gpo, out.at[0])
            red_z(3, 1, *last)
            red_sum(4, 1)
        else:
            red_x(2, 0)
            red_write(2, 1)
            red_z(3, 0, 0)
        scatter.core_sent()
        flush()
        sums = [0.0, 0.0]
        if first:
            gather = Gather(gm.at[0], gather_sems[0])
        for h in range(2):
            own = slice(h * H, (h + 1) * H)
            grad_a = scatter.finish(h)
            before = xs[own] if first else x_in[own].astype(F32)
            grad, gain, shift = norm_back(before, grad_a, vec(l, 0))
            grad = grad + x1[l, own]
            sums = [sums[0] + gain, sums[1] + shift]
            if first:
                xs[own] = grad
                gm[0, half(s, h)] = grad.astype(BF16)
                gather.start(h)
            else:
                gpo[own] = grad.astype(BF16)
        vg[16 * l : 16 * l + 1, :] = sums[0]
        vg[16 * l + 1 : 16 * l + 2, :] = sums[1]
        if not first:
            write_out(lambda: (gpo, gin.at[0]))
            gw5[...] = jnp.transpose(vg[...]).astype(BF16)
            red_x(5, 0)
        if first:
            red_z(3, 1, 0)
            red_z(1, 1, ORDER[0])

    red_z(1, 0, ORDER[0])
    red_sum(4, 0)
    red_z(1, 0, *ORDER[1:], 0)
    red_z(2, 0)
    red_z(5, 0)
    red_sum(3, 0)
    red_sum(1, 0)
    red_write(3, 0)
    red_sum(2, 0)
    red_sum(5, 0)
    red_write(1, 0)
    red_write(2, 0)
    red_write(5, 0)
    for i, ends in enumerate(local):
        if ends is not None:
            pltpu.make_async_copy(*ends(), near.at[i]).wait()
    flush()
    for g, i in sent_weights:
        ref = W[g].at[0, part(g, 0)]
        rc(ref, ref, x_peer, i).wait_send()


def fused_step(inputs, cotangent, image_lengths, attention, upward, downward, vectors, bias_up):
    DP = lax.axis_size("dp")
    S = lax.axis_size("seq")
    NZ = DP // 2
    L = attention.shape[0]
    T, D = inputs.shape[1], inputs.shape[2]
    N = S * T
    R = attention.shape[2]
    CH = R * S
    RP = (R + 15) // 16 * 16
    FJ = bias_up.shape[1]
    vmem, hbm = pl.BlockSpec(memory_space=pltpu.VMEM), pl.BlockSpec(memory_space=pl.ANY)
    V = pltpu.VMEM
    widths = {1: 640, 2: D, 3: D, 4: D, 5: 128}
    scratch = [
        V((L, D, 640), BF16), V((L, D, D), BF16), V((L, D, D), BF16), V((L, D, D), BF16),
        V((4 * T, D), BF16),
        V((6, T, D), BF16),
        V((L, N, D), BF16), V((L, N, D), BF16), V((L, N, D), BF16),
        V((L, 3, N, 128), BF16), V((L, 2, N, 128), BF16), V((L, 2, N, 128), BF16),
        V((L, 2, 128, N), BF16), V((2, 128, N), BF16),
        V((L, N, 256), BF16), V((L, T, D), BF16),
        V((N, 256), BF16), V((T, D), BF16),
        V((L, 3, 8, N), F32), V((2, 128, QBLOCK), F32),
        V((L, T, D), F32), V((T, D), F32), V((T, D), F32),
        V((L, N, D), BF16), V((L, N, D), BF16),
        V((N, 128), jnp.int32), V((8, N), jnp.int32),
        V((N, D), F32),
        V((N, 640), BF16),
        *[V((D, widths[g]), BF16) for g in range(1, 6)],
        *[V((NZ, CH // 2 if g == 2 else CH, widths[g]), BF16) for g in range(1, 6)],
        *[V((NZ - 1, CH // 2 if g == 2 else CH, widths[g]), BF16) for g in range(1, 6)],
        V((DP, CH // 2, D), BF16), V((DP, CH // 2, D // 2), BF16),
        *[V((2 if g == 2 else S, RP, widths[g]), BF16) for g in (1, 2, 3, 5)],
        *[V((2 if g == 2 else S, RP, widths[g]), BF16) for g in (1, 2, 3, 5)],
        V((128, 128), F32), V((32, D), F32), V((128, D), F32),
        pltpu.SemaphoreType.DMA((SEMS,)), pltpu.SemaphoreType.DMA((SEMS,)),
        pltpu.SemaphoreType.REGULAR((8,)), pltpu.SemaphoreType.REGULAR((8,)),
        V(attention.shape, F32), V(upward.shape, F32), V(downward.shape, F32),
        V((T, D), BF16),
        V(attention.shape, F32), V(upward.shape, F32), V(downward.shape, F32),
        pltpu.SemaphoreType.DMA((16,)),
    ]
    return pl.pallas_call(
        functools.partial(step_kernel, NZ),
        out_shape=(
            jax.ShapeDtypeStruct(inputs.shape, BF16),
            jax.ShapeDtypeStruct(inputs.shape, BF16),
            jax.ShapeDtypeStruct(attention.shape, F32),
            jax.ShapeDtypeStruct(upward.shape, F32),
            jax.ShapeDtypeStruct(downward.shape, F32),
            jax.ShapeDtypeStruct(vectors.shape, F32),
            jax.ShapeDtypeStruct(bias_up.shape, F32),
        ),
        in_specs=[hbm, hbm, pl.BlockSpec(memory_space=pltpu.SMEM), hbm, hbm, hbm, vmem, vmem],
        out_specs=(hbm,) * 5 + (vmem,) * 2,
        scratch_shapes=scratch,
        compiler_params=pltpu.CompilerParams(
            collective_id=0, has_side_effects=True, vmem_limit_bytes=VMEM_BYTES
        ),
    )(inputs, cotangent, image_lengths, attention, upward, downward, vectors, bias_up)


def fits_fused(inputs, attention, upward, bias_up, dp_count, seq_count):
    own_rows, width = attention.shape[2], attention.shape[3]
    return (
        seq_count == 4
        and dp_count == 8
        and inputs.shape == (1, QBLOCK, 768)
        and width == 768
        and own_rows % 8 == 0
        and upward.shape[2] == seq_count * width
        and bias_up.shape[1] % 16 == 0
    )


def update_kernel(rate, *refs):
    for member in range(5):
        gradient, master, moment, average = (refs[5 * k + member][...] for k in range(4))
        results = optimizer_step(gradient, master, moment, average, rate)
        for k in range(5):
            refs[22 + 5 * member + k][...] = results[k]
    for k in range(2):
        refs[47 + k][...] = refs[20 + k][...]


def fused_update(rate, output, input_grad, reduced, masters, moments, averages):
    attention, upward, downward, vectors, bias_up = masters
    blocks = [
        pl.BlockSpec((1,) + attention.shape[1:], lambda l: (l, 0, 0, 0)),
        pl.BlockSpec((1,) + upward.shape[1:], lambda l: (l, 0, 0)),
        pl.BlockSpec((1,) + downward.shape[1:], lambda l: (l, 0, 0)),
        pl.BlockSpec((1,) + vectors.shape[1:], lambda l: (l, 0, 0)),
        pl.BlockSpec(bias_up.shape, lambda l: (0, 0)),
    ]
    tokens = pl.BlockSpec((1, output.shape[1] // 2, output.shape[2]), lambda l: (0, l, 0))
    outs, specs = [], []
    for member in range(5):
        for k in range(5):
            outs.append(jax.ShapeDtypeStruct(masters[member].shape, BF16 if k == 4 else F32))
            specs.append(blocks[member])
    outs += [jax.ShapeDtypeStruct(output.shape, BF16)] * 2
    results = pl.pallas_call(
        functools.partial(update_kernel, rate),
        grid=(2,),
        out_shape=outs,
        in_specs=blocks * 4 + [tokens] * 2,
        out_specs=specs + [tokens] * 2,
        compiler_params=pltpu.CompilerParams(vmem_limit_bytes=VMEM_BYTES),
    )(*reduced, *masters, *moments, *averages, output, input_grad)
    return tuple(results[25:]) + tuple(results[:25])


def per_device(
    inputs,
    cotangent,
    image_lengths,
    attention_weight,
    attention_moment,
    attention_average,
    up_weight,
    up_moment,
    up_average,
    down_weight,
    down_moment,
    down_average,
    layer_vectors,
    vector_moment,
    vector_average,
    hidden_bias,
    bias_moment,
    bias_average,
):
    masters = (attention_weight, up_weight, down_weight, layer_vectors, hidden_bias)
    dp_count = lax.axis_size("dp")
    seq_count = lax.axis_size("seq")
    if fits_fused(inputs, attention_weight, up_weight, hidden_bias, dp_count, seq_count):
        output, input_grad, *reduced = fused_step(inputs, cotangent, image_lengths, *masters)
        moments = (attention_moment, up_moment, down_moment, vector_moment, bias_moment)
        averages = (attention_average, up_average, down_average, vector_average, bias_average)
        rate = LEARN_BASE / math.sqrt(inputs.shape[0] * inputs.shape[1] * dp_count * seq_count)
        return fused_update(rate, output, input_grad, reduced, masters, moments, averages)
    else:
        output, input_grad, *reduced = plain_step(inputs, cotangent, image_lengths, masters)
    total_tokens = inputs.shape[0] * inputs.shape[1] * dp_count * seq_count
    step_rate = LEARN_BASE / math.sqrt(total_tokens)
    states = (
        (attention_weight, attention_moment, attention_average),
        (up_weight, up_moment, up_average),
        (down_weight, down_moment, down_average),
        (layer_vectors, vector_moment, vector_average),
        (hidden_bias, bias_moment, bias_average),
    )
    outcome = [output, input_grad]
    for member in range(5):
        master, moment, average = states[member]
        outcome.extend(optimizer_step(reduced[member], master, moment, average, step_rate))
    return tuple(outcome)


def solution(mesh):
    placed = (
        P("dp", "seq", None),
        P("dp", "seq", None),
        P("dp", None),
        P(None, None, ("dp", "seq"), None),
        P(None, None, ("dp", "seq"), None),
        P(None, None, ("dp", "seq"), None),
        P(None, ("dp", "seq"), None),
        P(None, ("dp", "seq"), None),
        P(None, ("dp", "seq"), None),
        P(None, ("dp", "seq"), None),
        P(None, ("dp", "seq"), None),
        P(None, ("dp", "seq"), None),
        P(None, None, ("dp", "seq")),
        P(None, None, ("dp", "seq")),
        P(None, None, ("dp", "seq")),
        P(None, ("dp", "seq")),
        P(None, ("dp", "seq")),
        P(None, ("dp", "seq")),
    )
    return jax.shard_map(
        per_device,
        mesh=mesh,
        in_specs=placed,
        out_specs=(
            P("dp", "seq", None),
            P("dp", "seq", None),
            P(None, None, ("dp", "seq"), None),
            P(None, None, ("dp", "seq"), None),
            P(None, None, ("dp", "seq"), None),
            P(None, None, ("dp", "seq"), None),
            P(None, None, ("dp", "seq"), None),
            P(None, ("dp", "seq"), None),
            P(None, ("dp", "seq"), None),
            P(None, ("dp", "seq"), None),
            P(None, ("dp", "seq"), None),
            P(None, ("dp", "seq"), None),
            P(None, ("dp", "seq"), None),
            P(None, ("dp", "seq"), None),
            P(None, ("dp", "seq"), None),
            P(None, ("dp", "seq"), None),
            P(None, ("dp", "seq"), None),
            P(None, None, ("dp", "seq")),
            P(None, None, ("dp", "seq")),
            P(None, None, ("dp", "seq")),
            P(None, None, ("dp", "seq")),
            P(None, None, ("dp", "seq")),
            P(None, ("dp", "seq")),
            P(None, ("dp", "seq")),
            P(None, ("dp", "seq")),
            P(None, ("dp", "seq")),
            P(None, ("dp", "seq")),
        ),
        check_vma=False,
    )
```

```python
import functools
import math

import jax
import jax.numpy as jnp
from jax import lax
from jax.experimental import pallas as pl
from jax.experimental.pallas import tpu as pltpu
from jax.sharding import PartitionSpec as P

HEAD_DIM = 64
SEGS = 8


EPSILON = 1e-06
SCALE_SCORE = 0.125
MOMENTUM_RATE = 0.9
DECAY_RATE = 0.0001
AVERAGE_RATE = 0.5
LEARN_BASE = 0.1
VMEM_BYTES = 66900000


def as_sent(shard):
    return jax.tree.map(lambda a: a.astype(jnp.bfloat16) if a.dtype == jnp.float32 else a, shard)


def layer_norm(values, gain_row, shift_row):
    center = values - jnp.mean(values, axis=-1, keepdims=True)
    spread = jnp.mean(center * center, axis=-1, keepdims=True)
    return center * lax.rsqrt(spread + EPSILON) * gain_row + shift_row


def gelu_exact(values):
    return jax.nn.gelu(values, approximate=False)


def project(values, matrix):
    return jnp.einsum("rti,ij->rtj", values, matrix, preferred_element_type=jnp.float32)


def project_back(grad_rows, matrix):
    return jnp.einsum("rtj,ij->rti", grad_rows, matrix, preferred_element_type=jnp.float32)


def outer_sum(values, grad_rows):
    return jnp.einsum("rti,rtj->ij", values, grad_rows, preferred_element_type=jnp.float32)


def column_sum(grad_rows):
    return jnp.sum(grad_rows, axis=(0, 1), dtype=jnp.float32)


def segment_ids(image_lengths, row_len):
    upto = jnp.arange(SEGS)[:, None] <= jnp.arange(SEGS)[None, :]
    bounds = jnp.sum(jnp.where(upto[None], image_lengths[:, :, None], 0), axis=1, dtype=jnp.int32)
    places = jnp.arange(row_len, dtype=jnp.int32)
    return jnp.sum(
        (bounds[:, None, :] <= places[None, :, None]).astype(jnp.int32), axis=-1, dtype=jnp.int32
    )


def visible_block(seg_rows, offset, block_size):
    row_len = seg_rows.shape[0]
    seg_query = seg_rows[offset : offset + block_size]
    matching = seg_query[:, None] == seg_rows[None, :]
    open_key = seg_rows[None, :] != SEGS - 1
    query_place = offset + jnp.arange(block_size, dtype=jnp.int32)
    key_place = jnp.arange(row_len, dtype=jnp.int32)
    return matching & open_key | (query_place[:, None] == key_place[None, :])


def score_block(query_block, key_heads, seg_rows, offset):
    scores = (
        jnp.einsum("qhd,khd->hqk", query_block, key_heads, preferred_element_type=jnp.float32)
        * SCALE_SCORE
    )
    allowed = visible_block(seg_rows, offset, query_block.shape[0])
    return jnp.where(allowed[None], scores, -1e30)


def split_heads(row_values):
    return row_values.reshape(row_values.shape[0], row_values.shape[1] // HEAD_DIM, HEAD_DIM)


def attend_row(row_items):
    query_row, key_row, value_row, seg_rows = row_items
    row_len = query_row.shape[0]
    query_heads = split_heads(query_row)
    key_heads = split_heads(key_row)
    value_heads = split_heads(value_row)
    block_size = min(512, row_len)
    outputs = []
    totals = []
    for offset in range(0, row_len, block_size):
        scores = score_block(query_heads[offset : offset + block_size], key_heads, seg_rows, offset)
        top_score = jnp.max(scores, axis=-1, keepdims=True)
        exponent = jnp.exp(scores - top_score)
        denominator = jnp.sum(exponent, axis=-1, keepdims=True)
        probability = (exponent / denominator).astype(jnp.bfloat16)
        outputs.append(
            jnp.einsum("hqk,khd->qhd", probability, value_heads, preferred_element_type=jnp.float32)
        )
        totals.append(top_score[..., 0] + jnp.log(denominator[..., 0]))
    mixture = jnp.concatenate(outputs, axis=0).reshape(query_row.shape).astype(jnp.bfloat16)
    return (mixture, jnp.concatenate(totals, axis=1))


def attend_back(row_items):
    query_row, key_row, value_row, grad_row, log_total, seg_rows = row_items
    row_len = query_row.shape[0]
    query_heads = split_heads(query_row)
    key_heads = split_heads(key_row)
    value_heads = split_heads(value_row)
    grad_heads = split_heads(grad_row)
    block_size = min(512, row_len)
    key_grad = jnp.zeros(key_heads.shape, jnp.float32)
    value_grad = jnp.zeros(value_heads.shape, jnp.float32)
    query_grads = []
    for offset in range(0, row_len, block_size):
        query_block = query_heads[offset : offset + block_size]
        grad_block = grad_heads[offset : offset + block_size]
        scores = score_block(query_block, key_heads, seg_rows, offset)
        probability = jnp.exp(scores - log_total[:, offset : offset + block_size, None])
        prob_low = probability.astype(jnp.bfloat16)
        prob_grad = jnp.einsum(
            "qhd,khd->hqk", grad_block, value_heads, preferred_element_type=jnp.float32
        )
        inner_sum = jnp.sum(probability * prob_grad, axis=-1, keepdims=True)
        score_grad = (probability * (prob_grad - inner_sum)).astype(jnp.bfloat16)
        query_grads.append(
            jnp.einsum("hqk,khd->qhd", score_grad, key_heads, preferred_element_type=jnp.float32)
            * SCALE_SCORE
        )
        key_grad = (
            key_grad
            + jnp.einsum(
                "hqk,qhd->khd", score_grad, query_block, preferred_element_type=jnp.float32
            )
            * SCALE_SCORE
        )
        value_grad = value_grad + jnp.einsum(
            "hqk,qhd->khd", prob_low, grad_block, preferred_element_type=jnp.float32
        )
    flat_shape = query_row.shape
    query_grad = jnp.concatenate(query_grads, axis=0)
    return (
        query_grad.reshape(flat_shape).astype(jnp.bfloat16),
        key_grad.reshape(flat_shape).astype(jnp.bfloat16),
        value_grad.reshape(flat_shape).astype(jnp.bfloat16),
    )


def layer_forward(hidden_in, params, seg_full):
    attention, upward, downward, vectors, bias_up = params
    vector_values = vectors.astype(jnp.float32)
    normed = layer_norm(hidden_in, vector_values[0], vector_values[1]).astype(jnp.bfloat16)
    queries = (project(normed, attention[0]) + vector_values[2]).astype(jnp.bfloat16)
    key_rows = project(normed, attention[1]).astype(jnp.bfloat16)
    value_rows = (project(normed, attention[2]) + vector_values[3]).astype(jnp.bfloat16)
    query_full, key_full, value_full = (
        lax.all_to_all(queries, "seq", split_axis=2, concat_axis=1, tiled=True),
        lax.all_to_all(key_rows, "seq", split_axis=2, concat_axis=1, tiled=True),
        lax.all_to_all(value_rows, "seq", split_axis=2, concat_axis=1, tiled=True),
    )
    mixture, log_total = lax.map(attend_row, (query_full, key_full, value_full, seg_full))
    mixed_tokens = lax.all_to_all(mixture, "seq", split_axis=1, concat_axis=2, tiled=True)
    residual = hidden_in + (project(mixed_tokens, attention[3]) + vector_values[4])
    normed_two = layer_norm(residual, vector_values[5], vector_values[6]).astype(jnp.bfloat16)
    hidden_pre = project(normed_two, upward) + bias_up.astype(jnp.float32)
    hidden_act = gelu_exact(hidden_pre).astype(jnp.bfloat16)
    result = residual + (project(hidden_act, downward) + vector_values[7])
    saved_values = (
        hidden_in,
        normed,
        query_full,
        key_full,
        value_full,
        log_total,
        mixed_tokens,
        residual,
        normed_two,
        hidden_pre,
        hidden_act,
    )
    return (result, saved_values)


def layer_backward(grad_out, params, saved_values, seg_full):
    attention, upward, downward, vectors, bias_up = params
    vector_values = vectors.astype(jnp.float32)
    (
        hidden_in,
        normed,
        query_full,
        key_full,
        value_full,
        log_total,
        mixed_tokens,
        residual,
        normed_two,
        hidden_pre,
        hidden_act,
    ) = saved_values
    grad_mlp = grad_out.astype(jnp.bfloat16)
    grad_down = outer_sum(hidden_act, grad_mlp)
    grad_act = project_back(grad_mlp, downward)
    grad_pre = jax.vjp(gelu_exact, hidden_pre)[1](grad_act)[0].astype(jnp.bfloat16)
    grad_up = outer_sum(normed_two, grad_pre)
    grad_normed_two = project_back(grad_pre, upward)
    norm_pull_two = jax.vjp(layer_norm, residual, vector_values[5], vector_values[6])[1]
    grad_resid_norm, grad_gain_two, grad_shift_two = norm_pull_two(grad_normed_two)
    grad_residual = grad_out + grad_resid_norm
    grad_proj = grad_residual.astype(jnp.bfloat16)
    grad_outproj = outer_sum(mixed_tokens, grad_proj)
    grad_mixed = project_back(grad_proj, attention[3]).astype(jnp.bfloat16)
    grad_heads = lax.all_to_all(grad_mixed, "seq", split_axis=2, concat_axis=1, tiled=True)
    query_grad, key_grad, value_grad = lax.map(
        attend_back, (query_full, key_full, value_full, grad_heads, log_total, seg_full)
    )
    grad_query, grad_key, grad_value = (
        lax.all_to_all(query_grad, "seq", split_axis=1, concat_axis=2, tiled=True),
        lax.all_to_all(key_grad, "seq", split_axis=1, concat_axis=2, tiled=True),
        lax.all_to_all(value_grad, "seq", split_axis=1, concat_axis=2, tiled=True),
    )
    grad_wq = outer_sum(normed, grad_query)
    grad_wk = outer_sum(normed, grad_key)
    grad_wv = outer_sum(normed, grad_value)
    grad_normed = (
        project_back(grad_query, attention[0])
        + project_back(grad_key, attention[1])
        + project_back(grad_value, attention[2])
    )
    norm_pull_one = jax.vjp(layer_norm, hidden_in, vector_values[0], vector_values[1])[1]
    grad_in_norm, grad_gain_one, grad_shift_one = norm_pull_one(grad_normed)
    grad_in = grad_residual + grad_in_norm
    attention_terms = jnp.stack([grad_wq, grad_wk, grad_wv, grad_outproj])
    vector_terms = jnp.stack(
        [
            grad_gain_one,
            grad_shift_one,
            column_sum(grad_query),
            column_sum(grad_value),
            column_sum(grad_proj),
            grad_gain_two,
            grad_shift_two,
            column_sum(grad_mlp),
        ]
    )
    return (grad_in, (attention_terms, grad_up, grad_down, vector_terms, column_sum(grad_pre)))


def fold_terms(terms, dims, dp_count, seq_count):
    folded = []
    for member in range(len(terms)):
        term = terms[member]
        place = dims[member]
        shape = term.shape
        leading = math.prod(shape[:place])
        owned = shape[place] // (dp_count * seq_count)
        trailing = owned * math.prod(shape[place + 1 :])
        folded.append(term.reshape(leading, dp_count, seq_count, trailing))
    return tuple(folded)


def unfold_terms(received, terms, dims, dp_count, seq_count):
    results = []
    for member in range(len(terms)):
        shape = terms[member].shape
        place = dims[member]
        owned_shape = shape[:place] + (shape[place] // (dp_count * seq_count),) + shape[place + 1 :]
        results.append(jnp.sum(received[member], axis=(1, 2)).reshape(owned_shape))
    return tuple(results)


def optimizer_step(gradient, master, moment, average, step_rate):
    direction = gradient + DECAY_RATE * master
    moment_new = MOMENTUM_RATE * moment + direction
    master_new = master - step_rate * (direction + MOMENTUM_RATE * moment_new)
    average_new = AVERAGE_RATE * average + (1.0 - AVERAGE_RATE) * master_new
    return (gradient, moment_new, average_new, master_new, master_new.astype(jnp.bfloat16))


def plain_step(inputs, cotangent, image_lengths, masters):
    layer_count = masters[0].shape[0]
    dp_count = lax.axis_size("dp")
    seq_count = lax.axis_size("seq")
    seg_full = segment_ids(image_lengths, inputs.shape[1] * seq_count)

    def gather_layer(level_index):
        pieces = tuple((master[level_index].astype(jnp.bfloat16) for master in masters))
        return (
            lax.all_gather(pieces[0], ("dp", "seq"), axis=1, tiled=True),
            lax.all_gather(pieces[1], ("dp", "seq"), axis=0, tiled=True),
            lax.all_gather(pieces[2], ("dp", "seq"), axis=0, tiled=True),
            lax.all_gather(pieces[3], ("dp", "seq"), axis=1, tiled=True),
            lax.all_gather(pieces[4], ("dp", "seq"), axis=0, tiled=True),
        )

    hidden = inputs.astype(jnp.float32)
    kept_params = []
    kept_saved = []
    for level_index in range(layer_count):
        params = gather_layer(level_index)
        hidden, saved_values = layer_forward(hidden, params, seg_full)
        kept_params.append(params)
        kept_saved.append(saved_values)
    output = hidden.astype(jnp.bfloat16)
    stack_dims = (2, 1, 1, 2, 1)
    grad_hidden = cotangent.astype(jnp.float32)
    layer_terms = [None] * layer_count
    for level_index in reversed(range(layer_count)):
        params = kept_params[level_index]
        grad_hidden, terms_here = layer_backward(
            grad_hidden, params, kept_saved[level_index], seg_full
        )
        layer_terms[level_index] = terms_here
    stacked = tuple(
        (jnp.stack([terms_here[member] for terms_here in layer_terms]) for member in range(5))
    )
    folded = fold_terms(stacked, stack_dims, dp_count, seq_count)
    received = jax.tree.map(
        lambda part, own: part.astype(own.dtype),
        lax.all_to_all(
            lax.all_to_all(as_sent(folded), "dp", split_axis=1, concat_axis=1, tiled=True),
            "seq",
            split_axis=2,
            concat_axis=2,
            tiled=True,
        ),
        folded,
    )
    reduced = unfold_terms(received, stacked, stack_dims, dp_count, seq_count)
    return (output, grad_hidden.astype(jnp.bfloat16), *reduced)


MESH = pl.DeviceIdType.MESH
F32 = jnp.float32
BF16 = jnp.bfloat16
KEYS = 896
EDGE_KEYS = 640
QBLOCK = 256


def nt(left, right):
    return lax.dot_general(left, right, (((1,), (1,)), ((), ())), preferred_element_type=F32)


def nn(left, right):
    return lax.dot_general(left, right, (((1,), (0,)), ((), ())), preferred_element_type=F32)


def tn(left, right):
    return lax.dot_general(left, right, (((0,), (0,)), ((), ())), preferred_element_type=F32)


def norm_parts(values):
    center = values - jnp.mean(values, axis=-1, keepdims=True)
    scale = lax.rsqrt(jnp.mean(center * center, axis=-1, keepdims=True) + EPSILON)
    return center * scale, scale


def norm_back(values, grad, gain):
    unit, scale = norm_parts(values)
    pulled = grad * gain
    first = jnp.mean(pulled, axis=-1, keepdims=True)
    second = jnp.mean(pulled * unit, axis=-1, keepdims=True)
    result = scale * (pulled - first - unit * second)
    return (
        result,
        jnp.sum(grad * unit, axis=0, keepdims=True),
        jnp.sum(grad, axis=0, keepdims=True),
    )


SEMS = 108


def step_kernel(NZ, x_hbm, cot_hbm, lens, aw_hbm, uw_hbm, dw_hbm, lv, hb, *rest):
    (out, gin, gA_hbm, gU_hbm, gD_hbm, gV, gB) = rest[:7]
    (
        w1, w2, w3, w4, stg, rsl, gm, a, b, qh, kk, vv, kT, vT, oh, ofull, goh, gpo, lse, heads_t, wsnd, wrcv,
        x1, xs, xs_out, hact, gpb, segc, segr, facc, gq, gw1, gw2, gw3, gw4, gw5, xl1, xl2, xl3, xl4, xl5,
        zl1, zl2, zl3, zl4, zl5, cl, yl, ps1, ps2, ps3, ps5, pl1, pl2, pl3, pl5, tt, V, vg, snd, rcv,
        credx, credz, aw, uw, dw, x_in, gA, gU, gD, near,
    ) = rest[7:]
    W = {1: w1, 2: w2, 3: w3, 4: w4}
    GW = {1: gw1, 2: gw2, 3: gw3, 4: gw4, 5: gw5}
    XL = {1: xl1, 2: xl2, 3: xl3, 4: xl4, 5: xl5}
    ZL = {1: zl1, 2: zl2, 3: zl3, 4: zl4, 5: zl5}
    PS = {1: ps1, 2: ps2, 3: ps3, 5: ps5}
    PL = {1: pl1, 2: pl2, 3: pl3, 5: pl5}
    S = 4
    T, D = x_in.shape
    R = aw.shape[2]
    CH = R * S
    DP = NZ * 2
    ORDER = (1, NZ - 1) + tuple(range(2, NZ - 1))
    FJ = hb.shape[1]

    d = lax.axis_index("dp")
    s = lax.axis_index("seq")
    z, x = d // 2, d % 2
    y, c = s // 2, s % 2
    xp = 1 - x

    def xor(k):
        return ((y + k // 2) % 2) * 2 + (c + k % 2) % 2

    member = xor

    def dev(dd, ss):
        return {"dp": dd, "seq": ss}

    core_peer, y_peer, x_peer = dev(d, xor(1)), dev(d, xor(2)), dev(z * 2 + xp, s)

    def zdev(dz):
        return dev(((z + dz) % NZ) * 2 + x, s)

    count = [0]

    def sems(n):
        first = count[0]
        count[0] += n
        assert count[0] <= SEMS
        return first

    def rc(src, dst, device, i):
        return pltpu.make_async_remote_copy(
            src_ref=src, dst_ref=dst, send_sem=snd.at[i], recv_sem=rcv.at[i],
            device_id=device, device_id_type=MESH,
        )

    def weight_copy(ref, device, g, l, i):
        return pltpu.make_async_remote_copy(
            src_ref=ref, dst_ref=ref, send_sem=wsnd.at[2 * (g - 1) + l], recv_sem=wrcv.at[i],
            device_id=device, device_id_type=MESH,
        )

    pending = []

    def flush():
        for copy in pending:
            copy.wait_send()
        pending.clear()

    def rows(i):
        return pl.ds(pl.multiple_of(i * T, T), T)

    H = T // 2

    def half(i, h):
        return pl.ds(pl.multiple_of(i * T + h * H, H), H)

    def chunk(i):
        return pl.ds(pl.multiple_of(i * CH, CH), CH)

    local = []

    def move(src, dst):
        copy = pltpu.make_async_copy(src, dst, near.at[len(local)])
        local.append(None)
        copy.start()
        return copy

    def write_out(ends):
        i = len(local)
        local.append(ends)
        pltpu.make_async_copy(*ends(), near.at[i]).start()

    class Gather:
        def __init__(self, view, i):
            self.c1, self.c2, self.c3 = [], [], []
            for h in range(2):
                own, across = view.at[half(s, h)], view.at[half(xor(2), h)]
                self.c1.append(rc(own, own, core_peer, i + h))
                self.c2.append(rc(own, own, y_peer, i + 2 + h))
                self.c3.append(rc(across, across, core_peer, i + 4 + h))

        def start(self, h):
            self.c2[h].start()
            self.c1[h].start()

        def core(self):
            self.c1[0].wait_recv()
            self.c1[1].wait_recv()

        def forward(self, h):
            self.c2[h].wait_recv()
            self.c3[h].start()

        def last(self, h):
            self.c3[h].wait_recv()

        def done(self):
            pending.extend(self.c1 + self.c2 + self.c3)

    ag_sems, taken = {}, 0
    for g in W:
        for l in range(2):
            ag_sems[g, l] = taken
            taken += 2 * NZ - 1 if g != 2 else 2 * NZ + DP - 2

    def part(g, dd):
        if g == 2:
            return pl.ds(pl.multiple_of(dd * CH + c * (CH // 2), 16), CH // 2)
        return chunk(dd)

    def ag_z(g, l, *steps):
        i = ag_sems[g, l]
        own = W[g].at[l, part(g, d)]
        for dz in steps or ORDER:
            weight_copy(own, zdev(dz), g, l, i + dz - 1).start()

    def ag_x(g, l, *steps):
        i = ag_sems[g, l]
        for dz in steps:
            ref = W[g].at[l, part(g, ((z - dz + NZ) % NZ) * 2 + x)]
            if dz:
                weight_copy(ref, zdev(dz), g, l, i + dz - 1).wait_recv()
            weight_copy(ref, x_peer, g, l, i + NZ - 1 + dz).start()

    def ag_done(g, l):
        i = ag_sems[g, l] + NZ - 1
        for dz in range(NZ):
            ref = W[g].at[l, part(g, dz)]
            weight_copy(ref, x_peer, g, l, i + dz).wait_recv()

    def ag_core(g, l, start):
        i = ag_sems[g, l] + 2 * NZ - 2
        for k in range(1, DP):
            ref = W[g].at[l, part(g, (d + k) % DP)]
            copy = weight_copy(ref, core_peer, g, l, i + k)
            if start:
                copy.start()
            else:
                copy.wait_recv()

    red_sems = {g: sems(2 * NZ + 1 + DP if g == 2 else 2 * NZ + S - 2) for g in range(1, 6)}

    def columns(g, l):
        return g == 2 and l == 0

    def own_part(g, l, dd):
        rows_of = part(g, dd)
        return (rows_of, pl.ds(pl.multiple_of(y * (D // 2), 128), D // 2)) if columns(g, l) else (rows_of,)

    def landing(g, l, k):
        return (k, slice(None), slice(0, D // 2)) if columns(g, l) else (k,)

    def x_copy(g, l, dz):
        zi = (z + dz) % NZ
        return rc(
            GW[g].at[own_part(g, l, zi * 2 + xp)], XL[g].at[landing(g, l, dz)], x_peer,
            red_sems[g] + dz,
        )

    def z_copy(g, l, dz):
        return rc(
            GW[g].at[own_part(g, l, ((z + dz) % NZ) * 2 + x)], ZL[g].at[landing(g, l, dz - 1)],
            zdev(dz), red_sems[g] + NZ - 1 + dz,
        )

    def s_copies(g, l):
        i = red_sems[g] + 2 * NZ - 2
        return [
            rc(PS[g].at[(s + ds) % S], PL[g].at[s], dev(d, (s + ds) % S), i + ds)
            for ds in range(1, S)
        ]

    def half_copies(l, action):
        i = red_sems[2] + 2 * NZ - 1
        for k in range(2):
            to = 2 * c + k
            copy = pltpu.make_async_remote_copy(
                src_ref=PS[2].at[landing(2, l, k)], dst_ref=PL[2].at[landing(2, l, y)],
                send_sem=snd.at[i + k],
                recv_sem=rcv.at[i + y], device_id=dev(d, to), device_id_type=MESH,
            )
            pl.when(to != s)(functools.partial(action, copy))

    def half_arrivals(l):
        i = red_sems[2] + 2 * NZ - 1
        for k in range(2):
            ref = PL[2].at[landing(2, l, k)]
            copy = rc(ref, ref, core_peer, i + k)
            pl.when(2 * k + s // 2 != s)(lambda copy=copy: copy.wait_recv())

    def core_copies(l):
        i = red_sems[2] + 2 * NZ + 1
        other = CH // 2 * (1 - c)
        return [
            rc(
                gw2.at[pl.ds(pl.multiple_of(k * CH + other, 16), CH // 2)], cl.at[k], core_peer, i + k
            )
            for k in range(DP)
        ]

    def red_core(l):
        for copy in core_copies(l):
            copy.start()

    def core_sum(l):
        for k, copy in enumerate(core_copies(l)):
            copy.wait_recv()
            gw2[part(2, k)] = (gw2[part(2, k)].astype(F32) + cl[k].astype(F32)).astype(BF16)

    def y_copies():
        theirs = pl.ds(pl.multiple_of((1 - y) * (D // 2), 128), D // 2)
        return [rc(gw2.at[part(2, k), theirs], yl.at[k], y_peer, y_sems + k) for k in range(DP)]

    def red_y():
        core_sum(0)
        for copy in y_copies():
            copy.start()

    def y_sum():
        for k, copy in enumerate(y_copies()):
            copy.wait_recv()
            mine = own_part(2, 0, k)
            gw2[mine] = (gw2[mine].astype(F32) + yl[k].astype(F32)).astype(BF16)

    def red_x(g, l):
        if l == 0 and g != 5:
            pl.semaphore_wait(credx.at[g], 1)
        if g == 2:
            y_sum() if l == 0 else core_sum(l)
        for dz in ORDER + (0,):
            x_copy(g, l, dz).start()

    def red_z(g, l, *steps):
        for dz in steps or ORDER + (0,):
            x_copy(g, l, dz).wait_recv()
            mine = own_part(g, l, ((z + dz) % NZ) * 2 + x)
            GW[g][mine] = (
                GW[g][mine].astype(F32) + XL[g][landing(g, l, dz)].astype(F32)
            ).astype(BF16)
            if dz:
                if l == 0 and g != 5 and dz == ORDER[0]:
                    pl.semaphore_wait(credz.at[g], NZ - 1)
                z_copy(g, l, dz).start()
            elif l == 1 and g != 5:
                pl.semaphore_signal(credx.at[g], 1, device_id=x_peer, device_id_type=MESH)

    def red_sum(g, l):
        total = GW[g][own_part(g, l, d)].astype(F32)
        for dz in ORDER:
            z_copy(g, l, dz).wait_recv()
            total = total + ZL[g][landing(g, l, dz - 1)].astype(F32)
        for dz in ORDER:
            z_copy(g, l, dz).wait_send()
        for dz in range(NZ):
            x_copy(g, l, dz).wait_send()
        if g == 2:
            for copy in core_copies(l) + (y_copies() if l == 0 else []):
                copy.wait_send()
        if l == 1 and g != 5:
            for dz in range(1, NZ):
                pl.semaphore_signal(credz.at[g], 1, device_id=zdev(dz), device_id_type=MESH)
        if g == 4:
            gD[l] = total
            write_out(lambda: (gD.at[l], gD_hbm.at[l]))
            return
        if g == 5:
            tt[0:CH, :] = total
        wide = total.shape[1]
        pad = jnp.zeros((PS[g].shape[1] - R, wide), F32)
        for k in range(2 if g == 2 else S):
            piece = jnp.concatenate([total[R * k : R * (k + 1)], pad], axis=0)
            PS[g][landing(g, l, k)] = piece.astype(BF16)
        if g == 2:
            half_copies(l, lambda copy: copy.start())

            @pl.when(s // 2 == c)
            def _():
                PL[2][landing(2, l, y)] = PS[2][landing(2, l, y)]
            return
        PL[g][s] = PS[g][s]
        for copy in s_copies(g, l):
            copy.start()

    def red_write(g, l):
        if g == 2:
            half_arrivals(l)
            two = [PL[2][landing(2, l, k)].astype(F32)[0:R] for k in range(2)]
            gA[l, 3] = jnp.concatenate(two, axis=1) if l == 0 else two[0] + two[1]
            write_out(lambda: (gA.at[l, 3], gA_hbm.at[l, 3]))
            half_copies(l, lambda copy: copy.wait_send())
            return
        for copy in s_copies(g, l):
            copy.wait_recv()
        parts = [PL[g][k].astype(F32)[0:R] for k in range(S)]
        if g == 1:
            gA[l, 0] = jnp.concatenate([p[:, 0:192] for p in parts], axis=1)
            gA[l, 1] = jnp.concatenate(
                [q for p in parts for q in (p[:, 256:384], p[:, 192:256])], axis=1
            )
            gA[l, 2] = jnp.concatenate([p[:, 384:576] for p in parts], axis=1)
            write_out(lambda: (gA.at[l, 0:3], gA_hbm.at[l, 0:3]))
        elif g == 3:
            gU[l] = jnp.concatenate(
                [parts[k][:, FJ * i : FJ * (i + 1)] for i in range(DP) for k in range(S)], axis=1
            )
            write_out(lambda: (gU.at[l], gU_hbm.at[l]))
        else:
            biases = jnp.transpose(tt[...])
            tt[0:R, :] = parts[0] + parts[1] + parts[2] + parts[3]
            vectors = jnp.transpose(tt[...])
            for k in range(2):
                gV[k] = vectors[16 * k : 16 * k + 8, 0:R]
                gB[k : k + 1, :] = biases[16 * k + 8 : 16 * k + 9, 0:CH]
        for copy in s_copies(g, l):
            copy.wait_send()

    parity = [0]
    scatter_sems = (sems(5), sems(5))
    gather_sems = (sems(6), sems(6), sems(6))
    forward_sems, backward_sems, y_sems = sems(3), sems(6), sems(DP)

    class Scatter:
        def __init__(self, shifted=False):
            base = parity[0] * 3
            i = scatter_sems[parity[0]]
            parity[0] = 1 - parity[0]
            self.base = base
            self.shifted = shifted
            self.y_at = 3 * T if shifted else 2 * T
            self.r1 = rc(stg.at[T : 2 * T], rsl.at[base + 1], core_peer, i)
            self.r0, self.r2 = [], []
            for h in range(2):
                part = pl.ds(h * H, H)
                self.r0.append(rc(stg.at[part], rsl.at[base, part], core_peer, i + 1 + h))
                at = pl.ds(self.y_at + h * H, H)
                self.r2.append(rc(stg.at[at], rsl.at[base + 2, part], y_peer, i + 3 + h))

        def slot(self, k, h=None):
            at = 1 + k - 2 * (k // 3) if self.shifted else k
            return rows(at) if h is None else half(at, h)

        def send_core(self, h=None):
            if h is None:
                stg[T : 2 * T] = facc[self.slot(1)].astype(BF16)
                self.r1.start()
            else:
                stg[h * H : (h + 1) * H] = facc[self.slot(3, h)].astype(BF16)
                self.r0[h].start()

        def send_y(self, h):
            self.r0[h].wait_recv()
            stg[self.y_at + h * H : self.y_at + (h + 1) * H] = (
                facc[self.slot(2, h)] + rsl[self.base, h * H : (h + 1) * H].astype(F32)
            ).astype(BF16)
            self.r2[h].start()

        def core_sent(self):
            for copy in (self.r1, *self.r0):
                copy.wait_send()

        def received(self, h):
            if h == 0:
                self.r1.wait_recv()
            self.r2[h].wait_recv()
            self.r2[h].wait_send()
            own = slice(h * H, (h + 1) * H)
            return rsl[self.base + 1, own].astype(F32) + rsl[self.base + 2, own].astype(F32)

        def finish(self, h):
            return facc[self.slot(0, h)] + self.received(h)

    loads = [
        move(src, dst)
        for src, dst in (
            (aw_hbm, aw), (uw_hbm, uw), (x_hbm.at[0], gm.at[0, rows(s)]), (dw_hbm, dw),
            (x_hbm.at[0], x_in), (cot_hbm.at[0], gm.at[1, rows(s)]),
        )
    ]
    barrier = pltpu.get_barrier_semaphore()
    greeted = [core_peer, y_peer, dev(d, xor(3)), x_peer] + [zdev(dz) for dz in range(1, NZ)]
    for device in greeted:
        pl.semaphore_signal(barrier, inc=1, device_id=device, device_id_type=MESH)

    tt[...] = jnp.zeros_like(tt)
    tt[64:72, 0:R] = lv[0]
    tt[72:80, 0:R] = lv[1]
    tt[80:82, 0:CH] = hb[...]
    turned = jnp.transpose(tt[...])
    lane128 = lax.broadcasted_iota(jnp.int32, (1, 128), 1)
    vec_cols = jnp.where(lane128 < 80, turned[0:R, :], 0.0)[:, 64:128]
    bias_cols = jnp.where((lane128 >= 80) & (lane128 < 82), turned[0:CH, :], 0.0)
    loads[0].wait()
    for k in range(S):
        o = 192 * k
        two = []
        for l in range(2):
            wq, wk, wv = aw[l, 0], aw[l, 1], aw[l, 2]
            tail = vec_cols if l == 0 else jnp.zeros((R, 64), F32)
            two.append(
                jnp.concatenate(
                    [wq[:, o : o + 192], wk[:, o + 128 : o + 192], wk[:, o : o + 128],
                     wv[:, o : o + 192], tail],
                    axis=1,
                )
            )
        stg[144 * k : 144 * k + 48, 0:640] = jnp.concatenate(two, axis=0).astype(BF16)
    loads[1].wait()
    for k in range(S):
        two = [
            jnp.concatenate(
                [uw[l][:, (m * S + k) * FJ : (m * S + k + 1) * FJ] for m in range(DP)], axis=1
            )
            for l in range(2)
        ]
        stg[144 * k + 48 : 144 * k + 96, :] = jnp.concatenate([aw[0, 3], aw[1, 3]], axis=0).astype(BF16)
        stg[144 * k + 96 : 144 * k + 144, :] = jnp.concatenate(two, axis=0).astype(BF16)
    for load in loads[2:]:
        load.wait()
    pl.semaphore_wait(barrier, len(greeted))

    def piece_rows(k):
        return pl.multiple_of(k * 144, 16)

    def send_pieces(source, target):
        i = sems(S - 1)
        copies = []
        for ds in (2, 3, 1):
            to = xor(ds)
            copies.append(rc(source(to), target, dev(d, to), i + ds - 1))
        for copy in copies:
            copy.start()
        return copies

    pieces1 = send_pieces(
        lambda to: stg.at[pl.ds(piece_rows(to), 48), 0:640], rsl.at[s, 0:48, 0:640]
    )
    pieces2 = send_pieces(
        lambda to: stg.at[pl.ds(pl.multiple_of(piece_rows(to) + 48, 16), 96), :], rsl.at[s, 48:144, :]
    )
    gather_x = Gather(gm.at[0], gather_sems[0])
    gather_x.start(0)
    gather_x.start(1)
    w4[0, chunk(d)] = dw[0].astype(BF16)
    ag_z(4, 0, *ORDER[:2])
    ag_x(4, 0, 0)
    w4[1, chunk(d)] = dw[1].astype(BF16)
    ag_x(4, 1, 0)
    rsl[s, 0:48, 0:640] = stg[pl.ds(piece_rows(s), 48), 0:640]
    rsl[s, 48:144, :] = stg[pl.ds(pl.multiple_of(piece_rows(s) + 48, 16), 96), :]
    vg[...] = jnp.zeros_like(vg)
    for copy in pieces1:
        copy.wait_recv()
    got = [rsl[k, 0:48, 0:640].astype(F32) for k in range(S)]
    for l in range(2):
        full = jnp.concatenate([g[R * l : R * (l + 1)] for g in got], axis=0)
        if l == 0:
            full = jnp.concatenate([full[:, 0:512], full[:, 512:640] + bias_cols], axis=1)
        w1[l, chunk(d)] = full.astype(BF16)
    ag_z(1, 0)
    ag_x(1, 0, 0)
    ag_x(4, 0, ORDER[0])

    bounds = []
    running = jnp.int32(0)
    for k in range(SEGS):
        running = running + lens[0, k]
        bounds.append(running)
    N = S * T

    def segments(shape, dim):
        place = lax.broadcasted_iota(jnp.int32, shape, dim)
        seg = jnp.zeros(shape, jnp.int32)
        for bound in bounds:
            seg = seg + jnp.where(place >= bound, 1, 0)
        return jnp.where(seg == SEGS - 1, SEGS + place, seg)

    segr[...] = segments((8, N), 1)
    segc[...] = segments((N, 128), 0)

    ag_x(1, 0, ORDER[0])
    for copy in pieces2:
        copy.wait_recv()
    for g, at in ((2, 48), (3, 96)):
        got = [rsl[k, at : at + 48, :].astype(F32) for k in range(S)]
        for l in range(2):
            W[g][l, chunk(d)] = jnp.concatenate(
                [piece[R * l : R * (l + 1)] for piece in got], axis=0
            ).astype(BF16)
    for copy in pieces1 + pieces2:
        copy.wait_send()
    ag_x(1, 0, ORDER[1])
    ag_x(1, 0, *ORDER[2:])
    ag_z(2, 0)
    ag_z(3, 0)
    ag_z(4, 0, *ORDER[2:])
    ag_x(2, 0, 0)
    ag_x(3, 0, 0)
    gather_x.core()
    gather_x.forward(0)
    gather_x.forward(1)
    gather_cot = Gather(gm.at[1], gather_sems[2])
    gather_cot.start(0)
    gather_cot.start(1)
    ag_done(1, 0)
    V[...] = jnp.transpose(w1[0, :, 512:640].astype(F32))[64:96]
    gather_x.last(0)
    gather_x.last(1)
    gather_x.done()

    def vec(l, k):
        return V[8 * l + k : 8 * l + k + 1, :]

    def own_heads(row):
        total = jnp.zeros((1, 192), F32)
        for k in range(S):
            total = total + jnp.where(s == k, row[:, 192 * k : 192 * (k + 1)], 0.0)
        return total

    def at_heads(part):
        total = jnp.zeros((1, D), F32)
        for k in range(S):
            spread = [jnp.zeros((1, 192), F32)] * S
            spread[k] = part
            total = total + jnp.where(s == k, jnp.concatenate(spread, axis=1), 0.0)
        return total

    low = lax.broadcasted_iota(jnp.int32, (T, 128), 1) < 64
    low_rows = lax.broadcasted_iota(jnp.int32, (128, QBLOCK), 0) < 64

    def project_heads(l):
        bias = jnp.concatenate(
            [own_heads(vec(l, 2)), jnp.zeros((1, 192), F32), own_heads(vec(l, 3)), jnp.zeros((1, 64), F32)],
            axis=1,
        )

        @pl.loop(0, S)
        def _(i):
            r = rows(i)
            if l == 0:
                unit, _ = norm_parts(gm[0, r].astype(F32))
                a[0, r] = (unit * vec(0, 0) + vec(0, 1)).astype(BF16)
            full = (nn(a[l, r], w1[l]) + bias).astype(BF16).astype(F32)
            t0, t1, t2, t3, t4 = (full[:, 128 * j : 128 * (j + 1)] for j in range(5))
            t1r = pltpu.roll(t1, 64, 1)
            v4 = jnp.where(low, t4, 0.0)
            qh[l, 0, r] = (jnp.where(low, t0, 0.0) * SCALE_SCORE).astype(BF16)
            qh[l, 1, r] = (jnp.where(low, 0.0, t0) * SCALE_SCORE).astype(BF16)
            qh[l, 2, r] = (jnp.where(low, t1, 0.0) * SCALE_SCORE).astype(BF16)
            kk[l, 0, r] = t2.astype(BF16)
            kk[l, 1, r] = t1r.astype(BF16)
            vv[l, 0, r] = t3.astype(BF16)
            vv[l, 1, r] = v4.astype(BF16)
            kT[l, 0, :, r] = jnp.transpose(t2).astype(BF16)
            kT[l, 1, :, r] = jnp.transpose(t1r).astype(BF16)
            vT[0, :, r] = jnp.transpose(t3).astype(BF16)
            vT[1, :, r] = jnp.transpose(v4).astype(BF16)

    def by_queries(qb, block):
        q = pl.ds(pl.multiple_of(qb * QBLOCK, QBLOCK), QBLOCK)
        edge = (qb == 0) | (qb == N // QBLOCK - 1)
        for size, here in ((EDGE_KEYS, edge), (KEYS, jnp.logical_not(edge))):
            k = pl.ds(pl.multiple_of((qb // 2) * (N - size), 128), size)
            pl.when(here)(functools.partial(block, q, k))

    def keep_head(h, part):
        p = h // 2
        heads_t[p] = jnp.where(low_rows & (h == 1), heads_t[p], part)

    def attend_block(l, q, k):
        @pl.loop(0, 3)
        def _(h):
            p = h // 2
            allowed = jnp.concatenate([segc[k, :]] * 2, axis=1) == segr[0:1, q]
            scores = jnp.where(allowed, nt(kk[l, p, k], qh[l, h, q]), -1e30)
            top = jnp.max(scores, axis=0, keepdims=True)
            grown = jnp.exp(scores - top)
            total = jnp.sum(grown, axis=0, keepdims=True)
            lse[l, h, :, q] = jnp.broadcast_to(top + jnp.log(total), (8, QBLOCK))
            keep_head(h, nn(vT[p, :, k], grown.astype(BF16)) / total)

        for p in range(2):
            oh[l, q, 128 * p : 128 * (p + 1)] = jnp.transpose(heads_t[p]).astype(BF16)

    def attend(l, points):
        order = (2, 3, 1)
        copies = [
            rc(oh.at[l, rows(xor(k))], goh.at[rows(s)], dev(d, xor(k)), forward_sems + k - 1)
            for k in order
        ]

        @pl.loop(0, N // QBLOCK)
        def _(i):
            for at, action in points.items():
                pl.when(i == at)(action)
            by_queries(
                member((2 + i) * (1 - i // 2) + (3 - i) * (i // 2)), functools.partial(attend_block, l)
            )
            for at in range(3):
                pl.when(i == at)(copies[at].start)

        goh[rows(s)] = oh[l, rows(s)]
        pending.extend(copies)
        return copies

    def attend_grad_block(l, q, k):
        @pl.loop(0, 3)
        def _(h):
            p = h // 2

            def tile(i):
                return pl.ds(pl.multiple_of(128 * i, 128), 128)

            head = jnp.where(low == (h != 1), goh[q, tile(p)].astype(F32), 0.0)
            inner = jnp.sum(
                jnp.transpose(head * oh[l, q, tile(p)].astype(F32)), axis=0, keepdims=True
            )
            head = head.astype(BF16)
            queries = qh[l, h, q]
            allowed = jnp.concatenate([segc[k, :]] * 2, axis=1) == segr[0:1, q]
            scores = jnp.where(allowed, nt(kk[l, p, k], queries), -1e30)
            prob = jnp.exp(scores - lse[l, h, 0:1, q])
            grad = nt(vv[l, p, k], head)
            grad = (prob * (grad - inner)).astype(BF16)
            facc[k, tile(2 + p)] += nn(prob.astype(BF16), head)
            facc[k, tile(p)] += nn(grad, queries)
            keep_head(h, nn(kT[l, p, :, k], grad) * SCALE_SCORE)

        gq[q, 0:128] = jnp.transpose(heads_t[0]).astype(BF16)
        gq[q, 128:256] = jnp.transpose(jnp.where(low_rows, heads_t[1], 0.0)).astype(BF16)

    def attend_grad(l, copies, points):
        facc[:, 0:512] = jnp.zeros((N, 512), F32)

        @pl.loop(0, N // QBLOCK)
        def _(i):
            for at in range(1, S):
                pl.when(i == at)(lambda at=at: (copies[0, at].wait(), copies[1, at].wait())[0])
            for at, action in points.items():
                pl.when(i == at)(action)
            by_queries(member(i), functools.partial(attend_grad_block, l))

        @pl.loop(0, S)
        def _(i):
            r = rows(i)
            other = pltpu.roll(facc[r, 128:256], 64, 1)
            gq[r, 128:256] = (gq[r, 128:256].astype(F32) + other).astype(BF16)
            gq[r, 256:384] = facc[r, 0:128].astype(BF16)
            gq[r, 384:512] = facc[r, 256:384].astype(BF16)
            gq[r, 512:640] = facc[r, 384:512].astype(BF16)

    def exchange(h, copies):
        for ds in (2, 3, 1):
            to = xor(ds)
            copies[h, ds] = rc(
                gq.at[half(to, h), 0:256], goh.at[half(s, h)], dev(d, to),
                backward_sems + 3 * h + ds - 1,
            )
            copies[h, ds].start()

    def up_rows(l, r):
        pre = nn(b[l, r], w3[l]) + V[16 + l : 17 + l, :]
        cdf = 0.5 * (1.0 + lax.erf(pre * 0.7071067811865476))
        density = jnp.exp(-0.5 * pre * pre) * 0.3989422804014327
        hact[l, r] = (pre * cdf).astype(BF16)
        gpb[l, r] = (cdf + pre * density).astype(BF16)

    def up_chip(l, gather, points):
        @pl.loop(0, 2)
        def _(k):
            pl.when(k == 1)(gather.core)
            for at, action in points.items():
                pl.when(k == at)(action)
            up_rows(l, rows(member(k)))

    def up_across(l, gather, h):
        gather.forward(h)

        @pl.loop(0, 2)
        def _(q):
            pl.when(q == 1)(lambda: gather.last(h))
            up_rows(l, half(member(2 + q), h))

    def scatter_rows(term, shifted=False, across=True):
        scatter = Scatter(shifted)

        @pl.loop(0, S)
        def _(i):
            k, h = 3 - i % 2, i // 2
            facc[scatter.slot(k, h)] = term(half(member(k), h))
            pl.when(i == 0)(lambda: scatter.send_core(0))
            pl.when(i == 2)(lambda: scatter.send_core(1))
            if across:
                pl.when(i == 2)(lambda: scatter.send_y(0))

        @pl.loop(0, 2)
        def _(i):
            k = 1 - i
            facc[scatter.slot(k)] = term(rows(member(k)))
            pl.when(i == 0)(scatter.send_core)
            if across:
                pl.when(i == 0)(lambda: scatter.send_y(1))

        return scatter

    def back_rows(l, scatter, r, slot):
        grad_act = nt(gm[l, r], w4[l])
        grad_pre = (grad_act * gpb[l, r].astype(F32)).astype(BF16)
        gpb[l, r] = grad_pre
        facc[slot] = nt(grad_pre, w3[l])
        vg[16 * l + 8 : 16 * l + 9, :] += jnp.sum(grad_pre.astype(F32), axis=0, keepdims=True)

    def back_chip(l, scatter, gather):
        @pl.loop(0, 2)
        def _(i):
            k = i if gather is not None else 1 - i
            if gather is not None:
                pl.when(i == 1)(gather.core)
            back_rows(l, scatter, rows(member(k)), scatter.slot(k))
            pl.when(k == 1)(scatter.send_core)

    def back_across(l, scatter, gather, h):
        if gather is not None:
            gather.forward(h)

        @pl.loop(0, 2)
        def _(i):
            k = 2 + i if gather is not None else 3 - i
            if gather is not None:
                pl.when(i == 1)(lambda: gather.last(h))
            back_rows(l, scatter, half(member(k), h), scatter.slot(k, h))
            pl.when(k == 3)(lambda: scatter.send_core(h))

    def weight_grad(g, left, right):
        @pl.loop(0, 2)
        def _(i):
            m = pl.ds(pl.multiple_of(i * 384, 384), 384)
            GW[g][m, :] = tn(left(m), right()).astype(BF16)

    def column(values):
        return jnp.sum(values.astype(F32), axis=0, keepdims=True)

    last = ORDER[2:]
    for l in range(2):
        project_heads(l)
        if l == 0:
            ag_x(2, 0, *ORDER[:2])

            def core_stage():
                ag_done(2, 0)
                ag_core(2, 0, True)
                ag_x(3, 0, ORDER[1])
                gather_cot.core()
                gather_cot.forward(0)
                gather_cot.forward(1)

            copies = attend(
                0, {1: lambda: ag_x(2, 0, *last), 2: lambda: ag_x(3, 0, ORDER[0]), 3: core_stage}
            )
        else:

            def core_stage():
                ag_done(2, 1)
                ag_core(2, 1, True)

            copies = attend(
                1,
                {
                    1: lambda: ag_x(3, 1, *last),
                    2: lambda: ag_x(4, 1, ORDER[0]),
                    3: core_stage,
                },
            )
            ag_x(4, 1, ORDER[1])
        for copy in copies:
            copy.wait_recv()
        ag_core(2, l, False)
        ofull[l] = jnp.concatenate(
            [goh[T * k : T * (k + 1)].astype(F32)[:, 0:192] for k in range(S)], axis=1
        ).astype(BF16)
        before = x_in[...].astype(F32) if l == 0 else xs[...]
        middle = before + (nn(ofull[l], w2[l]) + vec(l, 4))
        x1[l] = middle
        unit, _ = norm_parts(middle)
        b[l, rows(s)] = (unit * vec(l, 5) + vec(l, 6)).astype(BF16)
        gather_b = Gather(b.at[l], gather_sems[1])
        gather_b.start(0)
        gather_b.start(1)
        if l == 0:
            ag_x(3, 0, *last)
            ag_z(1, 1)
            ag_z(2, 1)
            ag_x(4, 0, ORDER[1])
            ag_x(1, 1, 0)
            gather_cot.last(0)
            gather_cot.last(1)
            gather_cot.done()
        ag_done(3, l)
        if l == 1:
            up_chip(1, gather_b, {1: lambda: ag_x(4, 1, *last)})
            break
        up_chip(0, gather_b, {1: lambda: ag_x(4, 0, *last)})
        ag_x(2, 1, 0)
        ag_x(3, 1, 0)
        ag_z(3, 1)
        ag_z(4, 1)
        up_across(0, gather_b, 0)
        up_across(0, gather_b, 1)
        gather_b.done()
        ag_done(4, 0)
        scatter = scatter_rows(lambda r: nn(hact[0, r], w4[0]))
        ag_x(1, 1, *ORDER)
        scatter.core_sent()
        flush()
        gather_a = Gather(a.at[1], gather_sems[0])
        for h in range(2):
            own = slice(h * H, (h + 1) * H)
            after = x1[0, own] + (scatter.finish(h) + vec(0, 7))
            xs[own] = after
            unit, _ = norm_parts(after)
            a[1, half(s, h)] = (unit * vec(1, 0) + vec(1, 1)).astype(BF16)
            gather_a.start(h)
        ag_x(2, 1, *ORDER)
        ag_x(3, 1, ORDER[0])
        ag_done(1, 1)
        gather_a.core()
        gather_a.forward(0)
        ag_x(3, 1, ORDER[1])
        gather_a.forward(1)
        gather_a.last(0)
        gather_a.last(1)
        gather_a.done()

    for l in (1, 0):
        first = l == 1
        scatter = Scatter()

        def down_grad():
            weight_grad(4, lambda m: hact[l, :, m], lambda: gm[l])
            red_x(4, l)

        if first:
            ag_done(4, 1)
            back_chip(1, scatter, None)
            up_across(1, gather_b, 0)
            back_across(1, scatter, None, 0)
            scatter.send_y(0)
            up_across(1, gather_b, 1)
            gather_b.done()
            down_grad()
            back_across(1, scatter, None, 1)
            scatter.send_y(1)
        else:
            back_chip(0, scatter, gather)
            red_z(1, 1, ORDER[1])
            back_across(0, scatter, gather, 0)
            scatter.send_y(0)
            red_z(1, 1, *last)
            back_across(0, scatter, gather, 1)
            gather.done()
            red_z(1, 1, 0)
            scatter.send_y(1)
            red_z(2, 1, *ORDER[:2])
            down_grad()
            red_z(2, 1, *last, 0)
            red_sum(3, 1)
        vg[16 * l + 7 : 16 * l + 8, :] = column(gm[l, rows(s)])
        weight_grad(3, lambda m: b[l, :, m], lambda: gpb[l])
        red_x(3, l)
        scatter.core_sent()
        if first:
            scatter_out = scatter_rows(lambda r: nn(hact[1, r], w4[1]), True, False)
        else:
            out_copy.wait()
        flush()
        copies = {}
        sums = [0.0, 0.0, 0.0]
        for h in range(2):
            own = slice(h * H, (h + 1) * H)
            if h and not first:
                red_z(4, 0, ORDER[0])
            grad_b = scatter.finish(h)
            grad_x1, gain, shift = norm_back(x1[l, own], grad_b, vec(l, 5))
            grad_x1 = grad_x1 + (gm[1, half(s, h)].astype(F32) if first else xs[own])
            if first:
                xs_out[own] = x1[1, own] + facc[scatter_out.slot(0, h)]
            x1[l, own] = grad_x1
            gpo[own] = grad_x1.astype(BF16)
            back = nt(gpo[own], w2[l])
            for k in range(S):
                gq[half(k, h), 0:256] = jnp.concatenate(
                    [back[:, 192 * k : 192 * (k + 1)], jnp.zeros((H, 64), F32)], axis=1
                ).astype(BF16)
            exchange(h, copies)
            goh[half(s, h)] = gq[half(s, h), 0:256]
            sums = [sums[0] + gain, sums[1] + shift, sums[2] + column(gpo[own])]
        vg[16 * l + 5 : 16 * l + 6, :] = sums[0]
        vg[16 * l + 6 : 16 * l + 7, :] = sums[1]
        vg[16 * l + 4 : 16 * l + 5, :] = sums[2]
        if first:
            scatter_out.send_y(0)
            scatter_out.send_y(1)
        if first:
            red_z(4, 1, ORDER[0])
            points = {
                1: lambda: red_z(4, 1, ORDER[1]),
                3: lambda: red_z(4, 1, *last),
            }
        else:

            def late():
                red_z(4, 0, *last)
                red_sum(2, 1)
                weight_grad(2, lambda m: ofull[0, :, m], lambda: gpo[...])
                red_core(0)

            points = {
                0: lambda: red_sum(1, 1),
                1: lambda: red_z(4, 0, ORDER[1]),
                2: late,
                3: lambda: (red_y(), red_write(3, 1), red_write(1, 1))[1],
            }
        attend_grad(l, copies, points)
        sums = column(gq[...])
        vg[16 * l + 2 : 16 * l + 3, :] = at_heads(sums[:, 0:192])
        vg[16 * l + 3 : 16 * l + 4, :] = at_heads(sums[:, 384:576])
        if first:
            scatter_out.core_sent()
        red_z(4, l, 0)
        if not first:
            red_z(3, 0, ORDER[0])
        scatter = scatter_rows(lambda r: nt(gq[r], w1[l]))
        red_z(3, l, ORDER[0] if first else ORDER[1])
        weight_grad(1, lambda m: a[l, :, m], lambda: gq[...])
        red_x(1, l)
        if first:
            weight_grad(2, lambda m: ofull[1, :, m], lambda: gpo[...])
            red_core(1)
            red_z(3, 1, ORDER[1])
        if not first:
            red_z(3, 0, *last)
        if first:
            red_x(2, 1)
            for h in range(2):
                own = slice(h * H, (h + 1) * H)
                gpo[own] = (xs_out[own] + (scatter_out.received(h) + vec(1, 7))).astype(BF16)
            out_copy = move(gpo, out.at[0])
            red_z(3, 1, *last)
            red_sum(4, 1)
        else:
            red_x(2, 0)
            red_write(2, 1)
            red_z(3, 0, 0)
        scatter.core_sent()
        flush()
        sums = [0.0, 0.0]
        if first:
            gather = Gather(gm.at[0], gather_sems[0])
        for h in range(2):
            own = slice(h * H, (h + 1) * H)
            grad_a = scatter.finish(h)
            before = xs[own] if first else x_in[own].astype(F32)
            grad, gain, shift = norm_back(before, grad_a, vec(l, 0))
            grad = grad + x1[l, own]
            sums = [sums[0] + gain, sums[1] + shift]
            if first:
                xs[own] = grad
                gm[0, half(s, h)] = grad.astype(BF16)
                gather.start(h)
            else:
                gpo[own] = grad.astype(BF16)
        vg[16 * l : 16 * l + 1, :] = sums[0]
        vg[16 * l + 1 : 16 * l + 2, :] = sums[1]
        if not first:
            write_out(lambda: (gpo, gin.at[0]))
            gw5[...] = jnp.transpose(vg[...]).astype(BF16)
            red_x(5, 0)
        if first:
            red_z(3, 1, 0)
            red_z(1, 1, ORDER[0])

    red_z(1, 0, ORDER[0])
    red_sum(4, 0)
    red_z(1, 0, *ORDER[1:], 0)
    red_z(2, 0)
    red_z(5, 0)
    red_sum(3, 0)
    red_sum(1, 0)
    red_write(3, 0)
    red_sum(2, 0)
    red_sum(5, 0)
    red_write(1, 0)
    red_write(2, 0)
    red_write(5, 0)
    for i, ends in enumerate(local):
        if ends is not None:
            pltpu.make_async_copy(*ends(), near.at[i]).wait()
    flush()
    for g in W:
        for l in range(2):
            weight_copy(W[g].at[l, 0 : (2 * NZ - 1) * CH], x_peer, g, l, 0).wait_send()


def fused_step(inputs, cotangent, image_lengths, attention, upward, downward, vectors, bias_up):
    DP = lax.axis_size("dp")
    S = lax.axis_size("seq")
    NZ = DP // 2
    L = attention.shape[0]
    T, D = inputs.shape[1], inputs.shape[2]
    N = S * T
    R = attention.shape[2]
    CH = R * S
    RP = (R + 15) // 16 * 16
    FJ = bias_up.shape[1]
    vmem, hbm = pl.BlockSpec(memory_space=pltpu.VMEM), pl.BlockSpec(memory_space=pl.ANY)
    V = pltpu.VMEM
    widths = {1: 640, 2: D, 3: D, 4: D, 5: 128}
    scratch = [
        V((L, D, 640), BF16), V((L, D, D), BF16), V((L, D, D), BF16), V((L, D, D), BF16),
        V((4 * T, D), BF16),
        V((6, T, D), BF16),
        V((L, N, D), BF16), V((L, N, D), BF16), V((L, N, D), BF16),
        V((L, 3, N, 128), BF16), V((L, 2, N, 128), BF16), V((L, 2, N, 128), BF16),
        V((L, 2, 128, N), BF16), V((2, 128, N), BF16),
        V((L, N, 256), BF16), V((L, T, D), BF16),
        V((N, 256), BF16), V((T, D), BF16),
        V((L, 3, 8, N), F32), V((2, 128, QBLOCK), F32),
        pltpu.SemaphoreType.DMA((8,)), pltpu.SemaphoreType.DMA((70,)),
        V((L, T, D), F32), V((T, D), F32), V((T, D), F32),
        V((L, N, D), BF16), V((L, N, D), BF16),
        V((N, 128), jnp.int32), V((8, N), jnp.int32),
        V((N, D), F32),
        V((N, 640), BF16),
        *[V((D, widths[g]), BF16) for g in range(1, 6)],
        *[V((NZ, CH // 2 if g == 2 else CH, widths[g]), BF16) for g in range(1, 6)],
        *[V((NZ - 1, CH // 2 if g == 2 else CH, widths[g]), BF16) for g in range(1, 6)],
        V((DP, CH // 2, D), BF16), V((DP, CH // 2, D // 2), BF16),
        *[V((2 if g == 2 else S, RP, widths[g]), BF16) for g in (1, 2, 3, 5)],
        *[V((2 if g == 2 else S, RP, widths[g]), BF16) for g in (1, 2, 3, 5)],
        V((128, 128), F32), V((32, D), F32), V((128, D), F32),
        pltpu.SemaphoreType.DMA((SEMS,)), pltpu.SemaphoreType.DMA((SEMS,)),
        pltpu.SemaphoreType.REGULAR((8,)), pltpu.SemaphoreType.REGULAR((8,)),
        V(attention.shape, F32), V(upward.shape, F32), V(downward.shape, F32),
        V((T, D), BF16),
        V(attention.shape, F32), V(upward.shape, F32), V(downward.shape, F32),
        pltpu.SemaphoreType.DMA((16,)),
    ]
    return pl.pallas_call(
        functools.partial(step_kernel, NZ),
        out_shape=(
            jax.ShapeDtypeStruct(inputs.shape, BF16),
            jax.ShapeDtypeStruct(inputs.shape, BF16),
            jax.ShapeDtypeStruct(attention.shape, F32),
            jax.ShapeDtypeStruct(upward.shape, F32),
            jax.ShapeDtypeStruct(downward.shape, F32),
            jax.ShapeDtypeStruct(vectors.shape, F32),
            jax.ShapeDtypeStruct(bias_up.shape, F32),
        ),
        in_specs=[hbm, hbm, pl.BlockSpec(memory_space=pltpu.SMEM), hbm, hbm, hbm, vmem, vmem],
        out_specs=(hbm,) * 5 + (vmem,) * 2,
        scratch_shapes=scratch,
        compiler_params=pltpu.CompilerParams(
            collective_id=0, has_side_effects=True, vmem_limit_bytes=VMEM_BYTES
        ),
    )(inputs, cotangent, image_lengths, attention, upward, downward, vectors, bias_up)


def fits_fused(inputs, attention, upward, bias_up, dp_count, seq_count):
    own_rows, width = attention.shape[2], attention.shape[3]
    return (
        seq_count == 4
        and dp_count == 8
        and inputs.shape == (1, QBLOCK, 768)
        and width == 768
        and own_rows % 8 == 0
        and upward.shape[2] == seq_count * width
        and bias_up.shape[1] % 16 == 0
    )


def update_kernel(rate, *refs):
    for member in range(5):
        gradient, master, moment, average = (refs[5 * k + member][...] for k in range(4))
        results = optimizer_step(gradient, master, moment, average, rate)
        for k in range(5):
            refs[22 + 5 * member + k][...] = results[k]
    for k in range(2):
        refs[47 + k][...] = refs[20 + k][...]


def fused_update(rate, output, input_grad, reduced, masters, moments, averages):
    attention, upward, downward, vectors, bias_up = masters
    blocks = [
        pl.BlockSpec((1,) + attention.shape[1:], lambda l: (l, 0, 0, 0)),
        pl.BlockSpec((1,) + upward.shape[1:], lambda l: (l, 0, 0)),
        pl.BlockSpec((1,) + downward.shape[1:], lambda l: (l, 0, 0)),
        pl.BlockSpec((1,) + vectors.shape[1:], lambda l: (l, 0, 0)),
        pl.BlockSpec(bias_up.shape, lambda l: (0, 0)),
    ]
    tokens = pl.BlockSpec((1, output.shape[1] // 2, output.shape[2]), lambda l: (0, l, 0))
    outs, specs = [], []
    for member in range(5):
        for k in range(5):
            outs.append(jax.ShapeDtypeStruct(masters[member].shape, BF16 if k == 4 else F32))
            specs.append(blocks[member])
    outs += [jax.ShapeDtypeStruct(output.shape, BF16)] * 2
    results = pl.pallas_call(
        functools.partial(update_kernel, rate),
        grid=(2,),
        out_shape=outs,
        in_specs=blocks * 4 + [tokens] * 2,
        out_specs=specs + [tokens] * 2,
        compiler_params=pltpu.CompilerParams(vmem_limit_bytes=VMEM_BYTES),
    )(*reduced, *masters, *moments, *averages, output, input_grad)
    return tuple(results[25:]) + tuple(results[:25])


def per_device(
    inputs,
    cotangent,
    image_lengths,
    attention_weight,
    attention_moment,
    attention_average,
    up_weight,
    up_moment,
    up_average,
    down_weight,
    down_moment,
    down_average,
    layer_vectors,
    vector_moment,
    vector_average,
    hidden_bias,
    bias_moment,
    bias_average,
):
    masters = (attention_weight, up_weight, down_weight, layer_vectors, hidden_bias)
    dp_count = lax.axis_size("dp")
    seq_count = lax.axis_size("seq")
    if fits_fused(inputs, attention_weight, up_weight, hidden_bias, dp_count, seq_count):
        output, input_grad, *reduced = fused_step(inputs, cotangent, image_lengths, *masters)
        moments = (attention_moment, up_moment, down_moment, vector_moment, bias_moment)
        averages = (attention_average, up_average, down_average, vector_average, bias_average)
        rate = LEARN_BASE / math.sqrt(inputs.shape[0] * inputs.shape[1] * dp_count * seq_count)
        return fused_update(rate, output, input_grad, reduced, masters, moments, averages)
    else:
        output, input_grad, *reduced = plain_step(inputs, cotangent, image_lengths, masters)
    total_tokens = inputs.shape[0] * inputs.shape[1] * dp_count * seq_count
    step_rate = LEARN_BASE / math.sqrt(total_tokens)
    states = (
        (attention_weight, attention_moment, attention_average),
        (up_weight, up_moment, up_average),
        (down_weight, down_moment, down_average),
        (layer_vectors, vector_moment, vector_average),
        (hidden_bias, bias_moment, bias_average),
    )
    outcome = [output, input_grad]
    for member in range(5):
        master, moment, average = states[member]
        outcome.extend(optimizer_step(reduced[member], master, moment, average, step_rate))
    return tuple(outcome)


def solution(mesh):
    placed = (
        P("dp", "seq", None),
        P("dp", "seq", None),
        P("dp", None),
        P(None, None, ("dp", "seq"), None),
        P(None, None, ("dp", "seq"), None),
        P(None, None, ("dp", "seq"), None),
        P(None, ("dp", "seq"), None),
        P(None, ("dp", "seq"), None),
        P(None, ("dp", "seq"), None),
        P(None, ("dp", "seq"), None),
        P(None, ("dp", "seq"), None),
        P(None, ("dp", "seq"), None),
        P(None, None, ("dp", "seq")),
        P(None, None, ("dp", "seq")),
        P(None, None, ("dp", "seq")),
        P(None, ("dp", "seq")),
        P(None, ("dp", "seq")),
        P(None, ("dp", "seq")),
    )
    return jax.shard_map(
        per_device,
        mesh=mesh,
        in_specs=placed,
        out_specs=(
            P("dp", "seq", None),
            P("dp", "seq", None),
            P(None, None, ("dp", "seq"), None),
            P(None, None, ("dp", "seq"), None),
            P(None, None, ("dp", "seq"), None),
            P(None, None, ("dp", "seq"), None),
            P(None, None, ("dp", "seq"), None),
            P(None, ("dp", "seq"), None),
            P(None, ("dp", "seq"), None),
            P(None, ("dp", "seq"), None),
            P(None, ("dp", "seq"), None),
            P(None, ("dp", "seq"), None),
            P(None, ("dp", "seq"), None),
            P(None, ("dp", "seq"), None),
            P(None, ("dp", "seq"), None),
            P(None, ("dp", "seq"), None),
            P(None, ("dp", "seq"), None),
            P(None, None, ("dp", "seq")),
            P(None, None, ("dp", "seq")),
            P(None, None, ("dp", "seq")),
            P(None, None, ("dp", "seq")),
            P(None, None, ("dp", "seq")),
            P(None, ("dp", "seq")),
            P(None, ("dp", "seq")),
            P(None, ("dp", "seq")),
            P(None, ("dp", "seq")),
            P(None, ("dp", "seq")),
        ),
        check_vma=False,
    )
```
